32 devices in a mesh: seq: 16 (over z, x, core), row: 2 (over y).
Axes of the slice: x: 2, y: 2, z: 4, core: 2. Of those that a mesh axis runs over, the one named last changes fastest.
Arguments:
- inputs: bfloat16 [2, 2048, 768], P('row', 'seq'), may hold values from -6 to 6
- cotangent: bfloat16 [2, 2048, 768], P('row', 'seq'), may hold values from -6 to 6
- clip_lengths: int32 [2, 6], P('row'), may hold values from 1 to 2043, as said below
- query_weight: bfloat16 [768, 768], replicated, may hold values from -0.21875 to 0.21875
- query_bias: bfloat16 [768], replicated, may hold values from -3 to 3
- key_weight: bfloat16 [768, 768], replicated, may hold values from -0.21875 to 0.21875
- value_weight: bfloat16 [768, 768], replicated, may hold values from -0.21875 to 0.21875
- value_bias: bfloat16 [768], replicated, may hold values from -0.059814453 to 0.059814453
- out_weight: bfloat16 [768, 768], replicated, may hold values from -6 to 6
- out_bias: bfloat16 [768], replicated, may hold values from -2 to 2
- first_gain: bfloat16 [768], replicated, may hold values from 0.25 to 1.75
- first_shift: bfloat16 [768], replicated, may hold values from -2 to 2
- up_weight: bfloat16 [768, 3072], replicated, may hold values from -0.21875 to 0.21875
- up_bias: bfloat16 [3072], replicated, may hold values from -3 to 3
- down_weight: bfloat16 [3072, 768], replicated, may hold values from -0.109375 to 0.109375
- down_bias: bfloat16 [768], replicated, may hold values from -2 to 2
- second_gain: bfloat16 [768], replicated, may hold values from 0.25 to 1.75
- second_shift: bfloat16 [768], replicated, may hold values from -2 to 2
Outputs:
- outputs: bfloat16 [2, 2048, 768], P('row', 'seq')
- input_grad: float32 [2, 2048, 768], P('row', 'seq')
- grad_query_weight: float32 [768, 768], P('seq')
- grad_query_bias: float32 [768], P('seq')
- grad_key_weight: float32 [768, 768], P('seq')
- grad_value_weight: float32 [768, 768], P('seq')
- grad_value_bias: float32 [768], P('seq')
- grad_out_weight: float32 [768, 768], P('seq')
- grad_out_bias: float32 [768], P('seq')
- grad_first_gain: float32 [768], P('seq')
- grad_first_shift: float32 [768], P('seq')
- grad_up_weight: float32 [768, 3072], P('seq')
- grad_up_bias: float32 [3072], P('seq')
- grad_down_weight: float32 [3072, 768], P('seq')
- grad_down_bias: float32 [768], P('seq')
- grad_second_gain: float32 [768], P('seq')
- grad_second_shift: float32 [768], P('seq')
The draws below stay inside these ranges and needn't reach their ends.
Inputs may be any that keep to these rules, and one draw needn't show every extreme that they name: `clip_lengths`: each row's clip lengths sum to at most 2048; frames after that sum are padding; in every draw one row is filled to all 2048 frames.
All inputs are finite; a program needn't handle non-finite values.
Results may differ from the reference program's by a relative error of at most 0.028.
Values may be sent and summed in bfloat16 or wider, within the bound.
A program may use at most 128 MiB of HBM per device.

```python
import jax
import jax.numpy as jnp
from jax import lax

D = 768
H = 12
HD = 64
FF = 3072
FR_DEV = 128
CLIPS = 6
LEN = 2048
ROWS = 2


def draw_clip_lengths(key, part):
    key = jax.random.fold_in(key, 11)
    keys = jax.random.split(key, 4)
    short_most = max(1, FR_DEV // 16)
    shorts = jax.random.randint(keys[0], (ROWS, CLIPS), 1, short_most + 1)
    where_long = jax.random.randint(keys[1], (ROWS, 1), 0, CLIPS)
    padding = jax.random.randint(keys[2], (ROWS, 1), 0, FR_DEV // 4 + 1)
    full_row = jax.random.randint(keys[3], (1, 1), 0, ROWS)
    picked = jnp.arange(ROWS, dtype=jnp.int32)[:, None] == full_row
    shorts = jnp.where(picked, 1, shorts)
    padding = jnp.where(picked, 0, padding)
    chosen = jnp.arange(CLIPS, dtype=jnp.int32)[None, :] == where_long
    others = jnp.sum(jnp.where(chosen, 0, shorts), axis=1, keepdims=True)
    long_clip = LEN - others - padding
    return jnp.where(chosen, long_clip, shorts).astype(jnp.int32)


def shard_levels(own_key, shape, pieces, low, top_value):
    level, own = 1.0, jax.random.fold_in(own_key, 6)
    for dim, parts in pieces:
        steps = jnp.exp(jax.random.uniform(jax.random.fold_in(own, dim), (parts,), jnp.float32, low / len(pieces), top_value / len(pieces)))
        level = level * jnp.repeat(steps, shape[dim] // parts).reshape([-1 if axis == dim else 1 for axis in range(len(shape))])
    return level


def normal_values(own_key, dims, spread, bound, pieces=(), kind=jnp.bfloat16):
    drawn = jax.random.normal(own_key, dims, jnp.float32) * spread
    if len(pieces) > 0:
        drawn = shard_levels(own_key, dims, pieces, -0.22, 0.18) * drawn
    return jnp.clip(drawn, min=-bound, max=bound).astype(kind)


def setup_inputs(seed: int = 0) -> dict:
    key_list = jax.random.split(jax.random.key(seed), 19)
    return {
        "inputs": normal_values(key_list[0], (ROWS, LEN, D), 1.0, 6.0, ((0, 2), (1, 16))),
        "cotangent": normal_values(key_list[1], (ROWS, LEN, D), 1.0, 6.0, ((0, 2), (1, 16))),
        "clip_lengths": draw_clip_lengths(jax.random.fold_in(key_list[18], 71), 0),
        "query_weight": normal_values(key_list[3], (D, D), D ** -0.5, 0.21875),
        "query_bias": normal_values(key_list[4], (D,), 0.5, 3.0),
        "key_weight": normal_values(key_list[5], (D, D), D ** -0.5, 0.21875),
        "value_weight": normal_values(key_list[6], (D, D), D ** -0.5, 0.21875),
        "value_bias": normal_values(key_list[7], (D,), 0.01, 0.059814453),
        "out_weight": normal_values(key_list[8], (D, D), 1.0, 6.0),
        "out_bias": normal_values(key_list[9], (D,), 0.3, 2.0),
        "first_gain": jnp.clip(1.0 + 0.15 * jax.random.normal(key_list[10], (D,), jnp.float32), 0.25, 1.75).astype(jnp.bfloat16),
        "first_shift": normal_values(key_list[11], (D,), 0.3, 2.0),
        "up_weight": normal_values(key_list[12], (D, FF), D ** -0.5, 0.21875),
        "up_bias": normal_values(key_list[13], (FF,), 0.5, 3.0),
        "down_weight": normal_values(key_list[14], (FF, D), FF ** -0.5, 0.109375),
        "down_bias": normal_values(key_list[15], (D,), 0.3, 2.0),
        "second_gain": jnp.clip(1.0 + 0.15 * jax.random.normal(key_list[16], (D,), jnp.float32), 0.25, 1.75).astype(jnp.bfloat16),
        "second_shift": normal_values(key_list[17], (D,), 0.3, 2.0),
    }


EPSILON = 1e-05
HIGHEST = lax.Precision.HIGHEST
NEGATIVE = -1e+30

@jax.custom_vjp
def low(v):
    return lax.optimization_barrier(v.astype(jnp.bfloat16)).astype(jnp.float32)

@jax.custom_vjp
def low_back(v):
    return v

def low_keep(v):
    return (low(v), None)

def low_pass(kept, grad):
    return (grad,)

def back_keep(v):
    return (v, None)

def back_low(kept, grad):
    return (low(grad),)
low.defvjp(low_keep, low_pass)
low_back.defvjp(back_keep, back_low)

def segment_ids(lengths, positions):
    clip_ends = jnp.cumsum(lengths)
    counted = lax.optimization_barrier(jnp.sum((positions[:, None] >= clip_ends[None, :]).astype(jnp.int32), axis=1))
    return jnp.where(positions < clip_ends[-1], counted, -1).astype(jnp.int32)

def layer_norm(summed, gain, offset):
    centre = summed - lax.optimization_barrier(jnp.mean(summed, axis=-1, keepdims=True))
    variance = lax.optimization_barrier(jnp.mean(centre * centre, axis=-1, keepdims=True))
    return centre * lax.rsqrt(variance + EPSILON) * gain + offset

def attend_rows(queries, key_heads, value_heads, frame_ids, first_row, block_rows):
    query_part = lax.dynamic_slice_in_dim(queries, first_row, block_rows, 0)
    query_ids = lax.dynamic_slice_in_dim(frame_ids, first_row, block_rows, 0)
    scores = low_back(jnp.einsum('qhd,khd->hqk', query_part, key_heads, precision=HIGHEST) * 0.125)
    allowed = ((query_ids[:, None] == frame_ids[None, :]) & (frame_ids[None, :] >= 0))[None]
    row_top = lax.optimization_barrier(jnp.max(jnp.where(allowed, scores, NEGATIVE), axis=-1, keepdims=True))
    weights = jnp.exp(jnp.where(allowed, scores - row_top, -jnp.inf))
    totals = lax.optimization_barrier(jnp.sum(weights, axis=-1, keepdims=True))
    probs = low(weights / jnp.where(totals > 0.5, totals, 1.0))
    return jnp.einsum('hqk,khd->qhd', probs, value_heads, precision=HIGHEST)

def layer_row(row_values, lengths, params):
    query_weight, query_bias, key_weight, value_weight, value_bias, out_weight, out_bias, first_gain, first_shift, up_weight, up_bias, down_weight, down_bias, second_gain, second_shift = params
    seq_len = row_values.shape[0]
    frame_ids = segment_ids(lengths, jnp.arange(seq_len, dtype=jnp.int32))
    inputs_low = low(row_values)
    queries = low(low_back(jnp.dot(inputs_low, query_weight, precision=HIGHEST) + query_bias)).reshape(seq_len, H, HD)
    key_heads = low(low_back(jnp.dot(inputs_low, key_weight, precision=HIGHEST))).reshape(seq_len, H, HD)
    value_heads = low(low_back(jnp.dot(inputs_low, value_weight, precision=HIGHEST) + value_bias)).reshape(seq_len, H, HD)
    block_rows = min(512, seq_len)
    starts = jnp.arange(seq_len // block_rows, dtype=jnp.int32) * block_rows
    attend = jax.checkpoint(lambda first_row: attend_rows(queries, key_heads, value_heads, frame_ids, first_row, block_rows))
    attended = lax.map(attend, starts).reshape(seq_len, H * HD)
    mixed = low(low_back(attended))
    branch = low_back(jnp.dot(mixed, out_weight, precision=HIGHEST) + out_bias)
    normed = layer_norm(row_values + branch, first_gain, first_shift)
    hidden = low_back(jnp.dot(low(normed), up_weight, precision=HIGHEST) + up_bias)
    activated = low(jax.nn.gelu(hidden, approximate=False))
    feed_out = low_back(jnp.dot(activated, down_weight, precision=HIGHEST) + down_bias)
    return layer_norm(normed + feed_out, second_gain, second_shift)

def reference(inputs, cotangent, clip_lengths, query_weight, query_bias, key_weight, value_weight, value_bias, out_weight, out_bias, first_gain, first_shift, up_weight, up_bias, down_weight, down_bias, second_gain, second_shift):
    params = tuple((argument.astype(jnp.float32) for argument in (query_weight, query_bias, key_weight, value_weight, value_bias, out_weight, out_bias, first_gain, first_shift, up_weight, up_bias, down_weight, down_bias, second_gain, second_shift)))

    def forward(values_in, weights_in):
        row_layer = jax.checkpoint(lambda row_values, lengths: layer_row(row_values, lengths, weights_in))
        return lax.map(lambda row_pair: row_layer(row_pair[0], row_pair[1]), (values_in, clip_lengths))
    result, pullback = jax.vjp(forward, inputs.astype(jnp.float32), params)
    input_grad, weight_grads = pullback(cotangent.astype(jnp.float32))
    return (result.astype(jnp.bfloat16), input_grad, weight_grads[0], weight_grads[1], weight_grads[2], weight_grads[3], weight_grads[4], weight_grads[5], weight_grads[6], weight_grads[7], weight_grads[8], weight_grads[9], weight_grads[10], weight_grads[11], weight_grads[12], weight_grads[13], weight_grads[14])
```

```python
import functools
from types import SimpleNamespace as Refs

import jax
import jax.numpy as jnp
from jax import lax
from jax.experimental import pallas as pl
from jax.experimental.pallas import tpu as pltpu
from jax.sharding import PartitionSpec as P

H = 12
HEAD = 64
EPSILON = 1e-05
NEGATIVE = -1e30
MASKED = -2e30
MESH = pl.DeviceIdType.MESH
F32 = jnp.float32
BF16 = jnp.bfloat16


def nn(left, right):
    return lax.dot_general(left, right, (((1,), (0,)), ((), ())), preferred_element_type=F32)


def nt(left, right):
    return lax.dot_general(left, right, (((1,), (1,)), ((), ())), preferred_element_type=F32)


def norm_parts(summed):
    centre = summed - jnp.mean(summed, axis=-1, keepdims=True)
    variance = jnp.mean(centre * centre, axis=-1, keepdims=True)
    scale_inv = lax.rsqrt(variance + EPSILON)
    return (centre * scale_inv, scale_inv)


def norm_back(upstream, normal, scale_inv):
    return scale_inv * (
        upstream
        - jnp.mean(upstream, axis=-1, keepdims=True)
        - normal * jnp.mean(upstream * normal, axis=-1, keepdims=True)
    )


def gelu_parts(hidden):
    cumulative = 0.5 * (1.0 + lax.erf(hidden * 0.7071067811865476))
    density = jnp.exp(-0.5 * hidden * hidden) * 0.3989422804014327
    return hidden * cumulative, cumulative + hidden * density


Q_BIAS, V_BIAS, OUT_BIAS, GAIN1, SHIFT1, DOWN_BIAS, GAIN2, SHIFT2, UP_BIAS = range(9)


def layer_kernel(names, S, R, *refs):
    n = Refs(**dict(zip(names, refs, strict=True)))
    D = n.x.shape[1]
    F = n.x.shape[0]
    FF = n.wd_hbm.shape[0]
    T, DH, FH = 2 * F, D // 2, FF // 2
    C = S // 2
    N = C // 2
    CR = D // C
    CD = FF // C
    pairs = DH // (2 * HEAD)
    heads = DH // HEAD
    TILE = 256
    roomy = C <= 8
    tiles = FH // TILE

    place = lax.axis_index("seq")
    row = lax.axis_index("row")
    core = lax.rem(place, 2)
    chip = place // 2
    pos = jnp.where(lax.rem(chip, 2) == 0, chip // 2, C - 1 - chip // 2)

    def around(steps):
        return lax.rem(pos + (steps + C), C)

    def chip_at(where):
        return jnp.where(where < N, 2 * where, 2 * (C - 1 - where) + 1)

    sibling = (2 * chip + 1 - core, row)
    right = (2 * chip_at(around(1)) + core, row)
    left = (2 * chip_at(around(-1)) + core, row)
    ring = (right, left)
    parity = lax.rem(row, 2)
    mate_row = row + 1 - 2 * parity
    mate = (place, mate_row)
    others = []
    for dr in range(R):
        for dc in range(2):
            if dr or dc:
                others.append((lax.rem(row + dr, R), lax.rem(core + dc, 2)))

    def remote(src, dst, send, recv, device):
        return pltpu.make_async_remote_copy(
            src_ref=src, dst_ref=dst, send_sem=send, recv_sem=recv, device_id=device, device_id_type=MESH
        )

    started = []

    def start(copy):
        copy.start()
        started.append(copy)

    half_d = pl.multiple_of(core * DH, 128)
    half_f = pl.multiple_of(core * FH, 128)
    loads = []
    for source, target in (
        (n.wq_hbm.at[:, pl.ds(half_d, DH)], n.wq),
        (n.wk_hbm.at[:, pl.ds(half_d, DH)], n.wk),
        (n.wv_hbm.at[:, pl.ds(half_d, DH)], n.wv),
        (n.wo_hbm, n.wo),
        (n.wu_hbm.at[:, pl.ds(half_f, FH)], n.wu),
        (n.wd_hbm.at[pl.ds(half_f, FH)], n.wd),
    ):
        loads.append(pltpu.make_async_copy(source, target, n.load_sem.at[len(loads)]))
        loads[-1].start()

    barrier = pltpu.get_barrier_semaphore()
    partners = [right, left] + [(2 * chip + c, r) for r, c in others]
    for device in partners:
        pl.semaphore_signal(barrier, inc=1, device_id=device, device_id_type=MESH)
    pl.semaphore_wait(barrier, len(partners))

    xa = n.xa
    own_rows = pl.multiple_of(core * F, F)
    other_rows = pl.multiple_of((1 - core) * F, F)
    xa[pos, pl.ds(own_rows, F)] = n.x[...]

    def hop_view(where, piece):
        return xa.at[where, pl.ds(pl.multiple_of(own_rows + piece * (F // 2), F // 2), F // 2)]

    def hop_send(d, h, piece):
        view = hop_view(around((h - 1) * (2 * d - 1)), piece)
        return remote(view, view, n.g_send.at[d, h - 1, piece], n.g_recv.at[d, h - 1, piece], ring[d])

    def hop_recv(d, h, piece):
        view = hop_view(around(h * (2 * d - 1)), piece)
        return remote(view, view, n.g_send.at[d, h - 1, piece], n.g_recv.at[d, h - 1, piece], ring[d])

    def share_send(where):
        view = xa.at[where, pl.ds(own_rows, F)]
        return remote(view, view, n.s_send.at[where], n.s_recv.at[where], sibling)

    def share_recv(where):
        view = xa.at[where, pl.ds(other_rows, F)]
        return remote(view, view, n.s_send.at[where], n.s_recv.at[where], sibling)

    for piece in range(2):
        hop_send(0, 1, piece).start()
        hop_send(1, 1, piece).start()
        if piece == 0:
            share_send(pos).start()

    def gather_step(step):
        h, piece = 1 + step // 2, lax.rem(step, 2)

        @pl.when(step < 2 * N - 2)
        def _():
            hop_recv(0, h, piece).wait_recv()
            hop_recv(1, h, piece).wait_recv()

            @pl.when((h < N - 1) | (piece == 0))
            def _():
                hop_send(0, h + 1, piece).start()

            @pl.when((h < N - 1) | (piece == 1))
            def _():
                hop_send(1, h + 1, piece).start()

            @pl.when(piece == 1)
            def _():
                share_send(around(-h)).start()
                share_send(around(h)).start()

        @pl.when(step == 2 * N - 2)
        def _():
            hop_recv(0, N, 0).wait_recv()
            hop_recv(1, N, 1).wait_recv()
            share_send(around(N)).start()

    def gather_sent():
        for h in range(1, N + 1):
            for piece in range(2):
                for d in range(2):
                    if h < N or piece == d:
                        hop_send(d, h, piece).wait_send()

        def shared(where, carry):
            share_send(where).wait_send()
            return carry

        lax.fori_loop(0, C, shared, 0)

    for index, vector in enumerate(
        (n.bias_q, n.bias_v, n.bias_o, n.gain1, n.shift1, n.bias_d, n.gain2, n.shift2)
    ):
        n.vec[index : index + 1] = vector[...].astype(F32).reshape(1, D)
    for index in range(FF // D):
        n.vec[UP_BIAS + index : UP_BIAS + index + 1] = (
            n.bias_u[D * index : D * (index + 1)].astype(F32).reshape(1, D)
        )

    ends = []
    total = 0
    for i in range(n.lens.shape[1]):
        total = total + n.lens[0, i]
        ends.append(total)

    def ids(positions, padding):
        counted = jnp.zeros_like(positions)
        for end in ends:
            counted = counted + (positions >= end).astype(jnp.int32)
        return jnp.where(positions < ends[-1], counted, padding)

    query_ids = ids(lax.broadcasted_iota(jnp.int32, (1, T), 1) + chip * T, -1)

    def set_bias(where):
        key_ids = ids(lax.broadcasted_iota(jnp.int32, (T, 1), 0) + chip_at(where) * T, -2)
        n.bias[...] = jnp.where(key_ids == query_ids, 0.0, MASKED)

    lane = lax.broadcasted_iota(jnp.int32, (T, 2 * HEAD), 1)

    def head_masked(values, target):
        for pair in range(pairs):
            both = values[:, 2 * HEAD * pair : 2 * HEAD * (pair + 1)]
            target[2 * pair] = jnp.where(lane < HEAD, both, 0.0).astype(BF16)
            target[2 * pair + 1] = jnp.where(lane < HEAD, 0.0, both).astype(BF16)

    def key_rows(where):
        return pl.ds(pl.multiple_of(where * T, T), T)

    def forward_block(where):
        xk = xa[where]
        keys = nn(xk, n.wk[...]).astype(BF16)
        n.ka[key_rows(where), :] = keys
        if roomy:
            n.kt[:, key_rows(where)] = keys.T
        values = (nn(xk, n.wv[...]) + n.vec[V_BIAS : V_BIAS + 1, pl.ds(half_d, DH)]).astype(BF16)
        n.va[key_rows(where), :] = values
        values_t = values.T
        set_bias(where)
        for j in range(heads):
            pair = j // 2
            st = nt(keys[:, 2 * HEAD * pair : 2 * HEAD * (pair + 1)], n.qm[j]) + n.bias[...]
            top = n.top[j : j + 1]
            new_top = jnp.maximum(top, jnp.max(st, axis=0, keepdims=True))
            weights = jnp.exp(st - new_top)
            factor = jnp.exp(top - new_top)
            n.tot[j : j + 1] = n.tot[j : j + 1] * factor + jnp.sum(weights, axis=0, keepdims=True)
            n.top[j : j + 1] = new_top
            span = slice(HEAD * j, HEAD * (j + 1))
            n.ot[span] = n.ot[span] * factor + nn(values_t[span], weights.astype(BF16))

    n.top[...] = jnp.full(n.top.shape, NEGATIVE, F32)
    n.tot[...] = jnp.zeros(n.tot.shape, F32)
    n.ot[...] = jnp.zeros(n.ot.shape, F32)
    small = n.small.at[core]
    small[...] = jnp.zeros(small.shape, F32)

    for load in loads[:3]:
        load.wait()
    share_recv(pos).wait_recv()
    queries = (nn(xa[pos], n.wq[...]) + n.vec[Q_BIAS : Q_BIAS + 1, pl.ds(half_d, DH)]).astype(BF16)
    head_masked(queries.astype(F32) * 0.125, n.qm)

    def forward_step(step, carry):
        gather_step(step)

        @pl.when(step != 1)
        def _():
            index = jnp.maximum(step - 1, 0)
            where = around((index + 1) // 2 * (1 - 2 * lax.rem(index, 2)))

            @pl.when(step > 0)
            def _():
                share_recv(where).wait_recv()

            forward_block(where)

        return carry

    lax.fori_loop(0, 2 * N + 1, forward_step, 0)

    def turn_block(where, carry):
        n.xt[:, key_rows(where)] = xa[where].T
        return carry

    def turn_blocks(first, last):
        lax.fori_loop(first, last, turn_block, 0)

    gather_sent()
    safe = jnp.where(n.tot[...] > 0.5, n.tot[...], 1.0)
    n.lse[...] = n.top[...] + jnp.log(safe)
    for j in range(heads):
        span = slice(HEAD * j, HEAD * (j + 1))
        n.ot[span] = n.ot[span] / safe[j : j + 1]

    def swap(index, src, dst, landed):
        send, recv = n.m_send.at[index], n.m_recv.at[index]
        start(remote(src, dst, send, recv, sibling))
        return remote(src, landed, send, recv, sibling)

    def lend(index, src, dst, device, landed, recv_index=None):
        recv_index = index if recv_index is None else recv_index
        start(remote(src, dst, n.y_send.at[index], n.y_recv.at[recv_index], device))
        return remote(src, landed, n.y_send.at[index], n.y_recv.at[index], device)

    def sent(copy):
        started[:] = [other for other in started if other is not copy]
        copy.wait_send()

    obt = n.obt
    own_half = pl.ds(pl.multiple_of(core * DH, DH), DH)
    other_half = pl.ds(pl.multiple_of((1 - core) * DH, DH), DH)
    obt[own_half] = n.ot[...].astype(BF16)
    swapped = swap(0, obt.at[own_half], obt.at[own_half], obt.at[other_half])
    turn_blocks(0, C // 8)
    loads[3].wait()
    swapped.wait_recv()

    def vec(index):
        return n.vec[index : index + 1]

    mixed = obt[:, pl.ds(own_rows, F)].T
    branch = nn(mixed, n.wo[...]) + vec(OUT_BIAS)
    first_normal, first_scale = norm_parts(n.x[...].astype(F32) + branch)
    n.n1[...] = first_normal
    normed = first_normal * vec(GAIN1) + vec(SHIFT1)
    n.x1[...] = normed
    xb = n.xb
    xb[pl.ds(own_rows, F)] = normed.astype(BF16)
    swapped = swap(1, xb.at[pl.ds(own_rows, F)], xb.at[pl.ds(own_rows, F)], xb.at[pl.ds(other_rows, F)])
    xb_copy = started[-1]
    xbm = n.xbm
    lent_xb = lend(0, xb.at[pl.ds(own_rows, F)], xbm.at[pl.ds(own_rows, F)], mate, xbm.at[pl.ds(own_rows, F)])
    xb_lent = started[-1]
    turn_blocks(C // 8, 3 * C // 8)
    loads[4].wait()
    swapped.wait_recv()

    act, slope = n.act, n.slope
    acto, att = n.acto, n.att
    du = act

    def up_tile(t, carry):
        cols = pl.ds(pl.multiple_of(t * DH, DH), DH)
        bias = n.vec[
            pl.ds(UP_BIAS + core * (FH // D) + t // 2, 1), pl.ds(pl.multiple_of(lax.rem(t, 2) * DH, DH), DH)
        ]
        value, tangent = gelu_parts(nn(xb[...], n.wu[:, cols]) + bias)
        low = value.astype(BF16)
        act[:, cols] = low
        turned = low.T
        for c in range(DH // CD):
            for half in range(2):
                first = CD * c + CD // 2 * half
                acto[t * (DH // CD) + c, half] = turned[first : first + CD // 2]
        slope[:, cols] = tangent.astype(slope.dtype)
        return carry

    lax.fori_loop(0, FH // DH, up_tile, 0)
    own_ff = pl.ds(core * (C // 2), C // 2)
    other_ff = pl.ds((1 - core) * (C // 2), C // 2)
    lent_act = lend(1, acto.at[:, 1 - parity], att.at[1, own_ff], mate, att.at[1, own_ff])
    swapped_act = swap(2, acto.at[:, parity], att.at[0, own_ff], att.at[0, other_ff])
    loads[5].wait()
    part, part_in = n.part, n.part_in

    def down_tile(t, carry):
        cols = pl.ds(pl.multiple_of(t * TILE, TILE), TILE)
        part[:, cols] = nn(act[...], n.wd[:, cols])
        return carry

    lax.fori_loop(0, D // TILE, down_tile, 0)
    swapped = swap(3, part.at[pl.ds(other_rows, F)], part_in, part_in)
    part_copy = started[-1]
    lent_xb.wait_recv()
    swapped_xbm = swap(8, xbm.at[pl.ds(own_rows, F)], xbm.at[pl.ds(own_rows, F)], xbm.at[pl.ds(other_rows, F)])
    turn_blocks(3 * C // 8, 4 * C // 8)
    n.xbt[...] = xb[...].T
    upstream = n.cot[...].astype(F32)
    small[SHIFT2 : SHIFT2 + 1] = jnp.sum(upstream, axis=0, keepdims=True)
    swapped.wait_recv()
    second_normal, second_scale = norm_parts(
        n.x1[...] + part[pl.ds(own_rows, F)] + part_in[...] + vec(DOWN_BIAS)
    )
    n.out[...] = (second_normal * vec(GAIN2) + vec(SHIFT2)).astype(BF16)
    residual = norm_back(upstream * vec(GAIN2), second_normal, second_scale)
    n.grad_x[...] = residual
    low = residual.astype(BF16)
    df = n.df
    df[pl.ds(own_rows, F)] = low
    swapped = swap(4, df.at[pl.ds(own_rows, F)], df.at[pl.ds(own_rows, F)], df.at[pl.ds(other_rows, F)])
    dfm = n.dfm
    lent_df = []
    for c in range(2):
        start(
            remote(
                df.at[pl.ds(own_rows, F), pl.ds(DH * c, DH)],
                dfm.at[pl.ds(own_rows, F)],
                n.y_send.at[2 + c],
                n.y_recv.at[2 + core],
                (2 * chip + c, mate_row),
            )
        )
        lent_df.append(
            remote(
                df.at[pl.ds(own_rows, F), pl.ds(DH * c, DH)],
                dfm.at[pl.ds(F * c, F)],
                n.y_send.at[2 + c],
                n.y_recv.at[2 + c],
                (2 * chip + c, mate_row),
            )
        )
    small[GAIN2 : GAIN2 + 1] = jnp.sum(upstream * second_normal, axis=0, keepdims=True)
    small[DOWN_BIAS : DOWN_BIAS + 1] = jnp.sum(low.astype(F32), axis=0, keepdims=True)
    turn_blocks(4 * C // 8, 7 * C // 8)
    swapped.wait_recv()

    class Flow:
        def __init__(self, index, chunk, landing, split, ready=None):
            self.index, self.chunk, self.landing, self.split, self.ready = index, chunk, landing, split, ready

        def parts(self, d, distance):
            where = around(distance if d == 0 else -distance)
            src, dst = self.chunk(where), self.landing.at[d, distance - 1]
            if distance == N:
                src, dst = src.at[self.split[d]], dst.at[self.split[d]]
            send, recv = n.r_send.at[self.index, d, distance - 1], n.r_recv.at[self.index, d, distance - 1]
            return remote(src, dst, send, recv, ring[d]), dst

        def begin(self):
            if self.ready is not None:
                self.ready(around(N))
            start(self.parts(0, N)[0])
            start(self.parts(1, N)[0])

        def step(self, distance):
            for d in range(2):
                where = around(distance if d == 0 else -distance)
                if self.ready is not None:
                    self.ready(where)
                arriving, landed = self.parts(d, distance + 1)
                arriving.wait_recv()
                target = self.chunk(where)
                if distance + 1 == N:
                    target = target.at[self.split[d]]
                target[...] = (target[...].astype(F32) + landed[...].astype(F32)).astype(BF16)
                start(self.parts(d, distance)[0])

        def end(self):
            if self.ready is not None:
                self.ready(pos)
            found = self.chunk(pos)[...].astype(F32)
            for d in range(2):
                arriving, landed = self.parts(d, 1)
                arriving.wait_recv()
                found = found + landed[...].astype(F32)
            return found

    def add_lent(where):
        c = chip_at(where)
        lent_chunk(c).wait_recv()
        n.ap[c, parity] = (n.ap[c, parity].astype(F32) + n.am[c].astype(F32)).astype(BF16)

    def lent_chunk(c):
        return remote(
            n.ap.at[c, 1 - parity, pl.ds(0, 3)], n.am.at[c, pl.ds(0, 3)], n.ya_send.at[c], n.ya_recv.at[c], mate
        )

    whole = slice(None)
    flow_d = Flow(
        0, lambda where: n.gd_sum.at[chip_at(where)], n.gd_in, [pl.ds(0, CD // 4), pl.ds(CD // 4, CD // 4)]
    )
    flow_u = Flow(
        1,
        lambda where: n.gu_sum.at[chip_at(where)],
        n.gu_in,
        [(whole, pl.ds(0, FH // 4)), (whole, pl.ds(FH // 4, FH // 4))],
    )
    flow_a = Flow(
        2, lambda where: n.ap.at[chip_at(where), parity], n.ga_in, [pl.ds(0, 2), pl.ds(2, 2)], add_lent
    )
    flow_x = Flow(3, lambda where: n.ix_sum.at[where], n.ix_in, [pl.ds(0, F // 2), pl.ds(F // 2, F // 2)])

    def hidden_tile(t, carry):
        cols = pl.ds(pl.multiple_of(t * TILE, TILE), TILE)
        low = (nt(df[...], n.wd[cols, :]) * slope[:, cols].astype(F32)).astype(BF16)
        du[:, cols] = low
        small[
            pl.ds(UP_BIAS + core * (FH // D) + t // (D // TILE), 1),
            pl.ds(pl.multiple_of(lax.rem(t, D // TILE) * TILE, TILE), TILE),
        ] = jnp.sum(low.astype(F32), axis=0, keepdims=True)
        return carry

    lax.fori_loop(0, tiles, hidden_tile, 0)

    quarter = pl.multiple_of(parity * (FH // 2), FH // 2)
    other_quarter = pl.multiple_of((1 - parity) * (FH // 2), FH // 2)
    lent_du = lend(4, du.at[:, pl.ds(other_quarter, FH // 2)], n.dum, mate, n.dum)
    def back_tile(t, carry):
        cols = pl.ds(pl.multiple_of(t * TILE, TILE), TILE)
        part[:, cols] = nt(du[...], n.wu[cols, :])
        return carry

    sent(part_copy)
    lax.fori_loop(0, D // TILE, back_tile, 0)
    swapped = swap(5, part.at[pl.ds(other_rows, F)], part_in, part_in)
    part_copy = started[-1]

    turn_blocks(7 * C // 8, C)
    swapped.wait_recv()
    grad_normed = n.grad_x[...] + part[pl.ds(own_rows, F)] + part_in[...]
    normal = n.n1[...]
    small[GAIN1 : GAIN1 + 1] = jnp.sum(grad_normed * normal, axis=0, keepdims=True)
    small[SHIFT1 : SHIFT1 + 1] = jnp.sum(grad_normed, axis=0, keepdims=True)
    grad_branch = norm_back(grad_normed * vec(GAIN1), normal, first_scale)
    n.x1[...] = grad_branch
    low = grad_branch.astype(BF16)
    sent(xb_copy)
    sent(xb_lent)
    da = xb
    da[pl.ds(own_rows, F)] = low
    swapped = swap(6, da.at[pl.ds(own_rows, F)], da.at[pl.ds(own_rows, F)], da.at[pl.ds(other_rows, F)])
    small[OUT_BIAS : OUT_BIAS + 1] = jnp.sum(low.astype(F32), axis=0, keepdims=True)
    swapped_xbm.wait_recv()
    n.xmt[...] = xbm[...].T
    lent_act.wait_recv()
    swapped_actm = swap(9, att.at[1, own_ff], att.at[1, own_ff], att.at[1, other_ff])
    att[0, own_ff] = acto[:, parity]
    swapped.wait_recv()

    grad_mixed = nt(da[...], n.wo[own_half]).astype(BF16).astype(F32)
    head_masked(grad_mixed, n.dm)
    grad_mixed_t = grad_mixed.T
    for j in range(heads):
        span = slice(HEAD * j, HEAD * (j + 1))
        n.delta[j : j + 1] = jnp.sum(grad_mixed_t[span] * n.ot[span], axis=0, keepdims=True)

    def grad_down():
        swapped_act.wait_recv()
        swapped_actm.wait_recv()
        for lent in lent_df:
            lent.wait_recv()

        def tile(t, carry):
            two = pl.ds(2 * t, 2)
            found = nn(att[0, two].reshape(CD, T), df[:, pl.ds(half_d, DH)])
            found = found + nn(att[1, two].reshape(CD, T), dfm[...])
            n.gd_sum[two] = found.astype(BF16).reshape(2, CD // 2, DH)
            return carry

        lax.fori_loop(0, C // 2, tile, 0)

    def grad_up():
        lent_du.wait_recv()

        def tile(t, carry):
            cols = pl.ds(pl.multiple_of(t * TILE, TILE), TILE)
            found = nn(n.xbt[...], du[:, pl.ds(pl.multiple_of(quarter + t * TILE, TILE), TILE)])
            found = (found + nn(n.xmt[...], n.dum[:, cols])).astype(BF16)
            for c in range(C):
                n.gu_sum[c, :, cols] = found[CR * c : CR * (c + 1)]
            return carry

        lax.fori_loop(0, FH // 2 // TILE, tile, 0)

    def grad_attention(index, left, right):
        for t in range(2):
            found = nn(left(pl.ds(DH * t, DH)), right)
            for c in range(DH // CR):
                for half in range(2):
                    first = CR * c + CR // 2 * half
                    n.ap[DH // CR * t + c, half, index] = found[first : first + CR // 2].astype(BF16)

    n.dqt[...] = jnp.zeros(n.dqt.shape, F32)
    n.vsum[...] = jnp.zeros(n.vsum.shape, F32)

    def backward_block(where):
        rows = key_rows(where)
        set_bias(where)
        for pair in range(pairs):
            cols = slice(2 * HEAD * pair, 2 * HEAD * (pair + 1))
            keys, values = n.ka[rows, cols], n.va[rows, cols]
            grad_key, grad_value = 0.0, 0.0
            keys_t = n.kt[cols, rows] if roomy else keys.T
            for j in (2 * pair, 2 * pair + 1):
                st = nt(keys, n.qm[j]) + n.bias[...]
                probs = jnp.exp(st - n.lse[j : j + 1])
                grad_probs = nt(values, n.dm[j])
                grad_scores = (probs * (grad_probs - n.delta[j : j + 1])).astype(BF16)
                grad_value = grad_value + nn(probs.astype(BF16), n.dm[j])
                grad_key = grad_key + nn(grad_scores, n.qm[j])
                span = slice(HEAD * j, HEAD * (j + 1))
                n.dqt[span] += nn(keys_t[HEAD * (j % 2) : HEAD * (j % 2 + 1)], grad_scores)
            n.ka[rows, cols] = grad_key.astype(BF16)
            low = grad_value.astype(BF16)
            n.va[rows, cols] = low
            n.vsum[:, cols] += jnp.sum(low.astype(F32), axis=0, keepdims=True)
        return nt(n.ka[rows], n.wk[...]) + nt(n.va[rows], n.wv[...])

    def cross(where):
        send, recv = n.c_send.at[where], n.c_recv.at[where]
        return remote(xa.at[where, pl.ds(0, F)], xa.at[where, pl.ds(F, F)], send, recv, sibling)

    def key_block(where, extra=None):
        found = backward_block(where)
        if extra is not None:
            found = found + extra()
        part[...] = found
        xa[where, pl.ds(0, F)] = part[pl.ds(other_rows, F)].astype(BF16)
        n.ix_sum[where] = part[pl.ds(own_rows, F)].astype(BF16)

    def join(where):
        cross(where).wait_recv()
        n.ix_sum[where] = (
            n.ix_sum[where].astype(F32) + xa[where, pl.ds(F, F)].astype(F32)
        ).astype(BF16)

    sent(part_copy)
    key_block(around(N))
    start(cross(around(N)))
    grad_down()
    flow_d.begin()
    join(around(N))
    flow_x.begin()
    for distance in range(N - 1, 0, -1):

        def two_keys(i, carry, distance=distance):
            key_block(around((1 - 2 * i) * distance))
            return carry

        lax.fori_loop(0, 2, two_keys, 0)
        start(cross(around(distance)))
        start(cross(around(-distance)))
        if distance == N - 1:
            grad_up()
            flow_u.begin()
            grad_attention(3, lambda rows: obt[rows], da[:, pl.ds(half_d, DH)])
            lent_out = lend(5, n.ap.at[:, 1 - parity, 3], n.am.at[:, 3], mate, n.am.at[:, 3])
        join(around(distance))
        join(around(-distance))
        flow_x.step(distance)

    feed_steps = list(range(N - 1, -1, -1))

    def feed_step():
        if not feed_steps:
            return
        distance = feed_steps.pop(0)
        if distance > 0:
            flow_d.step(distance)
            flow_u.step(distance)
        else:
            n.fd[...] = flow_d.end().astype(n.fd.dtype)
            spread(0, n.fd, n.yd)
            found = flow_u.end()
            for c in range(2):
                n.fu[c] = found[CR // 2 * c : CR // 2 * (c + 1)].astype(n.fu.dtype)
            scatter(1, n.fu, n.yu, True)

    def query_part():
        grad_query = (n.dqt[...] * 0.125).T.astype(BF16)
        n.dq[...] = grad_query
        return nt(grad_query, n.wq[...])

    key_block(pos, query_part)
    start(cross(pos))
    small[Q_BIAS : Q_BIAS + 1, pl.ds(half_d, DH)] = jnp.sum(n.dq[...].astype(F32), axis=0, keepdims=True)
    small[V_BIAS : V_BIAS + 1, pl.ds(half_d, DH)] = n.vsum[...]
    small_swap = swap(7, small, small, n.small.at[1 - core])

    grad_attention(0, lambda rows: n.xt[rows, key_rows(pos)], n.dq[...])
    grad_attention(1, lambda rows: n.xt[rows], n.ka[...])
    grad_attention(2, lambda rows: n.xt[rows], n.va[...])
    for distance in range(N, -1, -1):
        for where in [around(distance)] + ([around(-distance)] if 0 < distance < N else []):
            start(lent_chunk(chip_at(where)))

    feed_step()
    small_swap.wait_recv()
    around_small = n.small_ring
    mine = pl.ds(pl.multiple_of(core * 8, 8), 8)
    around_small[pos] = n.small[0, mine] + n.small[1, mine]

    def small_send(d, h):
        view = around_small.at[around(1 - h if d == 0 else h - 1)]
        return remote(view, view, n.sr_send.at[d, h - 1], n.sr_recv.at[d, h - 1], ring[d])

    def small_recv(d, h):
        view = around_small.at[around(-h if d == 0 else h)]
        return remote(view, view, n.sr_send.at[d, h - 1], n.sr_recv.at[d, h - 1], ring[d])

    start(small_send(0, 1))
    start(small_send(1, 1))

    def scatter(index, source, gathered, split):
        gathered[row, core] = source[core] if split else source[...]
        for k, (r, c) in enumerate(others):
            view = source.at[c] if split else source
            start(
                remote(
                    view,
                    gathered.at[row, core],
                    n.f_send.at[index, k],
                    n.f_recv.at[index, row, core],
                    (2 * chip + c, r),
                )
            )

    def collect(index, source, gathered, split):
        for r, c in others:
            view = source.at[c] if split else source
            remote(
                view, gathered.at[r, c], n.f_send.at[index, 0], n.f_recv.at[index, r, c], (2 * chip + c, r)
            ).wait_recv()

    def spread(index, source, gathered):
        @pl.when(core == parity)
        def _():
            gathered[row // 2, core] = source[...]

        for k in range(R):
            copy = spread_copy(index, source, gathered, k)
            if k == 0:
                pl.when(core != parity)(copy.start)
            else:
                copy.start()

    def spread_copy(index, source, gathered, k):
        device = (2 * chip + parity, lax.rem(row + k, R))
        return remote(
            source, gathered.at[row // 2, core], n.f_send.at[index, k], n.f_recv.at[index, row // 2, core], device
        )

    def spread_done(index, source, gathered):
        for q in range(R // 2):
            for c in range(2):
                arriving = remote(
                    source, gathered.at[q, c], n.f_send.at[index, 0], n.f_recv.at[index, q, c], sibling
                )
                pl.when((2 * q + core != row) | (core != c))(arriving.wait_recv)
        for k in range(R):
            copy = spread_copy(index, source, gathered, k)
            if k == 0:
                pl.when(core != parity)(copy.wait_send)
            else:
                copy.wait_send()

    feed_step()
    lent_out.wait_recv()
    flow_a.begin()
    feed_step()
    join(pos)
    n.grad_x[...] = n.x1[...] + flow_x.end()

    for h in range(1, N + 1):
        small_recv(0, h).wait_recv()
        if h < N:
            small_recv(1, h).wait_recv()
            start(small_send(0, h + 1))
            if h + 1 < N:
                start(small_send(1, h + 1))
        if h < N:
            flow_a.step(N - h)
            feed_step()
    found = around_small[0]
    for where in range(1, C):
        found = found + around_small[where]
    n.fs[...] = found
    scatter(3, n.fs, n.ys, False)
    n.fa[...] = flow_a.end().astype(n.fa.dtype)
    spread(2, n.fa, n.ya)
    while feed_steps:
        feed_step()
    spread_done(0, n.fd, n.yd)
    collect(1, n.fu, n.yu, True)
    collect(3, n.fs, n.ys, False)
    spread_done(2, n.fa, n.ya)
    for copy in started:
        copy.wait_send()


def finish_kernel(out, grad_x, yd, yu, ya, ys, *targets):
    (
        to_out,
        to_grad_x,
        to_query,
        to_query_bias,
        to_key,
        to_value,
        to_value_bias,
        to_o,
        to_out_bias,
        to_gain1,
        to_shift1,
        to_up,
        to_up_bias,
        to_down,
        to_down_bias,
        to_gain2,
        to_shift2,
    ) = targets
    R = yu.shape[0]
    D = out.shape[1]
    place = lax.axis_index("seq")

    def over_rows(gathered, *index, first=0, by=1):
        found = gathered[(first, *index)].astype(F32)
        for r in range(first + by, gathered.shape[0], by):
            found = found + gathered[(r, *index)].astype(F32)
        return found

    to_out[...] = out[...]
    to_grad_x[...] = grad_x[...]
    for c in range(2):
        width = yd.shape[-1]
        to_down[:, width * c : width * (c + 1)] = over_rows(yd, c)
        for index, target in enumerate((to_query, to_key, to_value, to_o)):
            target[:, width * c : width * (c + 1)] = over_rows(ya, c, index)
        width = yu.shape[-1]
        for half in range(2):
            first = width * (2 * c + half)
            to_up[:, first : first + width] = over_rows(yu, c, first=half, by=2)
    sums = jnp.concatenate([over_rows(ys, 0), over_rows(ys, 1)])
    width = to_query_bias.shape[0]
    turned = pltpu.roll(sums, lax.rem(D - place * width, D), 1)
    for index, target in (
        (Q_BIAS, to_query_bias),
        (V_BIAS, to_value_bias),
        (OUT_BIAS, to_out_bias),
        (GAIN1, to_gain1),
        (SHIFT1, to_shift1),
        (DOWN_BIAS, to_down_bias),
        (GAIN2, to_gain2),
        (SHIFT2, to_shift2),
    ):
        target[...] = turned[index, :width]
    width = to_up_bias.shape[0]
    per = D // width
    turned = pltpu.roll(sums, lax.rem(D - lax.rem(place, per) * width, D), 1)
    line = lax.broadcasted_iota(jnp.int32, sums.shape, 0) == UP_BIAS + place // per
    to_up_bias[...] = jnp.sum(jnp.where(line, turned, 0.0), axis=0)[:width]


def on_device(
    inputs,
    cotangent,
    clip_lengths,
    query_weight,
    query_bias,
    key_weight,
    value_weight,
    value_bias,
    out_weight,
    out_bias,
    first_gain,
    first_shift,
    up_weight,
    up_bias,
    down_weight,
    down_bias,
    second_gain,
    second_shift,
):
    S, R = lax.axis_size("seq"), lax.axis_size("row")
    _, F, D = inputs.shape
    FF = up_weight.shape[1]
    C = S // 2
    N = C // 2
    T, DH, FH, CR, CD = 2 * F, D // 2, FF // 2, D // C, FF // C
    heads = DH // HEAD
    keys = C * T
    wire = BF16 if CR % 32 == 0 else F32
    wire_d = BF16 if CD % 32 == 0 else F32
    vmem = pl.BlockSpec(memory_space=pltpu.VMEM)
    hbm = pl.BlockSpec(memory_space=pl.ANY)
    operands = dict(
        x=(inputs[0], vmem),
        cot=(cotangent[0], vmem),
        lens=(clip_lengths, pl.BlockSpec(memory_space=pltpu.SMEM)),
        bias_q=(query_bias, vmem),
        bias_v=(value_bias, vmem),
        bias_o=(out_bias, vmem),
        gain1=(first_gain, vmem),
        shift1=(first_shift, vmem),
        bias_d=(down_bias, vmem),
        gain2=(second_gain, vmem),
        shift2=(second_shift, vmem),
        bias_u=(up_bias, vmem),
        wq_hbm=(query_weight, hbm),
        wk_hbm=(key_weight, hbm),
        wv_hbm=(value_weight, hbm),
        wo_hbm=(out_weight, hbm),
        wu_hbm=(up_weight, hbm),
        wd_hbm=(down_weight, hbm),
    )
    results = dict(
        out=((F, D), BF16),
        grad_x=((F, D), F32),
        yd=((R // 2, 2, CD // 2, DH), wire_d),
        yu=((R, 2, CR // 2, FH // 2), wire),
        ya=((R // 2, 2, 4, CR // 2, DH), wire),
        ys=((R, 2, 8, D), F32),
    )
    dma = pltpu.SemaphoreType.DMA
    scratch = dict(
        wq=pltpu.VMEM((D, DH), BF16),
        wk=pltpu.VMEM((D, DH), BF16),
        wv=pltpu.VMEM((D, DH), BF16),
        wo=pltpu.VMEM((D, D), BF16),
        wu=pltpu.VMEM((D, FH), BF16),
        wd=pltpu.VMEM((FH, D), BF16),
        xa=pltpu.VMEM((C, T, D), BF16),
        xt=pltpu.VMEM((D, keys), BF16),
        ka=pltpu.VMEM((keys, DH), BF16),
        va=pltpu.VMEM((keys, DH), BF16),
        bias=pltpu.VMEM((T, T), F32),
        qm=pltpu.VMEM((heads, T, 2 * HEAD), BF16),
        dm=pltpu.VMEM((heads, T, 2 * HEAD), BF16),
        vec=pltpu.VMEM((8 + FF // D, D), F32),
        top=pltpu.VMEM((8, T), F32),
        tot=pltpu.VMEM((8, T), F32),
        lse=pltpu.VMEM((8, T), F32),
        delta=pltpu.VMEM((8, T), F32),
        ot=pltpu.VMEM((DH, T), F32),
        dqt=pltpu.VMEM((DH, T), F32),
        dq=pltpu.VMEM((T, DH), BF16),
        vsum=pltpu.VMEM((1, DH), F32),
        obt=pltpu.VMEM((D, T), BF16),
        n1=pltpu.VMEM((F, D), F32),
        x1=pltpu.VMEM((F, D), F32),
        xb=pltpu.VMEM((T, D), BF16),
        xbt=pltpu.VMEM((D, T), BF16),
        df=pltpu.VMEM((T, D), BF16),
        act=pltpu.VMEM((T, FH), BF16),
        acto=pltpu.VMEM((C // 2, 2, CD // 2, T), BF16),
        att=pltpu.VMEM((2, C, CD // 2, T), BF16),
        xbm=pltpu.VMEM((T, D), BF16),
        xmt=pltpu.VMEM((D, T), BF16),
        dfm=pltpu.VMEM((T, DH), BF16),
        dum=pltpu.VMEM((T, FH // 2), BF16),
        slope=pltpu.VMEM((T, FH), F32 if C <= 8 else BF16),
        part=pltpu.VMEM((T, D), F32),
        part_in=pltpu.VMEM((F, D), F32),
        gd_sum=pltpu.VMEM((C, CD // 2, DH), BF16),
        gd_in=pltpu.VMEM((2, N, CD // 2, DH), BF16),
        gu_sum=pltpu.VMEM((C, CR, FH // 2), BF16),
        gu_in=pltpu.VMEM((2, N, CR, FH // 2), BF16),
        ap=pltpu.VMEM((C, 2, 4, CR // 2, DH), BF16),
        am=pltpu.VMEM((C, 4, CR // 2, DH), BF16),
        ga_in=pltpu.VMEM((2, N, 4, CR // 2, DH), BF16),
        ix_sum=pltpu.VMEM((C, F, D), BF16),
        ix_in=pltpu.VMEM((2, N, F, D), BF16),
        fd=pltpu.VMEM((CD // 2, DH), wire_d),
        fu=pltpu.VMEM((2, CR // 2, FH // 2), wire),
        fa=pltpu.VMEM((4, CR // 2, DH), wire),
        small=pltpu.VMEM((2, 16, D), F32),
        small_ring=pltpu.VMEM((C, 8, D), F32),
        fs=pltpu.VMEM((8, D), F32),
        load_sem=dma((6,)),
        g_send=dma((2, N, 2)),
        g_recv=dma((2, N, 2)),
        s_send=dma((C,)),
        s_recv=dma((C,)),
        m_send=dma((10,)),
        m_recv=dma((10,)),
        r_send=dma((4, 2, N)),
        r_recv=dma((4, 2, N)),
        y_send=dma((6,)),
        y_recv=dma((6,)),
        ya_send=dma((C,)),
        ya_recv=dma((C,)),
        c_send=dma((C,)),
        c_recv=dma((C,)),
        sr_send=dma((2, N)),
        sr_recv=dma((2, N)),
        f_send=dma((4, 2 * R - 1)),
        f_recv=dma((4, R, 2)),
    )
    if C <= 8:
        scratch.update(kt=pltpu.VMEM((DH, keys), BF16))
    names = [*operands, *results, *scratch]
    found = pl.pallas_call(
        functools.partial(layer_kernel, names, S, R),
        out_shape=[jax.ShapeDtypeStruct(shape, kind) for shape, kind in results.values()],
        in_specs=[spec for _, spec in operands.values()],
        out_specs=[vmem] * len(results),
        scratch_shapes=list(scratch.values()),
        compiler_params=pltpu.CompilerParams(
            collective_id=0, has_side_effects=True, vmem_limit_bytes=62 * 1024 * 1024
        ),
        name="layer",
    )(*[value for value, _ in operands.values()])
    shapes = [(F, D), (F, D), (D // S, D), (D // S,), (D // S, D), (D // S, D), (D // S,), (D // S, D)]
    shapes += [(D // S,)] * 3 + [(D // S, FF), (FF // S,), (FF // S, D)] + [(D // S,)] * 3
    kinds = [BF16] + [F32] * (len(shapes) - 1)
    final = pl.pallas_call(
        finish_kernel,
        out_shape=[jax.ShapeDtypeStruct(shape, kind) for shape, kind in zip(shapes, kinds, strict=True)],
        in_specs=[vmem] * len(found),
        out_specs=[vmem] * len(shapes),
        name="finish",
    )(*found)
    return (final[0][None], final[1][None], *final[2:])


def solution(mesh):
    shared = P("seq", None)
    part = P("seq")
    return jax.shard_map(
        on_device,
        mesh=mesh,
        in_specs=(P("row", "seq", None), P("row", "seq", None), P("row", None)) + (P(),) * 15,
        out_specs=(
            P("row", "seq", None),
            P("row", "seq", None),
            shared,
            part,
            shared,
            shared,
            part,
            shared,
            part,
            part,
            part,
            shared,
            part,
            shared,
            part,
            part,
            part,
        ),
        check_vma=False,
    )
```

```python
import functools
from types import SimpleNamespace as Refs

import jax
import jax.numpy as jnp
from jax import lax
from jax.experimental import pallas as pl
from jax.experimental.pallas import tpu as pltpu
from jax.sharding import PartitionSpec as P

H = 12
HEAD = 64
PIECES = 4
EPSILON = 1e-05
NEGATIVE = -1e30
MASKED = -2e30
MESH = pl.DeviceIdType.MESH
F32 = jnp.float32
BF16 = jnp.bfloat16


def nn(left, right):
    return lax.dot_general(left, right, (((1,), (0,)), ((), ())), preferred_element_type=F32)


def nt(left, right):
    return lax.dot_general(left, right, (((1,), (1,)), ((), ())), preferred_element_type=F32)


def norm_parts(summed):
    centre = summed - jnp.mean(summed, axis=-1, keepdims=True)
    variance = jnp.mean(centre * centre, axis=-1, keepdims=True)
    scale_inv = lax.rsqrt(variance + EPSILON)
    return (centre * scale_inv, scale_inv)


def norm_back(upstream, normal, scale_inv):
    return scale_inv * (
        upstream
        - jnp.mean(upstream, axis=-1, keepdims=True)
        - normal * jnp.mean(upstream * normal, axis=-1, keepdims=True)
    )


def gelu_parts(hidden):
    cumulative = 0.5 * (1.0 + lax.erf(hidden * 0.7071067811865476))
    density = jnp.exp(-0.5 * hidden * hidden) * 0.3989422804014327
    return hidden * cumulative, cumulative + hidden * density


Q_BIAS, V_BIAS, OUT_BIAS, GAIN1, SHIFT1, DOWN_BIAS, GAIN2, SHIFT2, UP_BIAS = range(9)


def layer_kernel(names, S, R, *refs):
    n = Refs(**dict(zip(names, refs, strict=True)))
    D = n.x.shape[1]
    F = n.x.shape[0]
    FF = n.wd_hbm.shape[0]
    T, DH, FH = 2 * F, D // 2, FF // 2
    C = S // 2
    N = C // 2
    CR = D // C
    CD = FF // C
    pairs = DH // (2 * HEAD)
    heads = DH // HEAD
    TILE = 256
    roomy = C <= 8
    tiles = FH // TILE

    place = lax.axis_index("seq")
    row = lax.axis_index("row")
    core = lax.rem(place, 2)
    chip = place // 2
    pos = jnp.where(lax.rem(chip, 2) == 0, chip // 2, C - 1 - chip // 2)

    def around(steps):
        return lax.rem(pos + (steps + C), C)

    def chip_at(where):
        return jnp.where(where < N, 2 * where, 2 * (C - 1 - where) + 1)

    sibling = (2 * chip + 1 - core, row)
    right = (2 * chip_at(around(1)) + core, row)
    left = (2 * chip_at(around(-1)) + core, row)
    ring = (right, left)
    parity = lax.rem(row, 2)
    mate_row = row + 1 - 2 * parity
    mate = (place, mate_row)
    others = []
    for dr in range(R):
        for dc in range(2):
            if dr or dc:
                others.append((lax.rem(row + dr, R), lax.rem(core + dc, 2)))

    def remote(src, dst, send, recv, device):
        return pltpu.make_async_remote_copy(
            src_ref=src, dst_ref=dst, send_sem=send, recv_sem=recv, device_id=device, device_id_type=MESH
        )

    started = []

    def start(copy):
        copy.start()
        started.append(copy)

    half_d = pl.multiple_of(core * DH, 128)
    half_f = pl.multiple_of(core * FH, 128)
    loads = []
    for source, target in (
        (n.wq_hbm.at[:, pl.ds(half_d, DH)], n.wq),
        (n.wk_hbm.at[:, pl.ds(half_d, DH)], n.wkv.at[:, pl.ds(0, DH)]),
        (n.wv_hbm.at[:, pl.ds(half_d, DH)], n.wkv.at[:, pl.ds(DH, DH)]),
        (n.wo_hbm, n.wo),
        (n.wu_hbm.at[:, pl.ds(half_f, FH)], n.wu),
        (n.wd_hbm.at[pl.ds(half_f, FH)], n.wd),
    ):
        loads.append(pltpu.make_async_copy(source, target, n.load_sem.at[len(loads)]))
        loads[-1].start()

    barrier = pltpu.get_barrier_semaphore()
    partners = [right, left] + [(2 * chip + c, r) for r, c in others]
    for device in partners:
        pl.semaphore_signal(barrier, inc=1, device_id=device, device_id_type=MESH)
    pl.semaphore_wait(barrier, len(partners))

    xa = n.xa
    own_rows = pl.multiple_of(core * F, F)
    other_rows = pl.multiple_of((1 - core) * F, F)
    xa[pos, pl.ds(own_rows, F)] = n.x[...]

    step_rows = F // PIECES

    def hop_view(where, piece):
        return xa.at[where, pl.ds(pl.multiple_of(own_rows + piece * step_rows, step_rows), step_rows)]

    def hop_send(d, h, piece):
        view = hop_view(around((h - 1) * (2 * d - 1)), piece)
        return remote(view, view, n.g_send.at[d, h - 1, piece], n.g_recv.at[d, h - 1, piece], ring[d])

    def hop_recv(d, h, piece):
        view = hop_view(around(h * (2 * d - 1)), piece)
        return remote(view, view, n.g_send.at[d, h - 1, piece], n.g_recv.at[d, h - 1, piece], ring[d])

    def share_send(where):
        view = xa.at[where, pl.ds(own_rows, F)]
        return remote(view, view, n.s_send.at[where], n.s_recv.at[where], sibling)

    def share_recv(where):
        view = xa.at[where, pl.ds(other_rows, F)]
        return remote(view, view, n.s_send.at[where], n.s_recv.at[where], sibling)

    for piece in range(PIECES):
        hop_send(0, 1, piece).start()
        hop_send(1, 1, piece).start()
        if piece == 0:
            share_send(pos).start()

    def gather_step(h, piece):
        hop_recv(0, h, piece).wait_recv()
        hop_recv(1, h, piece).wait_recv()

        @pl.when((h < N - 1) | (piece < PIECES // 2))
        def _():
            hop_send(0, h + 1, piece).start()

        @pl.when((h < N - 1) | (piece >= PIECES // 2))
        def _():
            hop_send(1, h + 1, piece).start()

        @pl.when(piece == PIECES - 1)
        def _():
            share_send(around(-h)).start()
            share_send(around(h)).start()

    def gather_last():
        for piece in range(PIECES):
            hop_recv(2 * piece // PIECES, N, piece).wait_recv()
        share_send(around(N)).start()

    def gather_sent():
        for h in range(1, N + 1):
            for piece in range(PIECES):
                for d in range(2):
                    if h < N or 2 * piece // PIECES == d:
                        hop_send(d, h, piece).wait_send()

        def shared(where, carry):
            share_send(where).wait_send()
            return carry

        lax.fori_loop(0, C, shared, 0)

    for index, vector in enumerate(
        (n.bias_q, n.bias_v, n.bias_o, n.gain1, n.shift1, n.bias_d, n.gain2, n.shift2)
    ):
        n.vec[index : index + 1] = vector[...].astype(F32).reshape(1, D)
    for index in range(FF // D):
        n.vec[UP_BIAS + index : UP_BIAS + index + 1] = (
            n.bias_u[D * index : D * (index + 1)].astype(F32).reshape(1, D)
        )

    ends = []
    total = 0
    for i in range(n.lens.shape[1]):
        total = total + n.lens[0, i]
        ends.append(total)

    def ids(positions, padding):
        counted = jnp.zeros_like(positions)
        for end in ends:
            counted = counted + (positions >= end).astype(jnp.int32)
        return jnp.where(positions < ends[-1], counted, padding)

    query_ids = ids(lax.broadcasted_iota(jnp.int32, (1, T), 1) + chip * T, -1)

    def score_bias(where):
        key_ids = ids(lax.broadcasted_iota(jnp.int32, (T, 1), 0) + chip_at(where) * T, -2)
        found = jnp.where(key_ids == query_ids, 0.0, MASKED)
        return jnp.concatenate([found, found], axis=1)

    lane = lax.broadcasted_iota(jnp.int32, (T, 2 * HEAD), 1)

    def head_masked(values, target):
        for pair in range(pairs):
            both = values[:, 2 * HEAD * pair : 2 * HEAD * (pair + 1)]
            target[pair, :T] = jnp.where(lane < HEAD, both, 0.0).astype(BF16)
            target[pair, T:] = jnp.where(lane < HEAD, 0.0, both).astype(BF16)

    def of_pair(j):
        return slice(T * (j % 2), T * (j % 2 + 1))

    def of_head(j):
        return slice(HEAD * j, HEAD * (j + 1))

    def key_rows(where):
        return pl.ds(pl.multiple_of(where * T, T), T)

    def forward_block(where):
        xk = xa[where]
        both = nn(xk, n.wkv[...])
        keys = both[:, :DH].astype(BF16)
        scores = [nt(keys[:, 2 * HEAD * p : 2 * HEAD * (p + 1)], n.qm[p]) for p in range(pairs)]
        n.kva[key_rows(where), :DH] = keys
        if roomy:
            n.kt[:, key_rows(where)] = keys.T
        values = (both[:, DH:] + n.vec[V_BIAS : V_BIAS + 1, pl.ds(half_d, DH)]).astype(BF16)
        n.kva[key_rows(where), DH:] = values
        values_t = values.T
        n.xt[:, key_rows(where)] = xk.T
        bias = score_bias(where)
        weights, factors = [], []
        for p in range(pairs):
            st = scores[p] + bias
            top = n.top[p]
            new_top = jnp.maximum(top, jnp.max(st, axis=0, keepdims=True))
            found = jnp.exp(st - new_top)
            factors.append(jnp.exp(top - new_top))
            n.tot[p] = n.tot[p] * factors[p] + jnp.sum(found, axis=0, keepdims=True)
            n.top[p] = new_top
            weights.append(found.astype(BF16))
        for j in range(heads):
            n.ot[of_head(j)] = n.ot[of_head(j)] * factors[j // 2][:, of_pair(j)] + nn(
                values_t[of_head(j)], weights[j // 2][:, of_pair(j)]
            )

    n.top[...] = jnp.full(n.top.shape, NEGATIVE, F32)
    n.tot[...] = jnp.zeros(n.tot.shape, F32)
    n.ot[...] = jnp.zeros(n.ot.shape, F32)
    small = n.small.at[core]
    small[...] = jnp.zeros(small.shape, F32)

    for load in loads[:3]:
        load.wait()
    share_recv(pos).wait_recv()
    queries = (nn(xa[pos], n.wq[...]) + n.vec[Q_BIAS : Q_BIAS + 1, pl.ds(half_d, DH)]).astype(BF16)
    head_masked(queries.astype(F32) * 0.125, n.qm)

    def forward_step(step, carry):
        h, piece = 1 + step // PIECES, lax.rem(step, PIECES)
        gather_step(h, piece)

        @pl.when((step == 0) | ((h > 1) & (piece < 2)))
        def _():
            where = around((h - 1) * (2 * piece - 1))

            @pl.when(step > 0)
            def _():
                share_recv(where).wait_recv()

            forward_block(where)

        return carry

    lax.fori_loop(0, PIECES * (N - 1), forward_step, 0)

    def forward_last(step, carry):
        where = around((N - 1) * (2 * step - 1) - lax.div(step, 2) * (2 * N - 3))

        @pl.when(step == 2)
        def _():
            gather_last()

        share_recv(where).wait_recv()
        forward_block(where)
        return carry

    lax.fori_loop(0, 3, forward_last, 0)

    gather_sent()
    safe = jnp.where(n.tot[...] > 0.5, n.tot[...], 1.0)
    n.lse[...] = n.top[...] + jnp.log(safe)
    for j in range(heads):
        n.ot[of_head(j)] = n.ot[of_head(j)] / safe[j // 2][:, of_pair(j)]

    def swap(index, src, dst, landed):
        send, recv = n.m_send.at[index], n.m_recv.at[index]
        start(remote(src, dst, send, recv, sibling))
        return remote(src, landed, send, recv, sibling)

    def lend(index, src, dst, device, landed, recv_index=None):
        recv_index = index if recv_index is None else recv_index
        start(remote(src, dst, n.y_send.at[index], n.y_recv.at[recv_index], device))
        return remote(src, landed, n.y_send.at[index], n.y_recv.at[index], device)

    def sent(copy):
        started[:] = [other for other in started if other is not copy]
        copy.wait_send()

    obt = n.obt
    own_half = pl.ds(pl.multiple_of(core * DH, DH), DH)
    other_half = pl.ds(pl.multiple_of((1 - core) * DH, DH), DH)
    obt[own_half] = n.ot[...].astype(BF16)
    swapped = swap(0, obt.at[own_half], obt.at[own_half], obt.at[other_half])
    loads[3].wait()
    swapped.wait_recv()

    def vec(index):
        return n.vec[index : index + 1]

    mixed = obt[:, pl.ds(own_rows, F)].T
    branch = nn(mixed, n.wo[...]) + vec(OUT_BIAS)
    first_normal, first_scale = norm_parts(n.x[...].astype(F32) + branch)
    n.n1[...] = first_normal
    normed = first_normal * vec(GAIN1) + vec(SHIFT1)
    n.x1[...] = normed
    xb = n.xb
    xb[pl.ds(own_rows, F)] = normed.astype(BF16)
    swapped = swap(1, xb.at[pl.ds(own_rows, F)], xb.at[pl.ds(own_rows, F)], xb.at[pl.ds(other_rows, F)])
    xb_copy = started[-1]
    xbm = n.xbm
    lent_xb = lend(0, xb.at[pl.ds(own_rows, F)], xbm.at[pl.ds(own_rows, F)], mate, xbm.at[pl.ds(own_rows, F)])
    xb_lent = started[-1]
    loads[4].wait()
    swapped.wait_recv()

    act, slope = n.act, n.slope
    acto, att = n.acto, n.att
    du = act

    def up_tile(t, carry):
        cols = pl.ds(pl.multiple_of(t * DH, DH), DH)
        bias = n.vec[
            pl.ds(UP_BIAS + core * (FH // D) + t // 2, 1), pl.ds(pl.multiple_of(lax.rem(t, 2) * DH, DH), DH)
        ]
        value, tangent = gelu_parts(nn(xb[...], n.wu[:, cols]) + bias)
        low = value.astype(BF16)
        act[:, cols] = low
        turned = low.T
        for c in range(DH // CD):
            for half in range(2):
                first = CD * c + CD // 2 * half
                acto[t * (DH // CD) + c, half] = turned[first : first + CD // 2]
        slope[:, cols] = tangent
        return carry

    lax.fori_loop(0, FH // DH, up_tile, 0)
    own_ff = pl.ds(core * (C // 2), C // 2)
    other_ff = pl.ds((1 - core) * (C // 2), C // 2)
    lent_act = lend(1, acto.at[:, 1 - parity], att.at[1, own_ff], mate, att.at[1, own_ff])
    swapped_act = swap(2, acto.at[:, parity], att.at[0, own_ff], att.at[0, other_ff])
    loads[5].wait()
    part, part_in = n.part, n.part_in

    def down_tile(t, carry):
        cols = pl.ds(pl.multiple_of(t * TILE, TILE), TILE)
        part[:, cols] = nn(act[...], n.wd[:, cols])
        return carry

    lax.fori_loop(0, D // TILE, down_tile, 0)
    swapped = swap(3, part.at[pl.ds(other_rows, F)], part_in, part_in)
    part_copy = started[-1]
    lent_xb.wait_recv()
    swapped_xbm = swap(8, xbm.at[pl.ds(own_rows, F)], xbm.at[pl.ds(own_rows, F)], xbm.at[pl.ds(other_rows, F)])
    n.xbt[...] = xb[...].T
    upstream = n.cot[...].astype(F32)
    small[SHIFT2 : SHIFT2 + 1] = jnp.sum(upstream, axis=0, keepdims=True)
    swapped.wait_recv()
    second_normal, second_scale = norm_parts(
        n.x1[...] + part[pl.ds(own_rows, F)] + part_in[...] + vec(DOWN_BIAS)
    )
    n.out[...] = (second_normal * vec(GAIN2) + vec(SHIFT2)).astype(BF16)
    residual = norm_back(upstream * vec(GAIN2), second_normal, second_scale)
    n.grad_x[...] = residual
    low = residual.astype(BF16)
    df = n.df
    df[pl.ds(own_rows, F)] = low
    swapped = swap(4, df.at[pl.ds(own_rows, F)], df.at[pl.ds(own_rows, F)], df.at[pl.ds(other_rows, F)])
    dfm = n.dfm
    lent_df = []
    for c in range(2):
        start(
            remote(
                df.at[pl.ds(own_rows, F), pl.ds(DH * c, DH)],
                dfm.at[pl.ds(own_rows, F)],
                n.y_send.at[2 + c],
                n.y_recv.at[2 + core],
                (2 * chip + c, mate_row),
            )
        )
        lent_df.append(
            remote(
                df.at[pl.ds(own_rows, F), pl.ds(DH * c, DH)],
                dfm.at[pl.ds(F * c, F)],
                n.y_send.at[2 + c],
                n.y_recv.at[2 + c],
                (2 * chip + c, mate_row),
            )
        )
    small[GAIN2 : GAIN2 + 1] = jnp.sum(upstream * second_normal, axis=0, keepdims=True)
    small[DOWN_BIAS : DOWN_BIAS + 1] = jnp.sum(low.astype(F32), axis=0, keepdims=True)
    swapped.wait_recv()

    class Flow:
        def __init__(self, index, chunk, landing, split, ready=None):
            self.index, self.chunk, self.landing, self.split, self.ready = index, chunk, landing, split, ready

        def parts(self, d, distance):
            where = around(distance if d == 0 else -distance)
            src, dst = self.chunk(where), self.landing.at[d, distance - 1]
            if distance == N:
                src, dst = src.at[self.split[d]], dst.at[self.split[d]]
            send, recv = n.r_send.at[self.index, d, distance - 1], n.r_recv.at[self.index, d, distance - 1]
            return remote(src, dst, send, recv, ring[d]), dst

        def begin(self):
            if self.ready is not None:
                self.ready(around(N))
            start(self.parts(0, N)[0])
            start(self.parts(1, N)[0])

        def step(self, distance):
            for d in range(2):
                where = around(distance if d == 0 else -distance)
                if self.ready is not None:
                    self.ready(where)
                arriving, landed = self.parts(d, distance + 1)
                arriving.wait_recv()
                target = self.chunk(where)
                if distance + 1 == N:
                    target = target.at[self.split[d]]
                target[...] = (target[...].astype(F32) + landed[...].astype(F32)).astype(BF16)
                start(self.parts(d, distance)[0])

        def end(self):
            if self.ready is not None:
                self.ready(pos)
            found = self.chunk(pos)[...].astype(F32)
            for d in range(2):
                arriving, landed = self.parts(d, 1)
                arriving.wait_recv()
                found = found + landed[...].astype(F32)
            return found

    def add_lent(where):
        c = chip_at(where)
        lent_chunk(c).wait_recv()
        n.ap[c, parity] = (n.ap[c, parity].astype(F32) + n.am[c].astype(F32)).astype(BF16)

    def lent_chunk(c):
        return remote(
            n.ap.at[c, 1 - parity, pl.ds(0, 3)], n.am.at[c, pl.ds(0, 3)], n.ya_send.at[c], n.ya_recv.at[c], mate
        )

    whole = slice(None)
    flow_d = Flow(
        0, lambda where: n.gd_sum.at[chip_at(where)], n.gd_in, [pl.ds(0, CD // 4), pl.ds(CD // 4, CD // 4)]
    )
    flow_u = Flow(
        1,
        lambda where: n.gu_sum.at[chip_at(where)],
        n.gu_in,
        [(whole, pl.ds(0, FH // 4)), (whole, pl.ds(FH // 4, FH // 4))],
    )
    flow_a = Flow(
        2, lambda where: n.ap.at[chip_at(where), parity], n.ga_in, [pl.ds(0, 2), pl.ds(2, 2)], add_lent
    )
    flow_x = Flow(3, lambda where: n.ix_sum.at[where], n.ix_in, [pl.ds(0, F // 2), pl.ds(F // 2, F // 2)])

    def hidden_tile(t, carry):
        cols = pl.ds(pl.multiple_of(t * TILE, TILE), TILE)
        low = (nt(df[...], n.wd[cols, :]) * slope[:, cols]).astype(BF16)
        du[:, cols] = low
        small[
            pl.ds(UP_BIAS + core * (FH // D) + t // (D // TILE), 1),
            pl.ds(pl.multiple_of(lax.rem(t, D // TILE) * TILE, TILE), TILE),
        ] = jnp.sum(low.astype(F32), axis=0, keepdims=True)
        return carry

    lax.fori_loop(0, tiles, hidden_tile, 0)

    quarter = pl.multiple_of(parity * (FH // 2), FH // 2)
    other_quarter = pl.multiple_of((1 - parity) * (FH // 2), FH // 2)
    lent_du = lend(4, du.at[:, pl.ds(other_quarter, FH // 2)], n.dum, mate, n.dum)
    def back_tile(t, carry):
        cols = pl.ds(pl.multiple_of(t * TILE, TILE), TILE)
        part[:, cols] = nt(du[...], n.wu[cols, :])
        return carry

    sent(part_copy)
    lax.fori_loop(0, D // TILE, back_tile, 0)
    swapped = swap(5, part.at[pl.ds(other_rows, F)], part_in, part_in)
    part_copy = started[-1]

    swapped.wait_recv()
    grad_normed = n.grad_x[...] + part[pl.ds(own_rows, F)] + part_in[...]
    normal = n.n1[...]
    small[GAIN1 : GAIN1 + 1] = jnp.sum(grad_normed * normal, axis=0, keepdims=True)
    small[SHIFT1 : SHIFT1 + 1] = jnp.sum(grad_normed, axis=0, keepdims=True)
    grad_branch = norm_back(grad_normed * vec(GAIN1), normal, first_scale)
    n.x1[...] = grad_branch
    low = grad_branch.astype(BF16)
    sent(xb_copy)
    sent(xb_lent)
    da = xb
    da[pl.ds(own_rows, F)] = low
    swapped = swap(6, da.at[pl.ds(own_rows, F)], da.at[pl.ds(own_rows, F)], da.at[pl.ds(other_rows, F)])
    small[OUT_BIAS : OUT_BIAS + 1] = jnp.sum(low.astype(F32), axis=0, keepdims=True)
    swapped_xbm.wait_recv()
    n.xmt[...] = xbm[...].T
    lent_act.wait_recv()
    swapped_actm = swap(9, att.at[1, own_ff], att.at[1, own_ff], att.at[1, other_ff])
    att[0, own_ff] = acto[:, parity]
    swapped.wait_recv()

    grad_mixed = nt(da[...], n.wo[own_half]).astype(BF16).astype(F32)
    head_masked(grad_mixed, n.dm)
    grad_mixed_t = grad_mixed.T
    for j in range(heads):
        n.delta[j // 2, :, of_pair(j)] = jnp.sum(grad_mixed_t[of_head(j)] * n.ot[of_head(j)], axis=0, keepdims=True)

    def grad_down():
        swapped_act.wait_recv()
        swapped_actm.wait_recv()
        for lent in lent_df:
            lent.wait_recv()

        def tile(t, carry):
            two = pl.ds(2 * t, 2)
            found = nn(att[0, two].reshape(CD, T), df[:, pl.ds(half_d, DH)])
            found = found + nn(att[1, two].reshape(CD, T), dfm[...])
            n.gd_sum[two] = found.astype(BF16).reshape(2, CD // 2, DH)
            return carry

        lax.fori_loop(0, C // 2, tile, 0)

    def grad_up():
        lent_du.wait_recv()

        def tile(t, carry):
            cols = pl.ds(pl.multiple_of(t * TILE, TILE), TILE)
            found = nn(n.xbt[...], du[:, pl.ds(pl.multiple_of(quarter + t * TILE, TILE), TILE)])
            found = (found + nn(n.xmt[...], n.dum[:, cols])).astype(BF16)
            for c in range(C):
                n.gu_sum[c, :, cols] = found[CR * c : CR * (c + 1)]
            return carry

        lax.fori_loop(0, FH // 2 // TILE, tile, 0)

    def grad_attention(indices, left, right):
        for t in range(2):
            found = nn(left(pl.ds(DH * t, DH)), right)
            for k, index in enumerate(indices):
                for c in range(DH // CR):
                    for half in range(2):
                        first = CR * c + CR // 2 * half
                        n.ap[DH // CR * t + c, half, index] = found[
                            first : first + CR // 2, DH * k : DH * (k + 1)
                        ].astype(BF16)

    n.dqt[...] = jnp.zeros(n.dqt.shape, F32)
    n.vsum[...] = jnp.zeros(n.vsum.shape, F32)

    def backward_block(where):
        rows = key_rows(where)
        bias = score_bias(where)
        keys_t = n.kt[:, rows] if roomy else n.kva[rows, :DH].T

        def wide(p, first=0):
            return slice(first + 2 * HEAD * p, first + 2 * HEAD * (p + 1))

        def long(p):
            return slice(2 * T * p, 2 * T * (p + 1))

        for p in range(pairs):
            n.slope[:, long(p)] = nt(n.kva[rows, wide(p)], n.qm[p])
            n.grad_probs[:, long(p)] = nt(n.kva[rows, wide(p, DH)], n.dm[p])
        for p in range(pairs):
            probs = jnp.exp(n.slope[:, long(p)] + bias - n.lse[p])
            n.probs[:, long(p)] = probs.astype(BF16)
            n.grad_scores[:, long(p)] = (probs * (n.grad_probs[:, long(p)] - n.delta[p])).astype(BF16)
        for p in range(pairs):
            low = nn(n.probs[:, long(p)], n.dm[p]).astype(BF16)
            n.kva[rows, wide(p, DH)] = low
            n.kva[rows, wide(p)] = nn(n.grad_scores[:, long(p)], n.qm[p]).astype(BF16)
            n.vsum[:, wide(p)] += jnp.sum(low.astype(F32), axis=0, keepdims=True)
        for j in range(heads):
            n.dqt[of_head(j)] += nn(keys_t[of_head(j)], n.grad_scores[:, T * j : T * (j + 1)])
        return nt(n.kva[rows], n.wkv[...])

    def cross(where):
        send, recv = n.c_send.at[where], n.c_recv.at[where]
        return remote(xa.at[where, pl.ds(0, F)], xa.at[where, pl.ds(F, F)], send, recv, sibling)

    def key_block(where, extra=None):
        found = backward_block(where)
        if extra is not None:
            found = found + extra()
        part[...] = found
        xa[where, pl.ds(0, F)] = part[pl.ds(other_rows, F)].astype(BF16)
        n.ix_sum[where] = part[pl.ds(own_rows, F)].astype(BF16)

    def join(where):
        cross(where).wait_recv()
        n.ix_sum[where] = (
            n.ix_sum[where].astype(F32) + xa[where, pl.ds(F, F)].astype(F32)
        ).astype(BF16)

    sent(part_copy)
    key_block(around(N))
    start(cross(around(N)))
    grad_down()
    flow_d.begin()
    join(around(N))
    flow_x.begin()

    def down_end():
        n.fd[...] = flow_d.end().astype(n.fd.dtype)
        spread(0, n.fd, n.yd)

    def up_end():
        found = flow_u.end()
        for c in range(2):
            n.fu[c] = found[CR // 2 * c : CR // 2 * (c + 1)].astype(n.fu.dtype)
        scatter(1, n.fu, n.yu, True)

    def input_step(distance):
        join(around(distance))
        join(around(-distance))
        flow_x.step(distance)

    def input_end():
        join(pos)
        n.grad_x[...] = n.x1[...] + flow_x.end()

    def attention_begin():
        lent_out.wait_recv()
        flow_a.begin()

    def attention_end():
        n.fa[...] = flow_a.end().astype(n.fa.dtype)
        spread(2, n.fa, n.ya)

    def chain(step, end):
        return [functools.partial(step, distance) for distance in range(N - 1, 0, -1)] + [end]

    chain_d = chain(flow_d.step, down_end)
    chain_u = chain(flow_u.step, up_end)
    chain_x = chain(input_step, input_end)
    chain_a = [attention_begin] + chain(flow_a.step, attention_end)

    def advance(one):
        if one:
            one.pop(0)()

    for distance in range(N - 1, 0, -1):

        def two_keys(i, carry, distance=distance):
            key_block(around((1 - 2 * i) * distance))
            return carry

        lax.fori_loop(0, 2, two_keys, 0)
        start(cross(around(distance)))
        start(cross(around(-distance)))
        if distance < N - 1:
            advance(chain_x)
        if distance == N - 2:
            grad_up()
            flow_u.begin()
            grad_attention([3], lambda rows: obt[rows], da[:, pl.ds(half_d, DH)])
            lent_out = lend(5, n.ap.at[:, 1 - parity, 3], n.am.at[:, 3], mate, n.am.at[:, 3])
        if distance >= N - 2:
            advance(chain_d)

    def query_part():
        grad_query = (n.dqt[...] * 0.125).T.astype(BF16)
        n.dq[...] = grad_query
        return nt(grad_query, n.wq[...])

    key_block(pos, query_part)
    start(cross(pos))
    advance(chain_u)
    small[Q_BIAS : Q_BIAS + 1, pl.ds(half_d, DH)] = jnp.sum(n.dq[...].astype(F32), axis=0, keepdims=True)
    small[V_BIAS : V_BIAS + 1, pl.ds(half_d, DH)] = n.vsum[...]
    small_swap = swap(7, small, small, n.small.at[1 - core])

    grad_attention([0], lambda rows: n.xt[rows, key_rows(pos)], n.dq[...])
    grad_attention([1, 2], lambda rows: n.xt[rows], n.kva[...])
    for distance in range(N, -1, -1):
        for where in [around(distance)] + ([around(-distance)] if 0 < distance < N else []):
            start(lent_chunk(chip_at(where)))

    small_swap.wait_recv()
    around_small = n.small_ring
    mine = pl.ds(pl.multiple_of(core * 8, 8), 8)
    around_small[pos] = n.small[0, mine] + n.small[1, mine]

    def small_send(d, h):
        view = around_small.at[around(1 - h if d == 0 else h - 1)]
        return remote(view, view, n.sr_send.at[d, h - 1], n.sr_recv.at[d, h - 1], ring[d])

    def small_recv(d, h):
        view = around_small.at[around(-h if d == 0 else h)]
        return remote(view, view, n.sr_send.at[d, h - 1], n.sr_recv.at[d, h - 1], ring[d])

    start(small_send(0, 1))
    start(small_send(1, 1))

    def scatter(index, source, gathered, split):
        gathered[row, core] = source[core] if split else source[...]
        for k, (r, c) in enumerate(others):
            view = source.at[c] if split else source
            start(
                remote(
                    view,
                    gathered.at[row, core],
                    n.f_send.at[index, k],
                    n.f_recv.at[index, row, core],
                    (2 * chip + c, r),
                )
            )

    def collect(index, source, gathered, split):
        for r, c in others:
            view = source.at[c] if split else source
            remote(
                view, gathered.at[r, c], n.f_send.at[index, 0], n.f_recv.at[index, r, c], (2 * chip + c, r)
            ).wait_recv()

    def spread(index, source, gathered):
        @pl.when(core == parity)
        def _():
            gathered[row // 2, core] = source[...]

        for k in range(R):
            copy = spread_copy(index, source, gathered, k)
            if k == 0:
                pl.when(core != parity)(copy.start)
            else:
                copy.start()

    def spread_copy(index, source, gathered, k):
        device = (2 * chip + parity, lax.rem(row + k, R))
        return remote(
            source, gathered.at[row // 2, core], n.f_send.at[index, k], n.f_recv.at[index, row // 2, core], device
        )

    def spread_done(index, source, gathered):
        for q in range(R // 2):
            for c in range(2):
                arriving = remote(
                    source, gathered.at[q, c], n.f_send.at[index, 0], n.f_recv.at[index, q, c], sibling
                )
                pl.when((2 * q + core != row) | (core != c))(arriving.wait_recv)
        for k in range(R):
            copy = spread_copy(index, source, gathered, k)
            if k == 0:
                pl.when(core != parity)(copy.wait_send)
            else:
                copy.wait_send()

    def small_step(h):
        small_recv(0, h).wait_recv()
        if h < N:
            small_recv(1, h).wait_recv()
            start(small_send(0, h + 1))
            if h + 1 < N:
                start(small_send(1, h + 1))

    def small_end():
        found = around_small[0]
        for where in range(1, C):
            found = found + around_small[where]
        n.fs[...] = found
        scatter(3, n.fs, n.ys, False)

    chain_s = [functools.partial(small_step, h) for h in range(1, N + 1)] + [small_end]
    while chain_d or chain_x or chain_a or chain_u or chain_s:
        advance(chain_d)
        advance(chain_x)
        advance(chain_a)
        advance(chain_u)
        advance(chain_s)
    spread_done(0, n.fd, n.yd)
    collect(1, n.fu, n.yu, True)
    collect(3, n.fs, n.ys, False)
    spread_done(2, n.fa, n.ya)
    for copy in started:
        copy.wait_send()


def finish_kernel(out, grad_x, yd, yu, ya, ys, *targets):
    (
        to_out,
        to_grad_x,
        to_query,
        to_query_bias,
        to_key,
        to_value,
        to_value_bias,
        to_o,
        to_out_bias,
        to_gain1,
        to_shift1,
        to_up,
        to_up_bias,
        to_down,
        to_down_bias,
        to_gain2,
        to_shift2,
    ) = targets
    R = yu.shape[0]
    D = out.shape[1]
    place = lax.axis_index("seq")

    def over_rows(gathered, *index, first=0, by=1):
        found = gathered[(first, *index)].astype(F32)
        for r in range(first + by, gathered.shape[0], by):
            found = found + gathered[(r, *index)].astype(F32)
        return found

    to_out[...] = out[...]
    to_grad_x[...] = grad_x[...]
    for c in range(2):
        width = yd.shape[-1]
        to_down[:, width * c : width * (c + 1)] = over_rows(yd, c)
        for index, target in enumerate((to_query, to_key, to_value, to_o)):
            target[:, width * c : width * (c + 1)] = over_rows(ya, c, index)
        width = yu.shape[-1]
        for half in range(2):
            first = width * (2 * c + half)
            to_up[:, first : first + width] = over_rows(yu, c, first=half, by=2)
    sums = jnp.concatenate([over_rows(ys, 0), over_rows(ys, 1)])
    width = to_query_bias.shape[0]
    turned = pltpu.roll(sums, lax.rem(D - place * width, D), 1)
    for index, target in (
        (Q_BIAS, to_query_bias),
        (V_BIAS, to_value_bias),
        (OUT_BIAS, to_out_bias),
        (GAIN1, to_gain1),
        (SHIFT1, to_shift1),
        (DOWN_BIAS, to_down_bias),
        (GAIN2, to_gain2),
        (SHIFT2, to_shift2),
    ):
        target[...] = turned[index, :width]
    width = to_up_bias.shape[0]
    per = D // width
    turned = pltpu.roll(sums, lax.rem(D - lax.rem(place, per) * width, D), 1)
    line = lax.broadcasted_iota(jnp.int32, sums.shape, 0) == UP_BIAS + place // per
    to_up_bias[...] = jnp.sum(jnp.where(line, turned, 0.0), axis=0)[:width]


def on_device(
    inputs,
    cotangent,
    clip_lengths,
    query_weight,
    query_bias,
    key_weight,
    value_weight,
    value_bias,
    out_weight,
    out_bias,
    first_gain,
    first_shift,
    up_weight,
    up_bias,
    down_weight,
    down_bias,
    second_gain,
    second_shift,
):
    S, R = lax.axis_size("seq"), lax.axis_size("row")
    _, F, D = inputs.shape
    FF = up_weight.shape[1]
    C = S // 2
    N = C // 2
    T, DH, FH, CR, CD = 2 * F, D // 2, FF // 2, D // C, FF // C
    heads = DH // HEAD
    keys = C * T
    wire = BF16 if CR % 32 == 0 else F32
    wire_d = BF16 if CD % 32 == 0 else F32
    vmem = pl.BlockSpec(memory_space=pltpu.VMEM)
    hbm = pl.BlockSpec(memory_space=pl.ANY)
    operands = dict(
        x=(inputs[0], vmem),
        cot=(cotangent[0], vmem),
        lens=(clip_lengths, pl.BlockSpec(memory_space=pltpu.SMEM)),
        bias_q=(query_bias, vmem),
        bias_v=(value_bias, vmem),
        bias_o=(out_bias, vmem),
        gain1=(first_gain, vmem),
        shift1=(first_shift, vmem),
        bias_d=(down_bias, vmem),
        gain2=(second_gain, vmem),
        shift2=(second_shift, vmem),
        bias_u=(up_bias, vmem),
        wq_hbm=(query_weight, hbm),
        wk_hbm=(key_weight, hbm),
        wv_hbm=(value_weight, hbm),
        wo_hbm=(out_weight, hbm),
        wu_hbm=(up_weight, hbm),
        wd_hbm=(down_weight, hbm),
    )
    results = dict(
        out=((F, D), BF16),
        grad_x=((F, D), F32),
        yd=((R // 2, 2, CD // 2, DH), wire_d),
        yu=((R, 2, CR // 2, FH // 2), wire),
        ya=((R // 2, 2, 4, CR // 2, DH), wire),
        ys=((R, 2, 8, D), F32),
    )
    dma = pltpu.SemaphoreType.DMA
    scratch = dict(
        wq=pltpu.VMEM((D, DH), BF16),
        wkv=pltpu.VMEM((D, D), BF16),
        wo=pltpu.VMEM((D, D), BF16),
        wu=pltpu.VMEM((D, FH), BF16),
        wd=pltpu.VMEM((FH, D), BF16),
        xa=pltpu.VMEM((C, T, D), BF16),
        xt=pltpu.VMEM((D, keys), BF16),
        kva=pltpu.VMEM((keys, D), BF16),
        qm=pltpu.VMEM((heads // 2, 2 * T, 2 * HEAD), BF16),
        dm=pltpu.VMEM((heads // 2, 2 * T, 2 * HEAD), BF16),
        grad_probs=pltpu.VMEM((T, heads * T), F32),
        probs=pltpu.VMEM((T, heads * T), BF16),
        grad_scores=pltpu.VMEM((T, heads * T), BF16),
        vec=pltpu.VMEM((8 + FF // D, D), F32),
        top=pltpu.VMEM((heads // 2, 1, 2 * T), F32),
        tot=pltpu.VMEM((heads // 2, 1, 2 * T), F32),
        lse=pltpu.VMEM((heads // 2, 1, 2 * T), F32),
        delta=pltpu.VMEM((heads // 2, 1, 2 * T), F32),
        ot=pltpu.VMEM((DH, T), F32),
        dqt=pltpu.VMEM((DH, T), F32),
        dq=pltpu.VMEM((T, DH), BF16),
        vsum=pltpu.VMEM((1, DH), F32),
        obt=pltpu.VMEM((D, T), BF16),
        n1=pltpu.VMEM((F, D), F32),
        x1=pltpu.VMEM((F, D), F32),
        xb=pltpu.VMEM((T, D), BF16),
        xbt=pltpu.VMEM((D, T), BF16),
        df=pltpu.VMEM((T, D), BF16),
        act=pltpu.VMEM((T, FH), BF16),
        acto=pltpu.VMEM((C // 2, 2, CD // 2, T), BF16),
        att=pltpu.VMEM((2, C, CD // 2, T), BF16),
        xbm=pltpu.VMEM((T, D), BF16),
        xmt=pltpu.VMEM((D, T), BF16),
        dfm=pltpu.VMEM((T, DH), BF16),
        dum=pltpu.VMEM((T, FH // 2), BF16),
        slope=pltpu.VMEM((T, FH), F32),
        part=pltpu.VMEM((T, D), F32),
        part_in=pltpu.VMEM((F, D), F32),
        gd_sum=pltpu.VMEM((C, CD // 2, DH), BF16),
        gd_in=pltpu.VMEM((2, N, CD // 2, DH), BF16),
        gu_sum=pltpu.VMEM((C, CR, FH // 2), BF16),
        gu_in=pltpu.VMEM((2, N, CR, FH // 2), BF16),
        ap=pltpu.VMEM((C, 2, 4, CR // 2, DH), BF16),
        am=pltpu.VMEM((C, 4, CR // 2, DH), BF16),
        ga_in=pltpu.VMEM((2, N, 4, CR // 2, DH), BF16),
        ix_sum=pltpu.VMEM((C, F, D), BF16),
        ix_in=pltpu.VMEM((2, N, F, D), BF16),
        fd=pltpu.VMEM((CD // 2, DH), wire_d),
        fu=pltpu.VMEM((2, CR // 2, FH // 2), wire),
        fa=pltpu.VMEM((4, CR // 2, DH), wire),
        small=pltpu.VMEM((2, 16, D), F32),
        small_ring=pltpu.VMEM((C, 8, D), F32),
        fs=pltpu.VMEM((8, D), F32),
        load_sem=dma((6,)),
        g_send=dma((2, N, PIECES)),
        g_recv=dma((2, N, PIECES)),
        s_send=dma((C,)),
        s_recv=dma((C,)),
        m_send=dma((10,)),
        m_recv=dma((10,)),
        r_send=dma((4, 2, N)),
        r_recv=dma((4, 2, N)),
        y_send=dma((6,)),
        y_recv=dma((6,)),
        ya_send=dma((C,)),
        ya_recv=dma((C,)),
        c_send=dma((C,)),
        c_recv=dma((C,)),
        sr_send=dma((2, N)),
        sr_recv=dma((2, N)),
        f_send=dma((4, 2 * R - 1)),
        f_recv=dma((4, R, 2)),
    )
    if C <= 8:
        scratch.update(kt=pltpu.VMEM((DH, keys), BF16))
    names = [*operands, *results, *scratch]
    found = pl.pallas_call(
        functools.partial(layer_kernel, names, S, R),
        out_shape=[jax.ShapeDtypeStruct(shape, kind) for shape, kind in results.values()],
        in_specs=[spec for _, spec in operands.values()],
        out_specs=[vmem] * len(results),
        scratch_shapes=list(scratch.values()),
        compiler_params=pltpu.CompilerParams(
            collective_id=0, has_side_effects=True, vmem_limit_bytes=62 * 1024 * 1024
        ),
        name="layer",
    )(*[value for value, _ in operands.values()])
    shapes = [(F, D), (F, D), (D // S, D), (D // S,), (D // S, D), (D // S, D), (D // S,), (D // S, D)]
    shapes += [(D // S,)] * 3 + [(D // S, FF), (FF // S,), (FF // S, D)] + [(D // S,)] * 3
    kinds = [BF16] + [F32] * (len(shapes) - 1)
    final = pl.pallas_call(
        finish_kernel,
        out_shape=[jax.ShapeDtypeStruct(shape, kind) for shape, kind in zip(shapes, kinds, strict=True)],
        in_specs=[vmem] * len(found),
        out_specs=[vmem] * len(shapes),
        name="finish",
    )(*found)
    return (final[0][None], final[1][None], *final[2:])


def solution(mesh):
    shared = P("seq", None)
    part = P("seq")
    return jax.shard_map(
        on_device,
        mesh=mesh,
        in_specs=(P("row", "seq", None), P("row", "seq", None), P("row", None)) + (P(),) * 15,
        out_specs=(
            P("row", "seq", None),
            P("row", "seq", None),
            shared,
            part,
            shared,
            shared,
            part,
            shared,
            part,
            part,
            part,
            shared,
            part,
            shared,
            part,
            part,
            part,
        ),
        check_vma=False,
    )
```

```python
import functools
from types import SimpleNamespace as Refs

import jax
import jax.numpy as jnp
from jax import lax
from jax.experimental import pallas as pl
from jax.experimental.pallas import tpu as pltpu
from jax.sharding import PartitionSpec as P

H = 12
HEAD = 64
PIECES = 4
EPSILON = 1e-05
NEGATIVE = -1e30
MASKED = -2e30
MESH = pl.DeviceIdType.MESH
F32 = jnp.float32
BF16 = jnp.bfloat16


def nn(left, right):
    return lax.dot_general(left, right, (((1,), (0,)), ((), ())), preferred_element_type=F32)


def nt(left, right):
    return lax.dot_general(left, right, (((1,), (1,)), ((), ())), preferred_element_type=F32)


def norm_parts(summed):
    centre = summed - jnp.mean(summed, axis=-1, keepdims=True)
    variance = jnp.mean(centre * centre, axis=-1, keepdims=True)
    scale_inv = lax.rsqrt(variance + EPSILON)
    return (centre * scale_inv, scale_inv)


def norm_back(upstream, normal, scale_inv):
    return scale_inv * (
        upstream
        - jnp.mean(upstream, axis=-1, keepdims=True)
        - normal * jnp.mean(upstream * normal, axis=-1, keepdims=True)
    )


def gelu_parts(hidden):
    cumulative = 0.5 * (1.0 + lax.erf(hidden * 0.7071067811865476))
    density = jnp.exp(-0.5 * hidden * hidden) * 0.3989422804014327
    return hidden * cumulative, cumulative + hidden * density


Q_BIAS, V_BIAS, OUT_BIAS, GAIN1, SHIFT1, DOWN_BIAS, GAIN2, SHIFT2, UP_BIAS = range(9)


def layer_kernel(names, S, R, *refs):
    n = Refs(**dict(zip(names, refs, strict=True)))
    D = n.x.shape[1]
    F = n.x.shape[0]
    FF = n.wd_hbm.shape[0]
    T, DH, FH = 2 * F, D // 2, FF // 2
    C = S // 2
    N = C // 2
    CR = D // C
    CD = FF // C
    pairs = DH // (2 * HEAD)
    heads = DH // HEAD
    TILE = 256
    roomy = C <= 8
    tiles = FH // TILE

    place = lax.axis_index("seq")
    row = lax.axis_index("row")
    core = lax.rem(place, 2)
    chip = place // 2
    pos = jnp.where(lax.rem(chip, 2) == 0, chip // 2, C - 1 - chip // 2)

    def around(steps):
        return lax.rem(pos + (steps + C), C)

    def chip_at(where):
        return jnp.where(where < N, 2 * where, 2 * (C - 1 - where) + 1)

    sibling = (2 * chip + 1 - core, row)
    right = (2 * chip_at(around(1)) + core, row)
    left = (2 * chip_at(around(-1)) + core, row)
    ring = (right, left)
    parity = lax.rem(row, 2)
    mate_row = row + 1 - 2 * parity
    mate = (place, mate_row)
    others = []
    for dr in range(R):
        for dc in range(2):
            if dr or dc:
                others.append((lax.rem(row + dr, R), lax.rem(core + dc, 2)))

    def remote(src, dst, send, recv, device):
        return pltpu.make_async_remote_copy(
            src_ref=src, dst_ref=dst, send_sem=send, recv_sem=recv, device_id=device, device_id_type=MESH
        )

    started = []

    def start(copy):
        copy.start()
        started.append(copy)

    barrier = pltpu.get_barrier_semaphore()
    partners = [right, left] + [(2 * chip + c, r) for r, c in others]
    for device in partners:
        pl.semaphore_signal(barrier, inc=1, device_id=device, device_id_type=MESH)

    half_d = pl.multiple_of(core * DH, 128)
    half_f = pl.multiple_of(core * FH, 128)
    loads = []
    for source, target in (
        (n.wq_hbm.at[:, pl.ds(half_d, DH)], n.wq),
        (n.wk_hbm.at[:, pl.ds(half_d, DH)], n.wkv.at[:, pl.ds(0, DH)]),
        (n.wv_hbm.at[:, pl.ds(half_d, DH)], n.wkv.at[:, pl.ds(DH, DH)]),
        (n.wo_hbm, n.wo),
        (n.wu_hbm.at[:, pl.ds(half_f, FH)], n.wu),
        (n.wd_hbm.at[pl.ds(half_f, FH)], n.wd),
    ):
        loads.append(pltpu.make_async_copy(source, target, n.load_sem.at[len(loads)]))
        loads[-1].start()

    xa = n.xa
    own_rows = pl.multiple_of(core * F, F)
    other_rows = pl.multiple_of((1 - core) * F, F)
    xa[pos, pl.ds(own_rows, F)] = n.x[...]
    for index, vector in enumerate(
        (n.bias_q, n.bias_v, n.bias_o, n.gain1, n.shift1, n.bias_d, n.gain2, n.shift2)
    ):
        n.vec[index : index + 1] = vector[...].astype(F32).reshape(1, D)
    for index in range(FF // D):
        n.vec[UP_BIAS + index : UP_BIAS + index + 1] = (
            n.bias_u[D * index : D * (index + 1)].astype(F32).reshape(1, D)
        )
    pl.semaphore_wait(barrier, len(partners))

    step_rows = F // PIECES

    def hop_view(where, piece):
        return xa.at[where, pl.ds(pl.multiple_of(own_rows + piece * step_rows, step_rows), step_rows)]

    def hop_send(d, h, turn):
        view = hop_view(around((h - 1) * (2 * d - 1)), lax.rem(turn + d * (PIECES // 2), PIECES))
        return remote(view, view, n.g_send.at[d, turn], n.g_recv.at[d, h - 1, turn], ring[d])

    def hop_recv(d, h, turn):
        view = hop_view(around(h * (2 * d - 1)), lax.rem(turn + d * (PIECES // 2), PIECES))
        return remote(view, view, n.g_send.at[d, turn], n.g_recv.at[d, h - 1, turn], ring[d])

    def share_send(where, d=0):
        view = xa.at[where, pl.ds(own_rows, F)]
        return remote(view, view, n.s_send.at[d], n.s_recv.at[where], sibling)

    def share_recv(where):
        view = xa.at[where, pl.ds(other_rows, F)]
        return remote(view, view, n.s_send.at[0], n.s_recv.at[where], sibling)

    for turn in range(PIECES):
        hop_send(0, 1, turn).start()
        hop_send(1, 1, turn).start()
        if turn == 0:
            share_send(pos).start()

    def gather_step(h, turn):
        for d in range(2):
            hop_recv(d, h, turn).wait_recv()
            hop_send(d, h, turn).wait_send()

        @pl.when((h < N - 1) | (turn < PIECES // 2))
        def _():
            hop_send(0, h + 1, turn).start()
            hop_send(1, h + 1, turn).start()

        @pl.when(turn == PIECES - 1)
        def _():
            share_send(pos, 0).wait_send()
            pl.when(h > 1)(share_send(pos, 1).wait_send)
            share_send(around(-h), 0).start()
            share_send(around(h), 1).start()

    def gather_last():
        for turn in range(PIECES // 2):
            for d in range(2):
                hop_recv(d, N, turn).wait_recv()
                hop_send(d, N, turn).wait_send()
        share_send(pos, 0).wait_send()
        share_send(around(N), 0).start()

    def gather_sent():
        share_send(pos, 0).wait_send()
        share_send(pos, 1).wait_send()

    ends = []
    total = 0
    for i in range(n.lens.shape[1]):
        total = total + n.lens[0, i]
        ends.append(total)

    def ids(positions, padding):
        counted = jnp.zeros_like(positions)
        for end in ends:
            counted = counted + (positions >= end).astype(jnp.int32)
        return jnp.where(positions < ends[-1], counted, padding)

    query_ids = ids(lax.broadcasted_iota(jnp.int32, (1, T), 1) + chip * T, -1)

    def score_bias(where):
        key_ids = ids(lax.broadcasted_iota(jnp.int32, (T, 1), 0) + chip_at(where) * T, -2)
        found = jnp.where(key_ids == query_ids, 0.0, MASKED)
        return jnp.concatenate([found, found], axis=1)

    lane = lax.broadcasted_iota(jnp.int32, (T, 2 * HEAD), 1)

    def head_masked(values, target):
        for pair in range(pairs):
            both = values[:, 2 * HEAD * pair : 2 * HEAD * (pair + 1)]
            target[pair, :T] = jnp.where(lane < HEAD, both, 0.0).astype(BF16)
            target[pair, T:] = jnp.where(lane < HEAD, 0.0, both).astype(BF16)

    def of_pair(j):
        return slice(T * (j % 2), T * (j % 2 + 1))

    def of_head(j):
        return slice(HEAD * j, HEAD * (j + 1))

    def key_rows(where):
        return pl.ds(pl.multiple_of(where * T, T), T)

    def forward_block(where):
        xk = xa[where]
        both = nn(xk, n.wkv[...])
        keys = both[:, :DH].astype(BF16)
        scores = [nt(keys[:, 2 * HEAD * p : 2 * HEAD * (p + 1)], n.qm[p]) for p in range(pairs)]
        n.kva[key_rows(where), :DH] = keys
        if roomy:
            n.kt[:, key_rows(where)] = keys.T
        values = (both[:, DH:] + n.vec[V_BIAS : V_BIAS + 1, pl.ds(half_d, DH)]).astype(BF16)
        n.kva[key_rows(where), DH:] = values
        values_t = values.T
        n.xt[:, key_rows(where)] = xk.T
        bias = score_bias(where)
        weights, factors = [], []
        for p in range(pairs):
            st = scores[p] + bias
            top = n.top[p]
            new_top = jnp.maximum(top, jnp.max(st, axis=0, keepdims=True))
            found = jnp.exp(st - new_top)
            factors.append(jnp.exp(top - new_top))
            n.tot[p] = n.tot[p] * factors[p] + jnp.sum(found, axis=0, keepdims=True)
            n.top[p] = new_top
            weights.append(found.astype(BF16))
        for j in range(heads):
            n.ot[of_head(j)] = n.ot[of_head(j)] * factors[j // 2][:, of_pair(j)] + nn(
                values_t[of_head(j)], weights[j // 2][:, of_pair(j)]
            )

    n.top[...] = jnp.full(n.top.shape, NEGATIVE, F32)
    n.tot[...] = jnp.zeros(n.tot.shape, F32)
    n.ot[...] = jnp.zeros(n.ot.shape, F32)
    small = n.small.at[core]
    small[...] = jnp.zeros(small.shape, F32)

    for load in loads[:3]:
        load.wait()
    share_recv(pos).wait_recv()
    queries = (nn(xa[pos], n.wq[...]) + n.vec[Q_BIAS : Q_BIAS + 1, pl.ds(half_d, DH)]).astype(BF16)
    head_masked(queries.astype(F32) * 0.125, n.qm)

    def forward_step(step, carry):
        h, turn = 1 + step // PIECES, lax.rem(step, PIECES)
        gather_step(h, turn)

        @pl.when((step == 0) | ((h > 1) & (turn < 2)))
        def _():
            where = around((h - 1) * (2 * turn - 1))

            @pl.when(step > 0)
            def _():
                share_recv(where).wait_recv()

            forward_block(where)

        return carry

    lax.fori_loop(0, PIECES * (N - 1), forward_step, 0)

    def forward_last(step, carry):
        where = around((N - 1) * (2 * step - 1) - lax.div(step, 2) * (2 * N - 3))

        @pl.when(step == 1)
        def _():
            gather_last()

        share_recv(where).wait_recv()
        forward_block(where)
        return carry

    lax.fori_loop(0, 3, forward_last, 0)

    gather_sent()
    safe = jnp.where(n.tot[...] > 0.5, n.tot[...], 1.0)
    n.lse[...] = n.top[...] + jnp.log(safe)
    for j in range(heads):
        n.ot[of_head(j)] = n.ot[of_head(j)] / safe[j // 2][:, of_pair(j)]

    def swap(index, src, dst, landed):
        send, recv = n.m_send.at[index], n.m_recv.at[index]
        start(remote(src, dst, send, recv, sibling))
        return remote(src, landed, send, recv, sibling)

    def lend(index, src, dst, device, landed, recv_index=None):
        recv_index = index if recv_index is None else recv_index
        start(remote(src, dst, n.y_send.at[index], n.y_recv.at[recv_index], device))
        return remote(src, landed, n.y_send.at[index], n.y_recv.at[index], device)

    def deliver(src, dst, index):
        copy = pltpu.make_async_copy(src, dst, n.out_sem.at[index])
        copy.start()
        delivered.append(copy)

    delivered = []

    def sent(copy):
        started[:] = [other for other in started if other is not copy]
        copy.wait_send()

    obt = n.obt
    own_half = pl.ds(pl.multiple_of(core * DH, DH), DH)
    other_half = pl.ds(pl.multiple_of((1 - core) * DH, DH), DH)
    obt[own_half] = n.ot[...].astype(BF16)
    swapped = swap(0, obt.at[own_half], obt.at[own_half], obt.at[other_half])
    loads[3].wait()
    branch = nn(obt[own_half, pl.ds(own_rows, F)].T, n.wo[own_half])
    swapped.wait_recv()

    def vec(index):
        return n.vec[index : index + 1]

    branch = branch + nn(obt[other_half, pl.ds(own_rows, F)].T, n.wo[other_half]) + vec(OUT_BIAS)
    first_normal, first_scale = norm_parts(n.x[...].astype(F32) + branch)
    n.n1[...] = first_normal
    normed = first_normal * vec(GAIN1) + vec(SHIFT1)
    n.x1[...] = normed
    xb = n.xb
    xb[pl.ds(own_rows, F)] = normed.astype(BF16)
    swapped = swap(1, xb.at[pl.ds(own_rows, F)], xb.at[pl.ds(own_rows, F)], xb.at[pl.ds(other_rows, F)])
    xbm = n.xbm
    lent_xb = lend(0, xb.at[pl.ds(own_rows, F)], xbm.at[pl.ds(own_rows, F)], mate, xbm.at[pl.ds(own_rows, F)])
    loads[4].wait()

    act, slope = n.act, n.slope
    acto, att = n.acto, n.att
    du = act

    def up_rows(rows):
        for t in range(FH // D):
            cols = slice(D * t, D * (t + 1))
            bias = n.vec[pl.ds(UP_BIAS + core * (FH // D) + t, 1)]
            value, tangent = gelu_parts(nn(xb[rows], n.wu[:, cols]) + bias)
            low = value.astype(BF16)
            act[rows, cols] = low
            turned = low.T
            for c in range(D // CD):
                for half in range(2):
                    for side in range(2):
                        first = CD * c + CD // 2 * half + CD // 4 * side
                        acto[side, D // CD * t + c, half, :, rows] = turned[first : first + CD // 4]
            slope[rows, cols] = tangent

    up_rows(pl.ds(own_rows, F))
    swapped.wait_recv()
    up_rows(pl.ds(other_rows, F))
    own_ff = pl.ds(core * (C // 2), C // 2)
    other_ff = pl.ds((1 - core) * (C // 2), C // 2)
    lent_act = lend(1, acto.at[1, :, 1 - parity], att.at[1, own_ff], mate, att.at[1, own_ff])
    swapped_first = swap(10, acto.at[0], n.atf.at[own_ff], n.atf.at[other_ff])
    swapped_act = swap(2, acto.at[1, :, parity], att.at[0, own_ff], att.at[0, other_ff])
    n.atf[own_ff] = acto[0]
    att[0, own_ff] = acto[1, :, parity]
    loads[5].wait()
    part = n.part

    def part_swap(index):
        n.part_out[index] = part[pl.ds(other_rows, F)].astype(BF16)
        return swap(3 + 2 * index, n.part_out.at[index], n.part_in.at[index], n.part_in.at[index])

    part[...] = nn(act[...], n.wd[...])
    part_arrives = part_swap(0)
    n.xbt[...] = xb[...].T
    upstream = n.cot[...].astype(F32)
    small[SHIFT2 : SHIFT2 + 1] = jnp.sum(upstream, axis=0, keepdims=True)
    part_arrives.wait_recv()
    second_normal, second_scale = norm_parts(
        n.x1[...] + part[pl.ds(own_rows, F)] + n.part_in[0].astype(F32) + vec(DOWN_BIAS)
    )
    n.out_low[...] = (second_normal * vec(GAIN2) + vec(SHIFT2)).astype(BF16)
    deliver(n.out_low, n.out, 0)
    residual = norm_back(upstream * vec(GAIN2), second_normal, second_scale)
    n.dh2[...] = residual
    low = residual.astype(BF16)
    df = n.df
    df[pl.ds(own_rows, F)] = low
    swapped = swap(4, df.at[pl.ds(own_rows, F)], df.at[pl.ds(own_rows, F)], df.at[pl.ds(other_rows, F)])
    dfm = n.dfm
    lent_df = []
    for c in range(2):
        start(
            remote(
                df.at[pl.ds(own_rows, F), pl.ds(DH * c, DH)],
                dfm.at[pl.ds(own_rows, F)],
                n.y_send.at[2 + c],
                n.y_recv.at[2 + core],
                (2 * chip + c, mate_row),
            )
        )
        lent_df.append(
            remote(
                df.at[pl.ds(own_rows, F), pl.ds(DH * c, DH)],
                dfm.at[pl.ds(F * c, F)],
                n.y_send.at[2 + c],
                n.y_recv.at[2 + c],
                (2 * chip + c, mate_row),
            )
        )
    small[GAIN2 : GAIN2 + 1] = jnp.sum(upstream * second_normal, axis=0, keepdims=True)
    small[DOWN_BIAS : DOWN_BIAS + 1] = jnp.sum(low.astype(F32), axis=0, keepdims=True)
    swapped.wait_recv()

    class Flow:
        def __init__(self, index, chunk, landing, split, ready=None):
            self.index, self.chunk, self.landing, self.split, self.ready = index, chunk, landing, split, ready
            self.last = [None, None]

        def parts(self, d, distance):
            where = around(distance if d == 0 else -distance)
            src, dst = self.chunk(where), self.landing.at[d, distance - 1]
            if distance == N:
                src, dst = src.at[self.split[d]], dst.at[self.split[d]]
            send, recv = n.r_send.at[self.index, d], n.r_recv.at[self.index, d, distance - 1]
            return remote(src, dst, send, recv, ring[d]), dst

        def put(self, d, distance):
            if distance < N:
                self.last[d].wait_send()
            self.last[d] = self.parts(d, distance)[0]
            self.last[d].start()

        def sent(self):
            for copy in self.last:
                copy.wait_send()

        def begin(self):
            if self.ready is not None:
                self.ready(around(N))
            self.put(0, N)
            self.put(1, N)

        def step(self, distance):
            for d in range(2):
                where = around(distance if d == 0 else -distance)
                if self.ready is not None:
                    self.ready(where)
                arriving, landed = self.parts(d, distance + 1)
                arriving.wait_recv()
                target = self.chunk(where)
                if distance + 1 == N:
                    target = target.at[self.split[d]]
                target[...] = (target[...].astype(F32) + landed[...].astype(F32)).astype(BF16)
                self.put(d, distance)

        def end(self):
            if self.ready is not None:
                self.ready(pos)
            found = self.chunk(pos)[...].astype(F32)
            for d in range(2):
                arriving, landed = self.parts(d, 1)
                arriving.wait_recv()
                found = found + landed[...].astype(F32)
            return found

    def add_lent(where):
        c = chip_at(where)
        lent_chunk(c).wait_recv()
        n.ap[c, parity] = (n.ap[c, parity].astype(F32) + n.am[c].astype(F32)).astype(BF16)

    def lent_chunk(c):
        return remote(
            n.ap.at[c, 1 - parity, pl.ds(0, 3)], n.am.at[c, pl.ds(0, 3)], n.ya_send.at[0], n.ya_recv.at[c], mate
        )

    whole = slice(None)
    if CD % 128 == 0:
        split_d = [pl.ds(0, CD // 8), pl.ds(CD // 8, CD // 8)]
    else:
        split_d = [(whole, pl.ds(0, 128)), (whole, pl.ds(128, DH - 128))]
    flow_d = Flow(0, lambda where: n.gd_sum.at[chip_at(where)], n.gd_in, split_d)
    flow_e = Flow(4, lambda where: n.ge_sum.at[chip_at(where)], n.ge_in, [pl.ds(0, 1), pl.ds(1, 1)])
    flow_u = Flow(
        1,
        lambda where: n.gu_sum.at[chip_at(where)],
        n.gu_in,
        [(whole, pl.ds(0, FH // 4)), (whole, pl.ds(FH // 4, FH // 4))],
    )
    flow_a = Flow(
        2, lambda where: n.ap.at[chip_at(where), parity], n.ga_in, [pl.ds(0, 2), pl.ds(2, 2)], add_lent
    )
    flow_x = Flow(3, lambda where: n.ix_sum.at[where], n.ix_in, [pl.ds(0, F // 2), pl.ds(F // 2, F // 2)])

    def scatter(index, source, gathered, split):
        deliver(source.at[core] if split else source, gathered.at[row, core], 2 + index)
        for k, (r, c) in enumerate(others):
            view = source.at[c] if split else source
            start(
                remote(
                    view,
                    gathered.at[row, core],
                    n.f_send.at[index, k],
                    n.f_recv.at[index, row, core],
                    (2 * chip + c, r),
                )
            )

    def collect(index, source, gathered, split):
        for r, c in others:
            view = source.at[c] if split else source
            remote(
                view, gathered.at[r, c], n.f_send.at[index, 0], n.f_recv.at[index, r, c], (2 * chip + c, r)
            ).wait_recv()

    def spread(index, source, gathered):
        pl.when(core == parity)(spread_own(index, source, gathered).start)
        for k in range(R):
            copy = spread_copy(index, source, gathered, k)
            if k == 0:
                pl.when(core != parity)(copy.start)
            else:
                copy.start()

    def spread_own(index, source, gathered):
        return pltpu.make_async_copy(source, gathered.at[row // 2, core], n.out_sem.at[2 + index])

    def spread_copy(index, source, gathered, k):
        device = (2 * chip + parity, lax.rem(row + k, R))
        return remote(
            source, gathered.at[row // 2, core], n.f_send.at[index, k], n.f_recv.at[index, row // 2, core], device
        )

    def spread_done(index, source, gathered):
        for q in range(R // 2):
            for c in range(2):
                arriving = remote(
                    source, gathered.at[q, c], n.f_send.at[index, 0], n.f_recv.at[index, q, c], sibling
                )
                pl.when((2 * q + core != row) | (core != c))(arriving.wait_recv)
        pl.when(core == parity)(spread_own(index, source, gathered).wait)
        for k in range(R):
            copy = spread_copy(index, source, gathered, k)
            if k == 0:
                pl.when(core != parity)(copy.wait_send)
            else:
                copy.wait_send()

    def down_end():
        n.fd[...] = flow_d.end().astype(n.fd.dtype)
        spread(0, n.fd, n.yd)

    def first_end():
        n.fe[...] = flow_e.end().astype(n.fe.dtype)
        scatter(4, n.fe, n.ye, True)

    def up_end():
        found = flow_u.end()
        for c in range(2):
            n.fu[c] = found[CR // 2 * c : CR // 2 * (c + 1)].astype(n.fu.dtype)
        scatter(1, n.fu, n.yu, True)

    def input_step(distance):
        join(around(distance))
        join(around(-distance))
        flow_x.step(distance)

    def input_end():
        join(pos)
        n.dh2[...] = n.x1[...] + flow_x.end()
        deliver(n.dh2, n.grad_x, 1)

    def attention_begin():
        lent_out.wait_recv()
        flow_a.begin()

    def attention_end():
        n.fa[...] = flow_a.end().astype(n.fa.dtype)
        spread(2, n.fa, n.ya)

    def chain(step, end):
        return [functools.partial(step, distance) for distance in range(N - 1, 0, -1)] + [end]

    chain_d = chain(flow_d.step, down_end)
    chain_u = chain(flow_u.step, up_end)
    chain_e = chain(flow_e.step, first_end)
    chain_x = chain(input_step, input_end)
    chain_a = [attention_begin] + chain(flow_a.step, attention_end)

    def advance(one):
        one.pop(0)()

    swapped_first.wait_recv()
    for t in range(C // 2):
        two = slice(2 * t, 2 * t + 2)
        found = nn(n.atf[two].reshape(CD, T), df[:, pl.ds(half_d, DH)])
        n.ge_sum[two] = found.astype(BF16).reshape(2, 2, CD // 4, DH)
    flow_e.begin()
    for t in range(FH // D):
        cols = slice(D * t, D * (t + 1))
        low = (nt(df[...], n.wd[cols, :]) * slope[:, cols]).astype(BF16)
        du[:, cols] = low
        small[pl.ds(UP_BIAS + core * (FH // D) + t, 1)] = jnp.sum(low.astype(F32), axis=0, keepdims=True)

    quarter = pl.multiple_of(parity * (FH // 2), FH // 2)
    other_quarter = pl.multiple_of((1 - parity) * (FH // 2), FH // 2)
    lent_du = lend(4, du.at[:, pl.ds(other_quarter, FH // 2)], n.dum, mate, n.dum)
    part[...] = nt(du[...], n.wu[...])
    part_arrives = part_swap(1)

    part_arrives.wait_recv()
    grad_normed = n.dh2[...] + part[pl.ds(own_rows, F)] + n.part_in[1].astype(F32)
    normal = n.n1[...]
    small[GAIN1 : GAIN1 + 1] = jnp.sum(grad_normed * normal, axis=0, keepdims=True)
    small[SHIFT1 : SHIFT1 + 1] = jnp.sum(grad_normed, axis=0, keepdims=True)
    grad_branch = norm_back(grad_normed * vec(GAIN1), normal, first_scale)
    n.x1[...] = grad_branch
    low = grad_branch.astype(BF16)
    da = n.da
    da[pl.ds(own_rows, F)] = low
    swapped = swap(6, da.at[pl.ds(own_rows, F)], da.at[pl.ds(own_rows, F)], da.at[pl.ds(other_rows, F)])
    small[OUT_BIAS : OUT_BIAS + 1] = jnp.sum(low.astype(F32), axis=0, keepdims=True)
    advance(chain_e)
    swapped.wait_recv()

    grad_mixed = nt(da[...], n.wo[own_half]).astype(BF16).astype(F32)
    head_masked(grad_mixed, n.dm)
    grad_mixed_t = grad_mixed.T
    for j in range(heads):
        n.delta[j // 2, :, of_pair(j)] = jnp.sum(grad_mixed_t[of_head(j)] * n.ot[of_head(j)], axis=0, keepdims=True)

    def grad_down():
        swapped_act.wait_recv()
        swapped_actm.wait_recv()
        rows = CD // 2
        for lent in lent_df:
            lent.wait_recv()
        for t in range(C // 2):
            two = slice(2 * t, 2 * t + 2)
            found = nn(att[0, two].reshape(rows, T), df[:, pl.ds(half_d, DH)])
            found = found + nn(att[1, two].reshape(rows, T), dfm[...])
            n.gd_sum[two] = found.astype(BF16).reshape(2, CD // 4, DH)

    def forward_xb():
        lent_xb.wait_recv()
        return swap(8, xbm.at[pl.ds(own_rows, F)], xbm.at[pl.ds(own_rows, F)], xbm.at[pl.ds(other_rows, F)])

    def grad_up():
        swapped_xbm.wait_recv()
        n.xmt[...] = xbm[...].T
        lent_du.wait_recv()
        for t in range(FH // 2 // TILE):
            cols = slice(TILE * t, TILE * (t + 1))
            found = nn(n.xbt[...], du[:, pl.ds(pl.multiple_of(quarter + t * TILE, TILE), TILE)])
            found = (found + nn(n.xmt[...], n.dum[:, cols])).astype(BF16)
            for c in range(C):
                n.gu_sum[c, :, cols] = found[CR * c : CR * (c + 1)]

    def grad_attention(indices, left, right):
        for t in range(2):
            found = nn(left(pl.ds(DH * t, DH)), right)
            for k, index in enumerate(indices):
                for c in range(DH // CR):
                    for half in range(2):
                        first = CR * c + CR // 2 * half
                        n.ap[DH // CR * t + c, half, index] = found[
                            first : first + CR // 2, DH * k : DH * (k + 1)
                        ].astype(BF16)

    n.dqt[...] = jnp.zeros(n.dqt.shape, F32)
    n.vsum[...] = jnp.zeros(n.vsum.shape, F32)

    def backward_block(where):
        rows = key_rows(where)
        bias = score_bias(where)
        keys_t = n.kt[:, rows] if roomy else n.kva[rows, :DH].T

        def wide(p, first=0):
            return slice(first + 2 * HEAD * p, first + 2 * HEAD * (p + 1))

        def long(p):
            return slice(2 * T * p, 2 * T * (p + 1))

        for p in range(pairs):
            n.slope[:, long(p)] = nt(n.kva[rows, wide(p)], n.qm[p])
            n.grad_probs[:, long(p)] = nt(n.kva[rows, wide(p, DH)], n.dm[p])
        for p in range(pairs):
            probs = jnp.exp(n.slope[:, long(p)] + bias - n.lse[p])
            n.probs[:, long(p)] = probs.astype(BF16)
            n.grad_scores[:, long(p)] = (probs * (n.grad_probs[:, long(p)] - n.delta[p])).astype(BF16)
        for p in range(pairs):
            low = nn(n.probs[:, long(p)], n.dm[p]).astype(BF16)
            n.kva[rows, wide(p, DH)] = low
            n.kva[rows, wide(p)] = nn(n.grad_scores[:, long(p)], n.qm[p]).astype(BF16)
            n.vsum[:, wide(p)] += jnp.sum(low.astype(F32), axis=0, keepdims=True)
        for j in range(heads):
            n.dqt[of_head(j)] += nn(keys_t[of_head(j)], n.grad_scores[:, T * j : T * (j + 1)])
        return nt(n.kva[rows], n.wkv[...])

    crossing, turn_of_cross = [], [0]

    def put_cross(where):
        if len(crossing) == 2:
            crossing.pop(0).wait_send()
        crossing.append(cross(where))
        crossing[-1].start()

    def cross(where):
        send, recv = n.c_send.at[turn_of_cross[0] % 2], n.c_recv.at[where]
        return remote(xa.at[where, pl.ds(0, F)], xa.at[where, pl.ds(F, F)], send, recv, sibling)

    def key_block(where, extra=None):
        found = backward_block(where)
        if extra is not None:
            found = found + extra()
        part[...] = found
        xa[where, pl.ds(0, F)] = part[pl.ds(other_rows, F)].astype(BF16)
        n.ix_sum[where] = part[pl.ds(own_rows, F)].astype(BF16)

    def join(where):
        cross(where).wait_recv()
        n.ix_sum[where] = (
            n.ix_sum[where].astype(F32) + xa[where, pl.ds(F, F)].astype(F32)
        ).astype(BF16)

    def query_part():
        grad_query = (n.dqt[...] * 0.125).T.astype(BF16)
        n.dq[...] = grad_query
        return nt(grad_query, n.wq[...])

    blocks = [N] + [side * d for d in range(N - 1, 0, -1) for side in (1, -1)] + [0]
    if N == 4:
        due = [""] * 8
        due[0], due[1], due[3], due[4], due[5], due[6], due[7] = "mFD", "e", "x", "ed", "U", "x", "ed"
        last = "uasuasuasduasxdsax"
    else:
        due = ["mFD", "e"] + ["ed"[b % 4 // 2] if b % 2 == 0 else "x" for b in range(2, 2 * N)]
        due[4] += "U"
        last = "eaxdus" * (N + 2)
    chains = dict(e=chain_e, d=chain_d, u=chain_u, x=chain_x, a=chain_a, s=[])

    def begin_input():
        join(around(N))
        flow_x.begin()

    def begin_down():
        grad_down()
        flow_d.begin()

    def begin_up():
        nonlocal swapped_xbm, lent_out
        swapped_xbm = forward_xb()
        grad_attention([3], lambda rows: obt[rows], da[:, pl.ds(half_d, DH)])
        lent_out = lend(5, n.ap.at[:, 1 - parity, 3], n.am.at[:, 3], mate, n.am.at[:, 3])
        grad_up()
        flow_u.begin()

    def mate_hidden():
        nonlocal swapped_actm
        lent_act.wait_recv()
        swapped_actm = swap(9, att.at[1, own_ff], att.at[1, own_ff], att.at[1, other_ff])

    swapped_xbm = lent_out = swapped_actm = None
    begins = dict(m=mate_hidden, F=begin_input, D=begin_down, U=begin_up)

    def work(letters):
        for letter in letters:
            if letter in begins:
                begins[letter]()
            elif chains[letter]:
                chains[letter].pop(0)()

    for index, step in enumerate(blocks):
        key_block(around(step), query_part if step == 0 else None)
        turn_of_cross[0] = index
        put_cross(around(step))
        work(due[index])
    small[Q_BIAS : Q_BIAS + 1, pl.ds(half_d, DH)] = jnp.sum(n.dq[...].astype(F32), axis=0, keepdims=True)
    small[V_BIAS : V_BIAS + 1, pl.ds(half_d, DH)] = n.vsum[...]
    small_swap = swap(7, small, small, n.small.at[1 - core])

    grad_attention([0], lambda rows: n.xt[rows, key_rows(pos)], n.dq[...])
    grad_attention([1, 2], lambda rows: n.xt[rows], n.kva[...])
    for distance in range(N, -1, -1):
        for where in [around(distance)] + ([around(-distance)] if 0 < distance < N else []):
            lent_chunk(chip_at(where)).start()

    small_swap.wait_recv()
    around_small = n.small_ring
    mine = pl.ds(pl.multiple_of(core * 8, 8), 8)
    around_small[pos] = n.small[0, mine] + n.small[1, mine]

    def small_send(d, h):
        view = around_small.at[around(1 - h if d == 0 else h - 1)]
        return remote(view, view, n.sr_send.at[d], n.sr_recv.at[d, h - 1], ring[d])

    def small_recv(d, h):
        view = around_small.at[around(-h if d == 0 else h)]
        return remote(view, view, n.sr_send.at[d], n.sr_recv.at[d, h - 1], ring[d])

    small_last = [None, None]

    def small_put(d, h):
        if small_last[d] is not None:
            small_last[d].wait_send()
        small_last[d] = small_send(d, h)
        small_last[d].start()

    small_put(0, 1)
    small_put(1, 1)

    def small_step(h):
        small_recv(0, h).wait_recv()
        if h < N:
            small_recv(1, h).wait_recv()
            small_put(0, h + 1)
            if h + 1 < N:
                small_put(1, h + 1)

    def small_end():
        found = around_small[0]
        for where in range(1, C):
            found = found + around_small[where]
        n.fs[...] = found
        scatter(3, n.fs, n.ys, False)

    chain_s = [functools.partial(small_step, h) for h in range(1, N + 1)] + [small_end]
    chains.update(s=chain_s)
    work(last)
    assert not any(chains.values())
    spread_done(0, n.fd, n.yd)
    collect(1, n.fu, n.yu, True)
    collect(4, n.fe, n.ye, True)
    collect(3, n.fs, n.ys, False)
    spread_done(2, n.fa, n.ya)
    for copy in started:
        copy.wait_send()
    for copy in delivered:
        copy.wait()
    for flow in (flow_e, flow_d, flow_u, flow_x, flow_a):
        flow.sent()
    remote(
        n.ap.at[:, 1 - parity, pl.ds(0, 3)], n.am.at[:, pl.ds(0, 3)], n.ya_send.at[0], n.ya_recv.at[0], mate
    ).wait_send()
    for copy in crossing:
        copy.wait_send()
    for copy in small_last:
        if copy is not None:
            copy.wait_send()


def finish_kernel(out, grad_x, yd, ye, yu, ya, ys, *targets):
    (
        to_out,
        to_grad_x,
        to_query,
        to_query_bias,
        to_key,
        to_value,
        to_value_bias,
        to_o,
        to_out_bias,
        to_gain1,
        to_shift1,
        to_up,
        to_up_bias,
        to_down,
        to_down_bias,
        to_gain2,
        to_shift2,
    ) = targets
    R = yu.shape[0]
    D = out.shape[1]
    place = lax.axis_index("seq")

    def over_rows(gathered, *index, first=0, by=1):
        found = gathered[(first, *index)].astype(F32)
        for r in range(first + by, gathered.shape[0], by):
            found = found + gathered[(r, *index)].astype(F32)
        return found

    to_out[...] = out[...]
    to_grad_x[...] = grad_x[...]
    for c in range(2):
        width = yd.shape[-1]
        rows = yd.shape[2]
        to_down[:rows, width * c : width * (c + 1)] = over_rows(ye, c)
        to_down[rows:, width * c : width * (c + 1)] = over_rows(yd, c)
        for index, target in enumerate((to_query, to_key, to_value, to_o)):
            target[:, width * c : width * (c + 1)] = over_rows(ya, c, index)
        width = yu.shape[-1]
        for half in range(2):
            first = width * (2 * c + half)
            to_up[:, first : first + width] = over_rows(yu, c, first=half, by=2)
    sums = jnp.concatenate([over_rows(ys, 0), over_rows(ys, 1)])
    width = to_query_bias.shape[0]
    turned = pltpu.roll(sums, lax.rem(D - place * width, D), 1)
    for index, target in (
        (Q_BIAS, to_query_bias),
        (V_BIAS, to_value_bias),
        (OUT_BIAS, to_out_bias),
        (GAIN1, to_gain1),
        (SHIFT1, to_shift1),
        (DOWN_BIAS, to_down_bias),
        (GAIN2, to_gain2),
        (SHIFT2, to_shift2),
    ):
        target[...] = turned[index, :width]
    width = to_up_bias.shape[0]
    per = D // width
    turned = pltpu.roll(sums, lax.rem(D - lax.rem(place, per) * width, D), 1)
    line = lax.broadcasted_iota(jnp.int32, sums.shape, 0) == UP_BIAS + place // per
    to_up_bias[...] = jnp.sum(jnp.where(line, turned, 0.0), axis=0)[:width]


def on_device(
    inputs,
    cotangent,
    clip_lengths,
    query_weight,
    query_bias,
    key_weight,
    value_weight,
    value_bias,
    out_weight,
    out_bias,
    first_gain,
    first_shift,
    up_weight,
    up_bias,
    down_weight,
    down_bias,
    second_gain,
    second_shift,
):
    S, R = lax.axis_size("seq"), lax.axis_size("row")
    _, F, D = inputs.shape
    FF = up_weight.shape[1]
    C = S // 2
    N = C // 2
    T, DH, FH, CR, CD = 2 * F, D // 2, FF // 2, D // C, FF // C
    heads = DH // HEAD
    keys = C * T
    wire = BF16 if CR % 32 == 0 else F32
    wire_d = BF16 if CD % 64 == 0 else F32
    vmem = pl.BlockSpec(memory_space=pltpu.VMEM)
    hbm = pl.BlockSpec(memory_space=pl.ANY)
    operands = dict(
        x=(inputs[0], vmem),
        cot=(cotangent[0], vmem),
        lens=(clip_lengths, pl.BlockSpec(memory_space=pltpu.SMEM)),
        bias_q=(query_bias, vmem),
        bias_v=(value_bias, vmem),
        bias_o=(out_bias, vmem),
        gain1=(first_gain, vmem),
        shift1=(first_shift, vmem),
        bias_d=(down_bias, vmem),
        gain2=(second_gain, vmem),
        shift2=(second_shift, vmem),
        bias_u=(up_bias, vmem),
        wq_hbm=(query_weight, hbm),
        wk_hbm=(key_weight, hbm),
        wv_hbm=(value_weight, hbm),
        wo_hbm=(out_weight, hbm),
        wu_hbm=(up_weight, hbm),
        wd_hbm=(down_weight, hbm),
    )
    results = dict(
        out=((F, D), BF16),
        grad_x=((F, D), F32),
        yd=((R // 2, 2, CD // 4, DH), wire_d),
        ye=((R, 2, CD // 4, DH), wire_d),
        yu=((R, 2, CR // 2, FH // 2), wire),
        ya=((R // 2, 2, 4, CR // 2, DH), wire),
        ys=((R, 2, 8, D), F32),
    )
    dma = pltpu.SemaphoreType.DMA
    scratch = dict(
        wq=pltpu.VMEM((D, DH), BF16),
        wkv=pltpu.VMEM((D, D), BF16),
        wo=pltpu.VMEM((D, D), BF16),
        wu=pltpu.VMEM((D, FH), BF16),
        wd=pltpu.VMEM((FH, D), BF16),
        xa=pltpu.VMEM((C, T, D), BF16),
        xt=pltpu.VMEM((D, keys), BF16),
        kva=pltpu.VMEM((keys, D), BF16),
        qm=pltpu.VMEM((heads // 2, 2 * T, 2 * HEAD), BF16),
        dm=pltpu.VMEM((heads // 2, 2 * T, 2 * HEAD), BF16),
        grad_probs=pltpu.VMEM((T, heads * T), F32),
        probs=pltpu.VMEM((T, heads * T), BF16),
        grad_scores=pltpu.VMEM((T, heads * T), BF16),
        out_low=pltpu.VMEM((F, D), BF16),
        dh2=pltpu.VMEM((F, D), F32),
        vec=pltpu.VMEM((8 + FF // D, D), F32),
        top=pltpu.VMEM((heads // 2, 1, 2 * T), F32),
        tot=pltpu.VMEM((heads // 2, 1, 2 * T), F32),
        lse=pltpu.VMEM((heads // 2, 1, 2 * T), F32),
        delta=pltpu.VMEM((heads // 2, 1, 2 * T), F32),
        ot=pltpu.VMEM((DH, T), F32),
        dqt=pltpu.VMEM((DH, T), F32),
        dq=pltpu.VMEM((T, DH), BF16),
        vsum=pltpu.VMEM((1, DH), F32),
        obt=pltpu.VMEM((D, T), BF16),
        n1=pltpu.VMEM((F, D), F32),
        x1=pltpu.VMEM((F, D), F32),
        xb=pltpu.VMEM((T, D), BF16),
        xbt=pltpu.VMEM((D, T), BF16),
        df=pltpu.VMEM((T, D), BF16),
        da=pltpu.VMEM((T, D), BF16),
        act=pltpu.VMEM((T, FH), BF16),
        acto=pltpu.VMEM((2, C // 2, 2, CD // 4, T), BF16),
        atf=pltpu.VMEM((C, 2, CD // 4, T), BF16),
        att=pltpu.VMEM((2, C, CD // 4, T), BF16),
        xbm=pltpu.VMEM((T, D), BF16),
        xmt=pltpu.VMEM((D, T), BF16),
        dfm=pltpu.VMEM((T, DH), BF16),
        dum=pltpu.VMEM((T, FH // 2), BF16),
        slope=pltpu.VMEM((T, FH), F32),
        part=pltpu.VMEM((T, D), F32),
        part_in=pltpu.VMEM((2, F, D), BF16),
        part_out=pltpu.VMEM((2, F, D), BF16),
        gd_sum=pltpu.VMEM((C, CD // 4, DH), BF16),
        gd_in=pltpu.VMEM((2, N, CD // 4, DH), BF16),
        ge_sum=pltpu.VMEM((C, 2, CD // 4, DH), BF16),
        ge_in=pltpu.VMEM((2, N, 2, CD // 4, DH), BF16),
        gu_sum=pltpu.VMEM((C, CR, FH // 2), BF16),
        gu_in=pltpu.VMEM((2, N, CR, FH // 2), BF16),
        ap=pltpu.VMEM((C, 2, 4, CR // 2, DH), BF16),
        am=pltpu.VMEM((C, 4, CR // 2, DH), BF16),
        ga_in=pltpu.VMEM((2, N, 4, CR // 2, DH), BF16),
        ix_sum=pltpu.VMEM((C, F, D), BF16),
        ix_in=pltpu.VMEM((2, N, F, D), BF16),
        fd=pltpu.VMEM((CD // 4, DH), wire_d),
        fe=pltpu.VMEM((2, CD // 4, DH), wire_d),
        fu=pltpu.VMEM((2, CR // 2, FH // 2), wire),
        fa=pltpu.VMEM((4, CR // 2, DH), wire),
        small=pltpu.VMEM((2, 16, D), F32),
        small_ring=pltpu.VMEM((C, 8, D), F32),
        fs=pltpu.VMEM((8, D), F32),
        load_sem=dma((6,)),
        g_send=dma((2, PIECES)),
        g_recv=dma((2, N, PIECES)),
        s_send=dma((2,)),
        s_recv=dma((C,)),
        m_send=dma((11,)),
        m_recv=dma((11,)),
        r_send=dma((5, 2)),
        r_recv=dma((5, 2, N)),
        out_sem=dma((7,)),
        y_send=dma((6,)),
        y_recv=dma((6,)),
        ya_send=dma((1,)),
        ya_recv=dma((C,)),
        c_send=dma((2,)),
        c_recv=dma((C,)),
        sr_send=dma((2,)),
        sr_recv=dma((2, N)),
        f_send=dma((5, 2 * R - 1)),
        f_recv=dma((5, R, 2)),
    )
    if C <= 8:
        scratch.update(kt=pltpu.VMEM((DH, keys), BF16))
    names = [*operands, *results, *scratch]
    found = pl.pallas_call(
        functools.partial(layer_kernel, names, S, R),
        out_shape=[jax.ShapeDtypeStruct(shape, kind) for shape, kind in results.values()],
        in_specs=[spec for _, spec in operands.values()],
        out_specs=[hbm] * len(results),
        scratch_shapes=list(scratch.values()),
        compiler_params=pltpu.CompilerParams(
            collective_id=0, has_side_effects=True, vmem_limit_bytes=62 * 1024 * 1024
        ),
        name="layer",
    )(*[value for value, _ in operands.values()])
    shapes = [(F, D), (F, D), (D // S, D), (D // S,), (D // S, D), (D // S, D), (D // S,), (D // S, D)]
    shapes += [(D // S,)] * 3 + [(D // S, FF), (FF // S,), (FF // S, D)] + [(D // S,)] * 3
    kinds = [BF16] + [F32] * (len(shapes) - 1)
    final = pl.pallas_call(
        finish_kernel,
        out_shape=[jax.ShapeDtypeStruct(shape, kind) for shape, kind in zip(shapes, kinds, strict=True)],
        in_specs=[vmem] * len(found),
        out_specs=[vmem] * len(shapes),
        name="finish",
    )(*found)
    return (final[0][None], final[1][None], *final[2:])


def solution(mesh):
    shared = P("seq", None)
    part = P("seq")
    return jax.shard_map(
        on_device,
        mesh=mesh,
        in_specs=(P("row", "seq", None), P("row", "seq", None), P("row", None)) + (P(),) * 15,
        out_specs=(
            P("row", "seq", None),
            P("row", "seq", None),
            shared,
            part,
            shared,
            shared,
            part,
            shared,
            part,
            part,
            part,
            shared,
            part,
            shared,
            part,
            part,
            part,
        ),
        check_vma=False,
    )
```

```python
import functools
from types import SimpleNamespace as Refs

import jax
import jax.numpy as jnp
from jax import lax
from jax.experimental import pallas as pl
from jax.experimental.pallas import tpu as pltpu
from jax.sharding import PartitionSpec as P

H = 12
HEAD = 64
PIECES = 4
EPSILON = 1e-05
NEGATIVE = -1e30
MASKED = -2e30
MESH = pl.DeviceIdType.MESH
F32 = jnp.float32
BF16 = jnp.bfloat16


def nn(left, right):
    return lax.dot_general(left, right, (((1,), (0,)), ((), ())), preferred_element_type=F32)


def nt(left, right):
    return lax.dot_general(left, right, (((1,), (1,)), ((), ())), preferred_element_type=F32)


def norm_parts(summed):
    centre = summed - jnp.mean(summed, axis=-1, keepdims=True)
    variance = jnp.mean(centre * centre, axis=-1, keepdims=True)
    scale_inv = lax.rsqrt(variance + EPSILON)
    return (centre * scale_inv, scale_inv)


def norm_back(upstream, normal, scale_inv):
    return scale_inv * (
        upstream
        - jnp.mean(upstream, axis=-1, keepdims=True)
        - normal * jnp.mean(upstream * normal, axis=-1, keepdims=True)
    )


def gelu_parts(hidden):
    cumulative = 0.5 * (1.0 + lax.erf(hidden * 0.7071067811865476))
    density = jnp.exp(-0.5 * hidden * hidden) * 0.3989422804014327
    return hidden * cumulative, cumulative + hidden * density


Q_BIAS, V_BIAS, OUT_BIAS, GAIN1, SHIFT1, DOWN_BIAS, GAIN2, SHIFT2, UP_BIAS = range(9)


def layer_kernel(names, S, R, *refs):
    n = Refs(**dict(zip(names, refs, strict=True)))
    D = n.x.shape[1]
    F = n.x.shape[0]
    FF = n.wd_hbm.shape[0]
    T, DH, FH = 2 * F, D // 2, FF // 2
    C = S // 2
    N = C // 2
    CR = D // C
    CD = FF // C
    pairs = DH // (2 * HEAD)
    heads = DH // HEAD
    TILE = 256
    roomy = C <= 8
    tiles = FH // TILE

    place = lax.axis_index("seq")
    row = lax.axis_index("row")
    core = lax.rem(place, 2)
    chip = place // 2
    pos = jnp.where(lax.rem(chip, 2) == 0, chip // 2, C - 1 - chip // 2)

    def around(steps):
        return lax.rem(pos + (steps + C), C)

    def chip_at(where):
        return jnp.where(where < N, 2 * where, 2 * (C - 1 - where) + 1)

    sibling = (2 * chip + 1 - core, row)
    right = (2 * chip_at(around(1)) + core, row)
    left = (2 * chip_at(around(-1)) + core, row)
    ring = (right, left)
    parity = lax.rem(row, 2)
    mate_row = row + 1 - 2 * parity
    mate = (place, mate_row)
    others = []
    for dr in range(R):
        for dc in range(2):
            if dr or dc:
                others.append((lax.rem(row + dr, R), lax.rem(core + dc, 2)))

    def remote(src, dst, send, recv, device):
        return pltpu.make_async_remote_copy(
            src_ref=src, dst_ref=dst, send_sem=send, recv_sem=recv, device_id=device, device_id_type=MESH
        )

    started = []

    def start(copy):
        copy.start()
        started.append(copy)

    barrier = pltpu.get_barrier_semaphore()
    partners = [right, left] + [(2 * chip + c, r) for r, c in others]
    for device in partners:
        pl.semaphore_signal(barrier, inc=1, device_id=device, device_id_type=MESH)

    xa = n.xa
    own_rows = pl.multiple_of(core * F, F)
    other_rows = pl.multiple_of((1 - core) * F, F)
    half_d = pl.multiple_of(core * DH, 128)
    half_f = pl.multiple_of(core * FH, 128)
    loads = []
    for source, target in (
        (n.x, xa.at[pos, pl.ds(own_rows, F)]),
        (n.wq_hbm.at[:, pl.ds(half_d, DH)], n.wq),
        (n.wk_hbm.at[:, pl.ds(half_d, DH)], n.wkv.at[:, pl.ds(0, DH)]),
        (n.wv_hbm.at[:, pl.ds(half_d, DH)], n.wkv.at[:, pl.ds(DH, DH)]),
        (n.lens_hbm, n.lens),
        (n.bias_q, n.thin0),
        (n.bias_v, n.thin1),
        (n.bias_o, n.thin2),
        (n.gain1, n.thin3),
        (n.shift1, n.thin4),
        (n.bias_d, n.thin5),
        (n.gain2, n.thin6),
        (n.shift2, n.thin7),
        (n.bias_u, n.thin_u),
        (n.wo_hbm, n.wo),
        (n.wu_hbm.at[:, pl.ds(half_f, FH)], n.wu),
        (n.wd_hbm.at[pl.ds(half_f, FH)], n.wd),
        (n.cot_hbm, n.cot),
    ):
        loads.append(pltpu.make_async_copy(source, target, n.load_sem.at[len(loads)]))
        loads[-1].start()

    pl.semaphore_wait(barrier, len(partners))

    step_rows = F // PIECES

    def hop_view(where, piece):
        return xa.at[where, pl.ds(pl.multiple_of(own_rows + piece * step_rows, step_rows), step_rows)]

    def hop_send(d, h, turn):
        view = hop_view(around((h - 1) * (2 * d - 1)), lax.rem(turn + d * (PIECES // 2), PIECES))
        return remote(view, view, n.g_send.at[d, turn], n.g_recv.at[d, h - 1, turn], ring[d])

    def hop_first(d, turn):
        first = lax.rem(turn + d * (PIECES // 2), PIECES)
        src = n.x.at[pl.ds(first * step_rows, step_rows)]
        return remote(src, hop_view(pos, first), n.g_send.at[d, turn], n.g_recv.at[d, 0, turn], ring[d])

    def hop_recv(d, h, turn):
        view = hop_view(around(h * (2 * d - 1)), lax.rem(turn + d * (PIECES // 2), PIECES))
        return remote(view, view, n.g_send.at[d, turn], n.g_recv.at[d, h - 1, turn], ring[d])

    def share_send(where, d=0):
        view = xa.at[where, pl.ds(own_rows, F)]
        return remote(view, view, n.s_send.at[d], n.s_recv.at[where], sibling)

    def share_recv(where):
        view = xa.at[where, pl.ds(other_rows, F)]
        return remote(view, view, n.s_send.at[0], n.s_recv.at[where], sibling)

    for turn in range(PIECES):
        hop_first(0, turn).start()
        hop_first(1, turn).start()
        if turn == 0:
            remote(n.x, xa.at[pos, pl.ds(own_rows, F)], n.s_send.at[0], n.s_recv.at[pos], sibling).start()

    def gather_step(h, turn):
        for d in range(2):
            hop_recv(d, h, turn).wait_recv()
            hop_send(d, h, turn).wait_send()

        @pl.when((h < N - 1) | (turn < PIECES // 2))
        def _():
            hop_send(0, h + 1, turn).start()
            hop_send(1, h + 1, turn).start()

        @pl.when(turn == PIECES - 1)
        def _():
            share_send(pos, 0).wait_send()
            pl.when(h > 1)(share_send(pos, 1).wait_send)
            share_send(around(-h), 0).start()
            share_send(around(h), 1).start()

    def gather_last():
        for turn in range(PIECES // 2):
            for d in range(2):
                hop_recv(d, N, turn).wait_recv()
                hop_send(d, N, turn).wait_send()
        share_send(pos, 0).wait_send()
        share_send(around(N), 0).start()

    def gather_sent():
        share_send(pos, 0).wait_send()
        share_send(pos, 1).wait_send()

    for load in loads[:14]:
        load.wait()
    for index, thin in enumerate((n.thin0, n.thin1, n.thin2, n.thin3, n.thin4, n.thin5, n.thin6, n.thin7)):
        n.vec[index : index + 1] = thin[...].astype(F32).reshape(1, D)
    for index in range(FF // D):
        n.vec[UP_BIAS + index : UP_BIAS + index + 1] = (
            n.thin_u[D * index : D * (index + 1)].astype(F32).reshape(1, D)
        )

    ends = []
    total = 0
    for i in range(n.lens.shape[1]):
        total = total + n.lens[0, i]
        ends.append(total)

    def ids(positions, padding):
        counted = jnp.zeros_like(positions)
        for end in ends:
            counted = counted + (positions >= end).astype(jnp.int32)
        return jnp.where(positions < ends[-1], counted, padding)

    query_ids = ids(lax.broadcasted_iota(jnp.int32, (1, T), 1) + chip * T, -1)

    def score_bias(where):
        key_ids = ids(lax.broadcasted_iota(jnp.int32, (T, 1), 0) + chip_at(where) * T, -2)
        found = jnp.where(key_ids == query_ids, 0.0, MASKED)
        return jnp.concatenate([found, found], axis=1)

    lane = lax.broadcasted_iota(jnp.int32, (T, 2 * HEAD), 1)

    def head_masked(values, target):
        for pair in range(pairs):
            both = values[:, 2 * HEAD * pair : 2 * HEAD * (pair + 1)]
            target[pair, :T] = jnp.where(lane < HEAD, both, 0.0).astype(BF16)
            target[pair, T:] = jnp.where(lane < HEAD, 0.0, both).astype(BF16)

    def of_pair(j):
        return slice(T * (j % 2), T * (j % 2 + 1))

    def of_head(j):
        return slice(HEAD * j, HEAD * (j + 1))

    def key_rows(where):
        return pl.ds(pl.multiple_of(where * T, T), T)

    def forward_block(where):
        xk = xa[where]
        both = nn(xk, n.wkv[...])
        keys = both[:, :DH].astype(BF16)
        scores = [nt(keys[:, 2 * HEAD * p : 2 * HEAD * (p + 1)], n.qm[p]) for p in range(pairs)]
        n.kva[key_rows(where), :DH] = keys
        if roomy:
            n.kt[:, key_rows(where)] = keys.T
        values = (both[:, DH:] + n.vec[V_BIAS : V_BIAS + 1, pl.ds(half_d, DH)]).astype(BF16)
        n.kva[key_rows(where), DH:] = values
        values_t = values.T
        n.xt[:, key_rows(where)] = xk.T
        bias = score_bias(where)
        weights, factors = [], []
        for p in range(pairs):
            st = scores[p] + bias
            top = n.top[p]
            new_top = jnp.maximum(top, jnp.max(st, axis=0, keepdims=True))
            found = jnp.exp(st - new_top)
            factors.append(jnp.exp(top - new_top))
            n.tot[p] = n.tot[p] * factors[p] + jnp.sum(found, axis=0, keepdims=True)
            n.top[p] = new_top
            weights.append(found.astype(BF16))
        for j in range(heads):
            n.ot[of_head(j)] = n.ot[of_head(j)] * factors[j // 2][:, of_pair(j)] + nn(
                values_t[of_head(j)], weights[j // 2][:, of_pair(j)]
            )

    n.top[...] = jnp.full(n.top.shape, NEGATIVE, F32)
    n.tot[...] = jnp.zeros(n.tot.shape, F32)
    n.ot[...] = jnp.zeros(n.ot.shape, F32)
    small = n.small.at[core]
    small[...] = jnp.zeros(small.shape, F32)

    share_recv(pos).wait_recv()
    queries = (nn(xa[pos], n.wq[...]) + n.vec[Q_BIAS : Q_BIAS + 1, pl.ds(half_d, DH)]).astype(BF16)
    head_masked(queries.astype(F32) * 0.125, n.qm)

    def forward_step(step, carry):
        h, turn = 1 + step // PIECES, lax.rem(step, PIECES)
        gather_step(h, turn)

        @pl.when((step == 0) | ((h > 1) & (turn < 2)))
        def _():
            where = around((h - 1) * (2 * turn - 1))

            @pl.when(step > 0)
            def _():
                share_recv(where).wait_recv()

            forward_block(where)

        return carry

    lax.fori_loop(0, PIECES * (N - 1), forward_step, 0)

    def forward_last(step, carry):
        where = around((N - 1) * (2 * step - 1) - lax.div(step, 2) * (2 * N - 3))

        @pl.when(step == 1)
        def _():
            gather_last()

        share_recv(where).wait_recv()
        forward_block(where)
        return carry

    lax.fori_loop(0, 3, forward_last, 0)

    gather_sent()
    safe = jnp.where(n.tot[...] > 0.5, n.tot[...], 1.0)
    n.lse[...] = n.top[...] + jnp.log(safe)
    for j in range(heads):
        n.ot[of_head(j)] = n.ot[of_head(j)] / safe[j // 2][:, of_pair(j)]

    swaps = []

    def swap(index, src, dst, landed):
        if len(swaps) >= 3:
            sent(swaps[-3])
        send, recv = n.m_send.at[len(swaps) % 3], n.m_recv.at[index]
        start(remote(src, dst, send, recv, sibling))
        swaps.append(started[-1])
        return remote(src, landed, send, recv, sibling)

    def lend(index, src, dst, device, landed, recv_index=None):
        recv_index = index if recv_index is None else recv_index
        start(remote(src, dst, n.y_send.at[index], n.y_recv.at[recv_index], device))
        return remote(src, landed, n.y_send.at[index], n.y_recv.at[index], device)

    def deliver(src, dst, index):
        copy = pltpu.make_async_copy(src, dst, n.out_sem.at[index])
        copy.start()
        delivered.append(copy)

    delivered = []

    def sent(copy):
        started[:] = [other for other in started if other is not copy]
        copy.wait_send()

    obt = n.obt
    own_half = pl.ds(pl.multiple_of(core * DH, DH), DH)
    other_half = pl.ds(pl.multiple_of((1 - core) * DH, DH), DH)
    obt[own_half] = n.ot[...].astype(BF16)
    swapped = swap(0, obt.at[own_half], obt.at[own_half], obt.at[other_half])
    loads[14].wait()
    branch = nn(obt[own_half, pl.ds(own_rows, F)].T, n.wo[own_half])
    swapped.wait_recv()

    def vec(index):
        return n.vec[index : index + 1]

    branch = branch + nn(obt[other_half, pl.ds(own_rows, F)].T, n.wo[other_half]) + vec(OUT_BIAS)
    first_normal, first_scale = norm_parts(xa[pos, pl.ds(own_rows, F)].astype(F32) + branch)
    n.n1[...] = first_normal
    normed = first_normal * vec(GAIN1) + vec(SHIFT1)
    n.x1[...] = normed
    xb = n.xb
    xb[pl.ds(own_rows, F)] = normed.astype(BF16)
    swapped = swap(1, xb.at[pl.ds(own_rows, F)], xb.at[pl.ds(own_rows, F)], xb.at[pl.ds(other_rows, F)])
    xbm = n.xbm
    lent_xb = lend(0, xb.at[pl.ds(own_rows, F)], xbm.at[pl.ds(own_rows, F)], mate, xbm.at[pl.ds(own_rows, F)])
    loads[15].wait()

    act, slope = n.act, n.slope
    acto, att = n.acto, n.att
    du = act

    def up_rows(rows):
        for t in range(FH // D):
            cols = slice(D * t, D * (t + 1))
            bias = n.vec[pl.ds(UP_BIAS + core * (FH // D) + t, 1)]
            value, tangent = gelu_parts(nn(xb[rows], n.wu[:, cols]) + bias)
            low = value.astype(BF16)
            act[rows, cols] = low
            turned = low.T
            for c in range(D // CD):
                for half in range(2):
                    for side in range(2):
                        first = CD * c + CD // 2 * half + CD // 4 * side
                        acto[side, D // CD * t + c, half, :, rows] = turned[first : first + CD // 4]
            slope[rows, cols] = tangent

    up_rows(pl.ds(own_rows, F))
    swapped.wait_recv()
    up_rows(pl.ds(other_rows, F))
    own_ff = pl.ds(core * (C // 2), C // 2)
    other_ff = pl.ds((1 - core) * (C // 2), C // 2)
    lent_act = lend(1, acto.at[1, :, 1 - parity], att.at[1, own_ff], mate, att.at[1, own_ff])
    swapped_first = swap(10, acto.at[0], n.atf.at[own_ff], n.atf.at[other_ff])
    swapped_act = swap(2, acto.at[1, :, parity], att.at[0, own_ff], att.at[0, other_ff])
    n.atf[own_ff] = acto[0]
    att[0, own_ff] = acto[1, :, parity]
    loads[16].wait()
    loads[17].wait()
    part = n.part

    def part_swap(index):
        n.part_out[index] = part[pl.ds(other_rows, F)].astype(BF16)
        return swap(3 + 2 * index, n.part_out.at[index], n.part_in.at[index], n.part_in.at[index])

    part[...] = nn(act[...], n.wd[...])
    part_arrives = part_swap(0)
    n.xbt[...] = xb[...].T
    upstream = n.cot[...].astype(F32)
    small[SHIFT2 : SHIFT2 + 1] = jnp.sum(upstream, axis=0, keepdims=True)
    part_arrives.wait_recv()
    second_normal, second_scale = norm_parts(
        n.x1[...] + part[pl.ds(own_rows, F)] + n.part_in[0].astype(F32) + vec(DOWN_BIAS)
    )
    n.out_low[...] = (second_normal * vec(GAIN2) + vec(SHIFT2)).astype(BF16)
    deliver(n.out_low, n.out, 0)
    residual = norm_back(upstream * vec(GAIN2), second_normal, second_scale)
    n.dh2[...] = residual
    low = residual.astype(BF16)
    df = n.df
    df[pl.ds(own_rows, F)] = low
    swapped = swap(4, df.at[pl.ds(own_rows, F)], df.at[pl.ds(own_rows, F)], df.at[pl.ds(other_rows, F)])
    dfm = n.dfm
    lent_df = []
    for c in range(2):
        start(
            remote(
                df.at[pl.ds(own_rows, F), pl.ds(DH * c, DH)],
                dfm.at[pl.ds(own_rows, F)],
                n.y_send.at[2 + c],
                n.y_recv.at[2 + core],
                (2 * chip + c, mate_row),
            )
        )
        lent_df.append(
            remote(
                df.at[pl.ds(own_rows, F), pl.ds(DH * c, DH)],
                dfm.at[pl.ds(F * c, F)],
                n.y_send.at[2 + c],
                n.y_recv.at[2 + c],
                (2 * chip + c, mate_row),
            )
        )
    small[GAIN2 : GAIN2 + 1] = jnp.sum(upstream * second_normal, axis=0, keepdims=True)
    small[DOWN_BIAS : DOWN_BIAS + 1] = jnp.sum(low.astype(F32), axis=0, keepdims=True)
    swapped.wait_recv()

    class Flow:
        def __init__(self, index, chunk, landing, split, ready=None):
            self.index, self.chunk, self.landing, self.split, self.ready = index, chunk, landing, split, ready
            self.last = [None, None]

        def parts(self, d, distance):
            where = around(distance if d == 0 else -distance)
            src, dst = self.chunk(where), self.landing.at[d, distance - 1]
            if distance == N:
                src, dst = src.at[self.split[d]], dst.at[self.split[d]]
            send, recv = n.r_send.at[self.index, d], n.r_recv.at[self.index, d, distance - 1]
            return remote(src, dst, send, recv, ring[d]), dst

        def put(self, d, distance):
            if distance < N:
                self.last[d].wait_send()
            self.last[d] = self.parts(d, distance)[0]
            self.last[d].start()

        def sent(self):
            for copy in self.last:
                copy.wait_send()

        def begin(self):
            if self.ready is not None:
                self.ready(around(N))
            self.put(0, N)
            self.put(1, N)

        def step(self, distance):
            for d in range(2):
                where = around(distance if d == 0 else -distance)
                if self.ready is not None:
                    self.ready(where)
                arriving, landed = self.parts(d, distance + 1)
                arriving.wait_recv()
                target = self.chunk(where)
                if distance + 1 == N:
                    target = target.at[self.split[d]]
                target[...] = (target[...].astype(F32) + landed[...].astype(F32)).astype(BF16)
                self.put(d, distance)

        def end(self):
            if self.ready is not None:
                self.ready(pos)
            found = self.chunk(pos)[...].astype(F32)
            for d in range(2):
                arriving, landed = self.parts(d, 1)
                arriving.wait_recv()
                found = found + landed[...].astype(F32)
            return found

    def add_lent(first, lent, where):
        c = chip_at(where)
        lent(c).wait_recv()
        both = pl.ds(first, 2)
        n.ap[c, parity, both] = (n.ap[c, parity, both].astype(F32) + n.am[c, both].astype(F32)).astype(BF16)

    def lent_query(c):
        return remote(n.ap.at[c, 1 - parity, 0], n.am.at[c, 0], n.yq_send.at[0], n.yq_recv.at[c], mate)

    def lent_pair(c):
        both = pl.ds(2, 2)
        return remote(n.ap.at[c, 1 - parity, both], n.am.at[c, both], n.ya_send.at[0], n.ya_recv.at[c], mate)

    whole = slice(None)
    if CD % 128 == 0:
        split_d = [pl.ds(0, CD // 8), pl.ds(CD // 8, CD // 8)]
    else:
        split_d = [(whole, pl.ds(0, 128)), (whole, pl.ds(128, DH - 128))]
    flow_d = Flow(0, lambda where: n.gd_sum.at[chip_at(where)], n.gd_in, split_d)
    flow_e = Flow(4, lambda where: n.ge_sum.at[chip_at(where)], n.ge_in, [pl.ds(0, 1), pl.ds(1, 1)])
    flow_u = Flow(
        1,
        lambda where: n.gu_sum.at[chip_at(where)],
        n.gu_in,
        [(whole, pl.ds(0, FH // 4)), (whole, pl.ds(FH // 4, FH // 4))],
    )
    flow_a = Flow(
        2,
        lambda where: n.ap.at[chip_at(where), parity, pl.ds(2, 2)],
        n.ga_in,
        [pl.ds(0, 1), pl.ds(1, 1)],
        functools.partial(add_lent, 2, lent_pair),
    )
    flow_b = Flow(
        5,
        lambda where: n.ap.at[chip_at(where), parity, pl.ds(0, 2)],
        n.gb_in,
        [pl.ds(0, 1), pl.ds(1, 1)],
        functools.partial(add_lent, 0, lent_query),
    )
    flow_x = Flow(3, lambda where: n.ix_sum.at[where], n.ix_in, [pl.ds(0, F // 2), pl.ds(F // 2, F // 2)])

    scattered = []

    def scatter(index, source, gathered, split):
        while scattered:
            sent(scattered.pop())
        deliver(source.at[core] if split else source, gathered.at[row, core], 2 + index)
        for k, (r, c) in enumerate(others):
            view = source.at[c] if split else source
            start(
                remote(
                    view, gathered.at[row, core], n.f_send.at[k], n.f_recv.at[index, row, core], (2 * chip + c, r)
                )
            )
            scattered.append(started[-1])

    def collect(index, source, gathered, split):
        for r, c in others:
            view = source.at[c] if split else source
            remote(
                view, gathered.at[r, c], n.f_send.at[0], n.f_recv.at[index, r, c], (2 * chip + c, r)
            ).wait_recv()

    def spread(index, source, gathered):
        pl.when(core == parity)(spread_own(index, source, gathered).start)
        for k in range(R):
            copy = spread_copy(index, source, gathered, k)
            if k == 0:
                pl.when(core != parity)(copy.start)
            else:
                copy.start()

    def spread_own(index, source, gathered):
        return pltpu.make_async_copy(source, gathered.at[row // 2, core], n.out_sem.at[2 + index])

    def spread_copy(index, source, gathered, k):
        device = (2 * chip + parity, lax.rem(row + k, R))
        return remote(
            source, gathered.at[row // 2, core], n.h_send.at[index, k], n.f_recv.at[index, row // 2, core], device
        )

    def spread_done(index, source, gathered):
        for q in range(R // 2):
            for c in range(2):
                arriving = remote(
                    source, gathered.at[q, c], n.h_send.at[index, 0], n.f_recv.at[index, q, c], sibling
                )
                pl.when((2 * q + core != row) | (core != c))(arriving.wait_recv)
        pl.when(core == parity)(spread_own(index, source, gathered).wait)
        for k in range(R):
            copy = spread_copy(index, source, gathered, k)
            if k == 0:
                pl.when(core != parity)(copy.wait_send)
            else:
                copy.wait_send()

    def down_end():
        n.fd[...] = flow_d.end().astype(n.fd.dtype)
        spread(0, n.fd, n.yd)

    def first_end():
        n.fe[...] = flow_e.end().astype(n.fe.dtype)
        scatter(4, n.fe, n.ye, True)

    def up_end():
        found = flow_u.end()
        for c in range(2):
            n.fu[c] = found[CR // 2 * c : CR // 2 * (c + 1)].astype(n.fu.dtype)
        scatter(5, n.fu, n.yu, True)

    def input_step(distance):
        join(around(distance))
        join(around(-distance))
        flow_x.step(distance)

    def input_end():
        join(pos)
        n.dh2[...] = n.x1[...] + flow_x.end()
        deliver(n.dh2, n.grad_x, 1)

    def query_begin():
        lent_out.wait_recv()
        flow_b.begin()

    def attention_end(flow, index, source, gathered):
        source[...] = flow.end().astype(source.dtype)
        spread(index, source, gathered)

    def chain(step, end):
        return [functools.partial(step, distance) for distance in range(N - 1, 0, -1)] + [end]

    chain_d = chain(flow_d.step, down_end)
    chain_u = chain(flow_u.step, up_end)
    chain_e = chain(flow_e.step, first_end)
    chain_x = chain(input_step, input_end)
    chain_a = [flow_a.begin] + chain(flow_a.step, functools.partial(attention_end, flow_a, 2, n.fa, n.ya))
    chain_b = [query_begin] + chain(flow_b.step, functools.partial(attention_end, flow_b, 1, n.fb, n.yb))

    def advance(one):
        one.pop(0)()

    swapped_first.wait_recv()
    for t in range(C // 2):
        two = slice(2 * t, 2 * t + 2)
        found = nn(n.atf[two].reshape(CD, T), df[:, pl.ds(half_d, DH)])
        n.ge_sum[two] = found.astype(BF16).reshape(2, 2, CD // 4, DH)
    flow_e.begin()
    for t in range(FH // D):
        cols = slice(D * t, D * (t + 1))
        low = (nt(df[...], n.wd[cols, :]) * slope[:, cols]).astype(BF16)
        du[:, cols] = low
        small[pl.ds(UP_BIAS + core * (FH // D) + t, 1)] = jnp.sum(low.astype(F32), axis=0, keepdims=True)

    quarter = pl.multiple_of(parity * (FH // 2), FH // 2)
    other_quarter = pl.multiple_of((1 - parity) * (FH // 2), FH // 2)
    lent_du = lend(4, du.at[:, pl.ds(other_quarter, FH // 2)], n.dum, mate, n.dum)
    part[...] = nt(du[...], n.wu[...])
    part_arrives = part_swap(1)

    part_arrives.wait_recv()
    grad_normed = n.dh2[...] + part[pl.ds(own_rows, F)] + n.part_in[1].astype(F32)
    normal = n.n1[...]
    small[GAIN1 : GAIN1 + 1] = jnp.sum(grad_normed * normal, axis=0, keepdims=True)
    small[SHIFT1 : SHIFT1 + 1] = jnp.sum(grad_normed, axis=0, keepdims=True)
    grad_branch = norm_back(grad_normed * vec(GAIN1), normal, first_scale)
    n.x1[...] = grad_branch
    low = grad_branch.astype(BF16)
    da = n.da
    da[pl.ds(own_rows, F)] = low
    swapped = swap(6, da.at[pl.ds(own_rows, F)], da.at[pl.ds(own_rows, F)], da.at[pl.ds(other_rows, F)])
    small[OUT_BIAS : OUT_BIAS + 1] = jnp.sum(low.astype(F32), axis=0, keepdims=True)
    advance(chain_e)
    swapped.wait_recv()

    grad_mixed = nt(da[...], n.wo[own_half]).astype(BF16).astype(F32)
    head_masked(grad_mixed, n.dm)
    grad_mixed_t = grad_mixed.T
    for j in range(heads):
        n.delta[j // 2, :, of_pair(j)] = jnp.sum(grad_mixed_t[of_head(j)] * n.ot[of_head(j)], axis=0, keepdims=True)

    def grad_down():
        swapped_act.wait_recv()
        swapped_actm.wait_recv()
        rows = CD // 2
        for lent in lent_df:
            lent.wait_recv()
        for t in range(C // 2):
            two = slice(2 * t, 2 * t + 2)
            found = nn(att[0, two].reshape(rows, T), df[:, pl.ds(half_d, DH)])
            found = found + nn(att[1, two].reshape(rows, T), dfm[...])
            n.gd_sum[two] = found.astype(BF16).reshape(2, CD // 4, DH)

    def forward_xb():
        lent_xb.wait_recv()
        return swap(8, xbm.at[pl.ds(own_rows, F)], xbm.at[pl.ds(own_rows, F)], xbm.at[pl.ds(other_rows, F)])

    def grad_up():
        swapped_xbm.wait_recv()
        n.xmt[...] = xbm[...].T
        lent_du.wait_recv()
        for t in range(FH // 2 // TILE):
            cols = slice(TILE * t, TILE * (t + 1))
            found = nn(n.xbt[...], du[:, pl.ds(pl.multiple_of(quarter + t * TILE, TILE), TILE)])
            found = (found + nn(n.xmt[...], n.dum[:, cols])).astype(BF16)
            for c in range(C):
                n.gu_sum[c, :, cols] = found[CR * c : CR * (c + 1)]

    def grad_attention(indices, left, right):
        for t in range(2):
            found = nn(left(pl.ds(DH * t, DH)), right)
            for k, index in enumerate(indices):
                for c in range(DH // CR):
                    for half in range(2):
                        first = CR * c + CR // 2 * half
                        n.ap[DH // CR * t + c, half, index] = found[
                            first : first + CR // 2, DH * k : DH * (k + 1)
                        ].astype(BF16)

    n.dqt[...] = jnp.zeros(n.dqt.shape, F32)
    n.vsum[...] = jnp.zeros(n.vsum.shape, F32)

    def backward_block(where):
        rows = key_rows(where)
        bias = score_bias(where)
        keys_t = n.kt[:, rows] if roomy else n.kva[rows, :DH].T

        def wide(p, first=0):
            return slice(first + 2 * HEAD * p, first + 2 * HEAD * (p + 1))

        def long(p):
            return slice(2 * T * p, 2 * T * (p + 1))

        for p in range(pairs):
            n.slope[:, long(p)] = nt(n.kva[rows, wide(p)], n.qm[p])
            n.grad_probs[:, long(p)] = nt(n.kva[rows, wide(p, DH)], n.dm[p])
        for p in range(pairs):
            probs = jnp.exp(n.slope[:, long(p)] + bias - n.lse[p])
            n.probs[:, long(p)] = probs.astype(BF16)
            n.grad_scores[:, long(p)] = (probs * (n.grad_probs[:, long(p)] - n.delta[p])).astype(BF16)
        for p in range(pairs):
            low = nn(n.probs[:, long(p)], n.dm[p]).astype(BF16)
            n.kva[rows, wide(p, DH)] = low
            n.kva[rows, wide(p)] = nn(n.grad_scores[:, long(p)], n.qm[p]).astype(BF16)
            n.vsum[:, wide(p)] += jnp.sum(low.astype(F32), axis=0, keepdims=True)
        for j in range(heads):
            n.dqt[of_head(j)] += nn(keys_t[of_head(j)], n.grad_scores[:, T * j : T * (j + 1)])
        return nt(n.kva[rows], n.wkv[...])

    crossing, turn_of_cross = [], [0]

    def put_cross(where):
        if len(crossing) == 2:
            crossing.pop(0).wait_send()
        crossing.append(cross(where))
        crossing[-1].start()

    def cross(where):
        send, recv = n.c_send.at[turn_of_cross[0] % 2], n.c_recv.at[where]
        return remote(xa.at[where, pl.ds(0, F)], xa.at[where, pl.ds(F, F)], send, recv, sibling)

    def key_block(where, extra=None):
        found = backward_block(where)
        if extra is not None:
            found = found + extra()
        part[...] = found
        xa[where, pl.ds(0, F)] = part[pl.ds(other_rows, F)].astype(BF16)
        n.ix_sum[where] = part[pl.ds(own_rows, F)].astype(BF16)

    def join(where):
        cross(where).wait_recv()
        n.ix_sum[where] = (
            n.ix_sum[where].astype(F32) + xa[where, pl.ds(F, F)].astype(F32)
        ).astype(BF16)

    def query_part():
        grad_query = (n.dqt[...] * 0.125).T.astype(BF16)
        n.dq[...] = grad_query
        return nt(grad_query, n.wq[...])

    around_small = n.small_ring
    mine = pl.ds(pl.multiple_of(core * 8, 8), 8)

    def small_send(d, h):
        view = around_small.at[around(1 - h if d == 0 else h - 1)]
        return remote(view, view, n.sr_send.at[d], n.sr_recv.at[d, h - 1], ring[d])

    def small_recv(d, h):
        view = around_small.at[around(-h if d == 0 else h)]
        return remote(view, view, n.sr_send.at[d], n.sr_recv.at[d, h - 1], ring[d])

    small_last = [None, None]

    def small_put(d, h):
        if small_last[d] is not None:
            small_last[d].wait_send()
        small_last[d] = small_send(d, h)
        small_last[d].start()


    def small_step(h):
        small_recv(0, h).wait_recv()
        if h < N:
            small_recv(1, h).wait_recv()
            small_put(0, h + 1)
            if h + 1 < N:
                small_put(1, h + 1)

    def small_end():
        found = around_small[0]
        for where in range(1, C):
            found = found + around_small[where]
        n.fs[...] = found
        scatter(3, n.fs, n.ys, False)

    chain_s = [functools.partial(small_step, h) for h in range(1, N + 1)] + [small_end]
    blocks = [N] + [side * d for d in range(N - 1, 0, -1) for side in (1, -1)] + [0]
    if N == 4:
        due = [""] * 8
        due[0], due[1], due[3], due[4], due[5], due[7] = "mF", "De", "dOx", "U", "e", "uSx"
        last = "basubasduaebsduabsxdsabx"
    else:
        due = ["mFD", "e"] + ["ed"[b % 4 // 2] if b % 2 == 0 else "x" for b in range(2, 2 * N)]
        due[4] += "OU"
        due[2 * N - 1] += "S"
        last = "ebaxdus" * (N + 2)
    chains = dict(e=chain_e, d=chain_d, u=chain_u, x=chain_x, a=chain_a, b=chain_b, s=chain_s)

    def begin_input():
        join(around(N))
        flow_x.begin()

    def begin_down():
        grad_down()
        flow_d.begin()

    def begin_up():
        nonlocal swapped_xbm
        swapped_xbm = forward_xb()
        grad_up()
        flow_u.begin()

    def begin_out():
        nonlocal lent_out
        grad_attention([1], lambda rows: obt[rows], da[:, pl.ds(half_d, DH)])
        lent_out = lend(5, n.ap.at[:, 1 - parity, 1], n.am.at[:, 1], mate, n.am.at[:, 1])

    def begin_small():
        small_swap.wait_recv()
        around_small[pos] = n.small[0, mine] + n.small[1, mine]
        small_put(0, 1)
        small_put(1, 1)

    def mate_hidden():
        nonlocal swapped_actm
        lent_act.wait_recv()
        swapped_actm = swap(9, att.at[1, own_ff], att.at[1, own_ff], att.at[1, other_ff])

    swapped_xbm = lent_out = swapped_actm = small_swap = None
    begins = dict(m=mate_hidden, F=begin_input, D=begin_down, U=begin_up, O=begin_out, S=begin_small)

    def work(letters):
        for letter in letters:
            if letter in begins:
                begins[letter]()
            elif chains[letter]:
                chains[letter].pop(0)()

    for index, step in enumerate(blocks):
        key_block(around(step), query_part if step == 0 else None)
        turn_of_cross[0] = index
        put_cross(around(step))
        if step == 0:
            small[Q_BIAS : Q_BIAS + 1, pl.ds(half_d, DH)] = jnp.sum(n.dq[...].astype(F32), axis=0, keepdims=True)
            small[V_BIAS : V_BIAS + 1, pl.ds(half_d, DH)] = n.vsum[...]
            small_swap = swap(7, small, small, n.small.at[1 - core])
        work(due[index])
    grad_attention([0], lambda rows: n.xt[rows, key_rows(pos)], n.dq[...])
    ordered = [around(d) for d in [N] + [side * d for d in range(N - 1, 0, -1) for side in (1, -1)] + [0]]
    for where in ordered[:3]:
        lent_query(chip_at(where)).start()
    grad_attention([2, 3], lambda rows: n.xt[rows], n.kva[...])
    for k, where in enumerate(ordered):
        if k >= 3:
            lent_query(chip_at(where)).start()
        lent_pair(chip_at(where)).start()

    work(last)
    assert not any(chains.values())
    spread_done(0, n.fd, n.yd)
    collect(5, n.fu, n.yu, True)
    collect(4, n.fe, n.ye, True)
    collect(3, n.fs, n.ys, False)
    spread_done(2, n.fa, n.ya)
    spread_done(1, n.fb, n.yb)
    for copy in started:
        copy.wait_send()
    for copy in delivered:
        copy.wait()
    for flow in (flow_e, flow_d, flow_u, flow_x, flow_a, flow_b):
        flow.sent()
    remote(n.ap.at[:, 1 - parity, 0], n.am.at[:, 0], n.yq_send.at[0], n.yq_recv.at[0], mate).wait_send()
    both = pl.ds(2, 2)
    remote(n.ap.at[:, 1 - parity, both], n.am.at[:, both], n.ya_send.at[0], n.ya_recv.at[0], mate).wait_send()
    for copy in crossing:
        copy.wait_send()
    for copy in small_last:
        if copy is not None:
            copy.wait_send()


def finish_kernel(out, grad_x, yd, ye, yu, ya, yb, ys, *targets):
    (
        to_out,
        to_grad_x,
        to_query,
        to_query_bias,
        to_key,
        to_value,
        to_value_bias,
        to_o,
        to_out_bias,
        to_gain1,
        to_shift1,
        to_up,
        to_up_bias,
        to_down,
        to_down_bias,
        to_gain2,
        to_shift2,
    ) = targets
    R = yu.shape[0]
    D = out.shape[1]
    place = lax.axis_index("seq")

    def over_rows(gathered, *index, first=0, by=1):
        found = gathered[(first, *index)].astype(F32)
        for r in range(first + by, gathered.shape[0], by):
            found = found + gathered[(r, *index)].astype(F32)
        return found

    to_out[...] = out[...]
    to_grad_x[...] = grad_x[...]
    for c in range(2):
        width = yd.shape[-1]
        rows = yd.shape[2]
        to_down[:rows, width * c : width * (c + 1)] = over_rows(ye, c)
        to_down[rows:, width * c : width * (c + 1)] = over_rows(yd, c)
        for gathered, index, target in ((yb, 0, to_query), (yb, 1, to_o), (ya, 0, to_key), (ya, 1, to_value)):
            target[:, width * c : width * (c + 1)] = over_rows(gathered, c, index)
        width = yu.shape[-1]
        for half in range(2):
            first = width * (2 * c + half)
            to_up[:, first : first + width] = over_rows(yu, c, first=half, by=2)
    sums = jnp.concatenate([over_rows(ys, 0), over_rows(ys, 1)])
    width = to_query_bias.shape[0]
    turned = pltpu.roll(sums, lax.rem(D - place * width, D), 1)
    for index, target in (
        (Q_BIAS, to_query_bias),
        (V_BIAS, to_value_bias),
        (OUT_BIAS, to_out_bias),
        (GAIN1, to_gain1),
        (SHIFT1, to_shift1),
        (DOWN_BIAS, to_down_bias),
        (GAIN2, to_gain2),
        (SHIFT2, to_shift2),
    ):
        target[...] = turned[index, :width]
    width = to_up_bias.shape[0]
    per = D // width
    turned = pltpu.roll(sums, lax.rem(D - lax.rem(place, per) * width, D), 1)
    line = lax.broadcasted_iota(jnp.int32, sums.shape, 0) == UP_BIAS + place // per
    to_up_bias[...] = jnp.sum(jnp.where(line, turned, 0.0), axis=0)[:width]


def on_device(
    inputs,
    cotangent,
    clip_lengths,
    query_weight,
    query_bias,
    key_weight,
    value_weight,
    value_bias,
    out_weight,
    out_bias,
    first_gain,
    first_shift,
    up_weight,
    up_bias,
    down_weight,
    down_bias,
    second_gain,
    second_shift,
):
    S, R = lax.axis_size("seq"), lax.axis_size("row")
    _, F, D = inputs.shape
    FF = up_weight.shape[1]
    C = S // 2
    N = C // 2
    T, DH, FH, CR, CD = 2 * F, D // 2, FF // 2, D // C, FF // C
    heads = DH // HEAD
    keys = C * T
    wire = BF16 if CR % 32 == 0 else F32
    wire_d = BF16 if CD % 64 == 0 else F32
    vmem = pl.BlockSpec(memory_space=pltpu.VMEM)
    hbm = pl.BlockSpec(memory_space=pl.ANY)
    operands = dict(
        x=(inputs[0], hbm),
        cot_hbm=(cotangent[0], hbm),
        lens_hbm=(clip_lengths, hbm),
        bias_q=(query_bias, hbm),
        bias_v=(value_bias, hbm),
        bias_o=(out_bias, hbm),
        gain1=(first_gain, hbm),
        shift1=(first_shift, hbm),
        bias_d=(down_bias, hbm),
        gain2=(second_gain, hbm),
        shift2=(second_shift, hbm),
        bias_u=(up_bias, hbm),
        wq_hbm=(query_weight, hbm),
        wk_hbm=(key_weight, hbm),
        wv_hbm=(value_weight, hbm),
        wo_hbm=(out_weight, hbm),
        wu_hbm=(up_weight, hbm),
        wd_hbm=(down_weight, hbm),
    )
    results = dict(
        out=((F, D), BF16),
        grad_x=((F, D), F32),
        yd=((R // 2, 2, CD // 4, DH), wire_d),
        ye=((R, 2, CD // 4, DH), wire_d),
        yu=((R, 2, CR // 2, FH // 2), wire),
        ya=((R // 2, 2, 2, CR // 2, DH), wire),
        yb=((R // 2, 2, 2, CR // 2, DH), wire),
        ys=((R, 2, 8, D), F32),
    )
    dma = pltpu.SemaphoreType.DMA
    scratch = dict(
        wq=pltpu.VMEM((D, DH), BF16),
        wkv=pltpu.VMEM((D, D), BF16),
        wo=pltpu.VMEM((D, D), BF16),
        wu=pltpu.VMEM((D, FH), BF16),
        wd=pltpu.VMEM((FH, D), BF16),
        xa=pltpu.VMEM((C, T, D), BF16),
        xt=pltpu.VMEM((D, keys), BF16),
        kva=pltpu.VMEM((keys, D), BF16),
        qm=pltpu.VMEM((heads // 2, 2 * T, 2 * HEAD), BF16),
        dm=pltpu.VMEM((heads // 2, 2 * T, 2 * HEAD), BF16),
        grad_probs=pltpu.VMEM((T, heads * T), F32),
        probs=pltpu.VMEM((T, heads * T), BF16),
        grad_scores=pltpu.VMEM((T, heads * T), BF16),
        cot=pltpu.VMEM((F, D), BF16),
        lens=pltpu.SMEM(clip_lengths.shape, jnp.int32),
        thin0=pltpu.VMEM((D,), BF16),
        thin1=pltpu.VMEM((D,), BF16),
        thin2=pltpu.VMEM((D,), BF16),
        thin3=pltpu.VMEM((D,), BF16),
        thin4=pltpu.VMEM((D,), BF16),
        thin5=pltpu.VMEM((D,), BF16),
        thin6=pltpu.VMEM((D,), BF16),
        thin7=pltpu.VMEM((D,), BF16),
        thin_u=pltpu.VMEM((FF,), BF16),
        out_low=pltpu.VMEM((F, D), BF16),
        dh2=pltpu.VMEM((F, D), F32),
        vec=pltpu.VMEM((8 + FF // D, D), F32),
        top=pltpu.VMEM((heads // 2, 1, 2 * T), F32),
        tot=pltpu.VMEM((heads // 2, 1, 2 * T), F32),
        lse=pltpu.VMEM((heads // 2, 1, 2 * T), F32),
        delta=pltpu.VMEM((heads // 2, 1, 2 * T), F32),
        ot=pltpu.VMEM((DH, T), F32),
        dqt=pltpu.VMEM((DH, T), F32),
        dq=pltpu.VMEM((T, DH), BF16),
        vsum=pltpu.VMEM((1, DH), F32),
        obt=pltpu.VMEM((D, T), BF16),
        n1=pltpu.VMEM((F, D), F32),
        x1=pltpu.VMEM((F, D), F32),
        xb=pltpu.VMEM((T, D), BF16),
        xbt=pltpu.VMEM((D, T), BF16),
        df=pltpu.VMEM((T, D), BF16),
        da=pltpu.VMEM((T, D), BF16),
        act=pltpu.VMEM((T, FH), BF16),
        acto=pltpu.VMEM((2, C // 2, 2, CD // 4, T), BF16),
        atf=pltpu.VMEM((C, 2, CD // 4, T), BF16),
        att=pltpu.VMEM((2, C, CD // 4, T), BF16),
        xbm=pltpu.VMEM((T, D), BF16),
        xmt=pltpu.VMEM((D, T), BF16),
        dfm=pltpu.VMEM((T, DH), BF16),
        dum=pltpu.VMEM((T, FH // 2), BF16),
        slope=pltpu.VMEM((T, FH), F32),
        part=pltpu.VMEM((T, D), F32),
        part_in=pltpu.VMEM((2, F, D), BF16),
        part_out=pltpu.VMEM((2, F, D), BF16),
        gd_sum=pltpu.VMEM((C, CD // 4, DH), BF16),
        gd_in=pltpu.VMEM((2, N, CD // 4, DH), BF16),
        ge_sum=pltpu.VMEM((C, 2, CD // 4, DH), BF16),
        ge_in=pltpu.VMEM((2, N, 2, CD // 4, DH), BF16),
        gu_sum=pltpu.VMEM((C, CR, FH // 2), BF16),
        gu_in=pltpu.VMEM((2, N, CR, FH // 2), BF16),
        ap=pltpu.VMEM((C, 2, 4, CR // 2, DH), BF16),
        am=pltpu.VMEM((C, 4, CR // 2, DH), BF16),
        ga_in=pltpu.VMEM((2, N, 2, CR // 2, DH), BF16),
        gb_in=pltpu.VMEM((2, N, 2, CR // 2, DH), BF16),
        ix_sum=pltpu.VMEM((C, F, D), BF16),
        ix_in=pltpu.VMEM((2, N, F, D), BF16),
        fd=pltpu.VMEM((CD // 4, DH), wire_d),
        fe=pltpu.VMEM((2, CD // 4, DH), wire_d),
        fu=pltpu.VMEM((2, CR // 2, FH // 2), wire),
        fa=pltpu.VMEM((2, CR // 2, DH), wire),
        fb=pltpu.VMEM((2, CR // 2, DH), wire),
        small=pltpu.VMEM((2, 16, D), F32),
        small_ring=pltpu.VMEM((C, 8, D), F32),
        fs=pltpu.VMEM((8, D), F32),
        load_sem=dma((18,)),
        g_send=dma((2, PIECES)),
        g_recv=dma((2, N, PIECES)),
        s_send=dma((2,)),
        s_recv=dma((C,)),
        m_send=dma((3,)),
        m_recv=dma((11,)),
        r_send=dma((6, 2)),
        r_recv=dma((6, 2, N)),
        out_sem=dma((8,)),
        y_send=dma((6,)),
        y_recv=dma((6,)),
        ya_send=dma((1,)),
        ya_recv=dma((C,)),
        yq_send=dma((1,)),
        yq_recv=dma((C,)),
        c_send=dma((2,)),
        c_recv=dma((C,)),
        sr_send=dma((2,)),
        sr_recv=dma((2, N)),
        f_send=dma((2 * R - 1,)),
        h_send=dma((3, R)),
        f_recv=dma((6, R, 2)),
    )
    if C <= 8:
        scratch.update(kt=pltpu.VMEM((DH, keys), BF16))
    names = [*operands, *results, *scratch]
    roomy = C <= 8
    found = pl.pallas_call(
        functools.partial(layer_kernel, names, S, R),
        out_shape=[(pltpu.VMEM if roomy else jax.ShapeDtypeStruct)(shape, kind) for shape, kind in results.values()],
        in_specs=[spec for _, spec in operands.values()],
        out_specs=[hbm] * len(results),
        scratch_shapes=list(scratch.values()),
        compiler_params=pltpu.CompilerParams(
            collective_id=0, has_side_effects=True, vmem_limit_bytes=(56 if roomy else 62) * 1024 * 1024
        ),
        name="layer",
    )(*[value for value, _ in operands.values()])
    shapes = [(F, D), (F, D), (D // S, D), (D // S,), (D // S, D), (D // S, D), (D // S,), (D // S, D)]
    shapes += [(D // S,)] * 3 + [(D // S, FF), (FF // S,), (FF // S, D)] + [(D // S,)] * 3
    kinds = [BF16] + [F32] * (len(shapes) - 1)
    if roomy:
        found = [pltpu.with_memory_space_constraint(one, pltpu.VMEM) for one in found]
    final = pl.pallas_call(
        finish_kernel,
        out_shape=[jax.ShapeDtypeStruct(shape, kind) for shape, kind in zip(shapes, kinds, strict=True)],
        in_specs=[vmem] * len(found),
        out_specs=[vmem] * len(shapes),
        name="finish",
    )(*found)
    return (final[0][None], final[1][None], *final[2:])


def solution(mesh):
    shared = P("seq", None)
    part = P("seq")
    return jax.shard_map(
        on_device,
        mesh=mesh,
        in_specs=(P("row", "seq", None), P("row", "seq", None), P("row", None)) + (P(),) * 15,
        out_specs=(
            P("row", "seq", None),
            P("row", "seq", None),
            shared,
            part,
            shared,
            shared,
            part,
            shared,
            part,
            part,
            part,
            shared,
            part,
            shared,
            part,
            part,
            part,
        ),
        check_vma=False,
    )
```

```python
import functools
from types import SimpleNamespace as Refs

import jax
import jax.numpy as jnp
from jax import lax
from jax.experimental import pallas as pl
from jax.experimental.pallas import tpu as pltpu
from jax.sharding import PartitionSpec as P

H = 12
HEAD = 64
PIECES = 4
EPSILON = 1e-05
NEGATIVE = -1e30
MASKED = -2e30
MESH = pl.DeviceIdType.MESH
F32 = jnp.float32
BF16 = jnp.bfloat16


def nn(left, right):
    return lax.dot_general(left, right, (((1,), (0,)), ((), ())), preferred_element_type=F32)


def nt(left, right):
    return lax.dot_general(left, right, (((1,), (1,)), ((), ())), preferred_element_type=F32)


def norm_parts(summed):
    centre = summed - jnp.mean(summed, axis=-1, keepdims=True)
    variance = jnp.mean(centre * centre, axis=-1, keepdims=True)
    scale_inv = lax.rsqrt(variance + EPSILON)
    return (centre * scale_inv, scale_inv)


def norm_back(upstream, normal, scale_inv):
    return scale_inv * (
        upstream
        - jnp.mean(upstream, axis=-1, keepdims=True)
        - normal * jnp.mean(upstream * normal, axis=-1, keepdims=True)
    )


def gelu_parts(hidden):
    cumulative = 0.5 * (1.0 + lax.erf(hidden * 0.7071067811865476))
    density = jnp.exp(-0.5 * hidden * hidden) * 0.3989422804014327
    return hidden * cumulative, cumulative + hidden * density


Q_BIAS, V_BIAS, OUT_BIAS, GAIN1, SHIFT1, DOWN_BIAS, GAIN2, SHIFT2, UP_BIAS = range(9)


def layer_kernel(names, S, R, *refs):
    n = Refs(**dict(zip(names, refs, strict=True)))
    D = n.x.shape[1]
    F = n.x.shape[0]
    FF = n.wd_hbm.shape[0]
    T, DH, FH = 2 * F, D // 2, FF // 2
    C = S // 2
    N = C // 2
    CR = D // C
    CD = FF // C
    pairs = DH // (2 * HEAD)
    heads = DH // HEAD
    TILE = 256
    roomy = C <= 8
    tiles = FH // TILE

    place = lax.axis_index("seq")
    row = lax.axis_index("row")
    core = lax.rem(place, 2)
    chip = place // 2
    pos = jnp.where(lax.rem(chip, 2) == 0, chip // 2, C - 1 - chip // 2)

    def around(steps):
        return lax.rem(pos + (steps + C), C)

    def chip_at(where):
        return jnp.where(where < N, 2 * where, 2 * (C - 1 - where) + 1)

    sibling = (2 * chip + 1 - core, row)
    right = (2 * chip_at(around(1)) + core, row)
    left = (2 * chip_at(around(-1)) + core, row)
    ring = (right, left)
    parity = lax.rem(row, 2)
    mate_row = row + 1 - 2 * parity
    mate = (place, mate_row)
    others = []
    for dr in range(R):
        for dc in range(2):
            if dr or dc:
                others.append((lax.rem(row + dr, R), lax.rem(core + dc, 2)))

    def remote(src, dst, send, recv, device):
        return pltpu.make_async_remote_copy(
            src_ref=src, dst_ref=dst, send_sem=send, recv_sem=recv, device_id=device, device_id_type=MESH
        )

    started = []

    def start(copy):
        copy.start()
        started.append(copy)

    barrier = pltpu.get_barrier_semaphore()
    partners = [right, left] + [(2 * chip + c, r) for r, c in others]
    for device in partners:
        pl.semaphore_signal(barrier, inc=1, device_id=device, device_id_type=MESH)

    xa = n.xa
    own_rows = pl.multiple_of(core * F, F)
    other_rows = pl.multiple_of((1 - core) * F, F)
    half_d = pl.multiple_of(core * DH, 128)
    half_f = pl.multiple_of(core * FH, 128)
    loads = []
    for source, target in (
        (n.x, xa.at[pos, pl.ds(own_rows, F)]),
        (n.wq_hbm.at[:, pl.ds(half_d, DH)], n.wq),
        (n.wk_hbm.at[:, pl.ds(half_d, DH)], n.wkv.at[:, pl.ds(0, DH)]),
        (n.wv_hbm.at[:, pl.ds(half_d, DH)], n.wkv.at[:, pl.ds(DH, DH)]),
        (n.lens_hbm, n.lens),
        (n.bias_q, n.thin0),
        (n.bias_v, n.thin1),
        (n.bias_o, n.thin2),
        (n.gain1, n.thin3),
        (n.shift1, n.thin4),
        (n.bias_d, n.thin5),
        (n.gain2, n.thin6),
        (n.shift2, n.thin7),
        (n.bias_u, n.thin_u),
        (n.wo_hbm, n.wo),
        (n.wu_hbm.at[:, pl.ds(half_f, FH)], n.wu),
        (n.wd_hbm.at[pl.ds(half_f, FH)], n.wd),
        (n.cot_hbm, n.cot),
    ):
        loads.append(pltpu.make_async_copy(source, target, n.load_sem.at[len(loads)]))
        loads[-1].start()

    pl.semaphore_wait(barrier, len(partners))

    step_rows = F // PIECES

    def hop_view(where, piece):
        return xa.at[where, pl.ds(pl.multiple_of(own_rows + piece * step_rows, step_rows), step_rows)]

    def hop_send(d, h, turn):
        view = hop_view(around((h - 1) * (2 * d - 1)), lax.rem(turn + d * (PIECES // 2), PIECES))
        return remote(view, view, n.g_send.at[d, turn], n.g_recv.at[d, h - 1, turn], ring[d])

    def hop_first(d, turn):
        first = lax.rem(turn + d * (PIECES // 2), PIECES)
        src = n.x.at[pl.ds(first * step_rows, step_rows)]
        return remote(src, hop_view(pos, first), n.g_send.at[d, turn], n.g_recv.at[d, 0, turn], ring[d])

    def hop_recv(d, h, turn):
        view = hop_view(around(h * (2 * d - 1)), lax.rem(turn + d * (PIECES // 2), PIECES))
        return remote(view, view, n.g_send.at[d, turn], n.g_recv.at[d, h - 1, turn], ring[d])

    def share_send(where, d=0):
        view = xa.at[where, pl.ds(own_rows, F)]
        return remote(view, view, n.s_send.at[d], n.s_recv.at[where], sibling)

    def share_recv(where):
        view = xa.at[where, pl.ds(other_rows, F)]
        return remote(view, view, n.s_send.at[0], n.s_recv.at[where], sibling)

    for turn in range(PIECES):
        hop_first(0, turn).start()
        hop_first(1, turn).start()
        if turn == 0:
            remote(n.x, xa.at[pos, pl.ds(own_rows, F)], n.s_send.at[0], n.s_recv.at[pos], sibling).start()

    def gather_step(h, turn):
        for d in range(2):
            hop_recv(d, h, turn).wait_recv()
            hop_send(d, h, turn).wait_send()

        @pl.when((h < N - 1) | (turn < PIECES // 2))
        def _():
            hop_send(0, h + 1, turn).start()
            hop_send(1, h + 1, turn).start()

        @pl.when(turn == PIECES - 1)
        def _():
            share_send(pos, 0).wait_send()
            pl.when(h > 1)(share_send(pos, 1).wait_send)
            share_send(around(-h), 0).start()
            share_send(around(h), 1).start()

    def gather_last():
        for turn in range(PIECES // 2):
            for d in range(2):
                hop_recv(d, N, turn).wait_recv()
                hop_send(d, N, turn).wait_send()
        share_send(pos, 0).wait_send()
        share_send(around(N), 0).start()

    def gather_sent():
        share_send(pos, 0).wait_send()
        share_send(pos, 1).wait_send()

    for load in loads[:14]:
        load.wait()
    for index, thin in enumerate((n.thin0, n.thin1, n.thin2, n.thin3, n.thin4, n.thin5, n.thin6, n.thin7)):
        n.vec[index : index + 1] = thin[...].astype(F32).reshape(1, D)
    for index in range(FF // D):
        n.vec[UP_BIAS + index : UP_BIAS + index + 1] = (
            n.thin_u[D * index : D * (index + 1)].astype(F32).reshape(1, D)
        )

    ends = []
    total = 0
    for i in range(n.lens.shape[1]):
        total = total + n.lens[0, i]
        ends.append(total)

    def ids(positions, padding):
        counted = jnp.zeros_like(positions)
        for end in ends:
            counted = counted + (positions >= end).astype(jnp.int32)
        return jnp.where(positions < ends[-1], counted, padding)

    query_ids = ids(lax.broadcasted_iota(jnp.int32, (1, T), 1) + chip * T, -1)

    def score_bias(where, first=0, size=None):
        size = T if size is None else size
        key_ids = ids(lax.broadcasted_iota(jnp.int32, (size, 1), 0) + (chip_at(where) * T + first), -2)
        found = jnp.where(key_ids == query_ids, 0.0, MASKED)
        return jnp.concatenate([found, found], axis=1)

    lane = lax.broadcasted_iota(jnp.int32, (T, 2 * HEAD), 1)

    def head_masked(values, target):
        for pair in range(pairs):
            both = values[:, 2 * HEAD * pair : 2 * HEAD * (pair + 1)]
            target[pair, :T] = jnp.where(lane < HEAD, both, 0.0).astype(BF16)
            target[pair, T:] = jnp.where(lane < HEAD, 0.0, both).astype(BF16)

    def of_pair(j):
        return slice(T * (j % 2), T * (j % 2 + 1))

    def of_head(j):
        return slice(HEAD * j, HEAD * (j + 1))

    def key_rows(where):
        return pl.ds(pl.multiple_of(where * T, T), T)

    def forward_block(where, first=0, size=None):
        size = T if size is None else size
        rows = pl.ds(pl.multiple_of(where * T + first, size), size)
        xk = xa[where, pl.ds(first, size)]
        both = nn(xk, n.wkv[...])
        keys = both[:, :DH].astype(BF16)
        scores = [nt(keys[:, 2 * HEAD * p : 2 * HEAD * (p + 1)], n.qm[p]) for p in range(pairs)]
        n.kva[rows, :DH] = keys
        if roomy:
            n.kt[:, rows] = keys.T
        values = (both[:, DH:] + n.vec[V_BIAS : V_BIAS + 1, pl.ds(half_d, DH)]).astype(BF16)
        n.kva[rows, DH:] = values
        values_t = values.T
        n.xt[:, rows] = xk.T
        bias = score_bias(where, first, size)
        weights, factors = [], []
        for p in range(pairs):
            st = scores[p] + bias
            top = n.top[p]
            new_top = jnp.maximum(top, jnp.max(st, axis=0, keepdims=True))
            found = jnp.exp(st - new_top)
            factors.append(jnp.exp(top - new_top))
            n.tot[p] = n.tot[p] * factors[p] + jnp.sum(found, axis=0, keepdims=True)
            n.top[p] = new_top
            weights.append(found.astype(BF16))
        for j in range(heads):
            n.ot[of_head(j)] = n.ot[of_head(j)] * factors[j // 2][:, of_pair(j)] + nn(
                values_t[of_head(j)], weights[j // 2][:, of_pair(j)]
            )

    n.top[...] = jnp.full(n.top.shape, NEGATIVE, F32)
    n.tot[...] = jnp.zeros(n.tot.shape, F32)
    n.ot[...] = jnp.zeros(n.ot.shape, F32)
    small = n.small.at[core]
    small[...] = jnp.zeros(small.shape, F32)

    share_recv(pos).wait_recv()
    queries = (nn(xa[pos], n.wq[...]) + n.vec[Q_BIAS : Q_BIAS + 1, pl.ds(half_d, DH)]).astype(BF16)
    head_masked(queries.astype(F32) * 0.125, n.qm)

    def forward_step(step, carry):
        h, turn = 1 + step // PIECES, lax.rem(step, PIECES)
        gather_step(h, turn)

        @pl.when((step == 0) | ((h > 1) & (turn < 2)))
        def _():
            where = around((h - 1) * (2 * turn - 1))

            @pl.when(step > 0)
            def _():
                share_recv(where).wait_recv()

            forward_block(where)

        return carry

    lax.fori_loop(0, PIECES * (N - 1), forward_step, 0)

    def forward_last(step, carry):
        where = around((N - 1) * (2 * step - 1))

        @pl.when(step == 1)
        def _():
            gather_last()

        share_recv(where).wait_recv()
        forward_block(where)
        return carry

    lax.fori_loop(0, 2, forward_last, 0)

    def forward_half(step, carry):
        @pl.when(step == 1)
        def _():
            share_recv(around(N)).wait_recv()

        forward_block(around(N), pl.multiple_of(own_rows + step * (other_rows - own_rows), F), F)
        return carry

    lax.fori_loop(0, 2, forward_half, 0)

    gather_sent()
    safe = jnp.where(n.tot[...] > 0.5, n.tot[...], 1.0)
    n.lse[...] = n.top[...] + jnp.log(safe)
    for j in range(heads):
        n.ot[of_head(j)] = n.ot[of_head(j)] / safe[j // 2][:, of_pair(j)]

    swaps = []

    def swap(index, src, dst, landed):
        if len(swaps) >= 3:
            sent(swaps[-3])
        send, recv = n.m_send.at[len(swaps) % 3], n.m_recv.at[index]
        start(remote(src, dst, send, recv, sibling))
        swaps.append(started[-1])
        return remote(src, landed, send, recv, sibling)

    def lend(index, src, dst, device, landed, recv_index=None):
        recv_index = index if recv_index is None else recv_index
        start(remote(src, dst, n.y_send.at[index], n.y_recv.at[recv_index], device))
        return remote(src, landed, n.y_send.at[index], n.y_recv.at[index], device)

    def deliver(src, dst, index):
        copy = pltpu.make_async_copy(src, dst, n.out_sem.at[index])
        copy.start()
        delivered.append(copy)

    delivered = []

    def sent(copy):
        started[:] = [other for other in started if other is not copy]
        copy.wait_send()

    obt = n.obt
    own_half = pl.ds(pl.multiple_of(core * DH, DH), DH)
    other_half = pl.ds(pl.multiple_of((1 - core) * DH, DH), DH)
    obt[own_half] = n.ot[...].astype(BF16)
    swapped = swap(0, obt.at[own_half], obt.at[own_half], obt.at[other_half])
    loads[14].wait()
    branch = nn(obt[own_half, pl.ds(own_rows, F)].T, n.wo[own_half])
    swapped.wait_recv()

    def vec(index):
        return n.vec[index : index + 1]

    branch = branch + nn(obt[other_half, pl.ds(own_rows, F)].T, n.wo[other_half]) + vec(OUT_BIAS)
    first_normal, first_scale = norm_parts(xa[pos, pl.ds(own_rows, F)].astype(F32) + branch)
    n.n1[...] = first_normal
    normed = first_normal * vec(GAIN1) + vec(SHIFT1)
    n.x1[...] = normed
    xb = n.xb
    xb[pl.ds(own_rows, F)] = normed.astype(BF16)
    swapped = swap(1, xb.at[pl.ds(own_rows, F)], xb.at[pl.ds(own_rows, F)], xb.at[pl.ds(other_rows, F)])
    xbm = n.xbm
    lent_xb = lend(0, xb.at[pl.ds(own_rows, F)], xbm.at[pl.ds(own_rows, F)], mate, xbm.at[pl.ds(own_rows, F)])
    loads[15].wait()

    act, slope = n.act, n.slope
    acto, att = n.acto, n.att
    du = act

    def up_rows(rows):
        for t in range(FH // D):
            cols = slice(D * t, D * (t + 1))
            bias = n.vec[pl.ds(UP_BIAS + core * (FH // D) + t, 1)]
            value, tangent = gelu_parts(nn(xb[rows], n.wu[:, cols]) + bias)
            low = value.astype(BF16)
            act[rows, cols] = low
            turned = low.T
            for c in range(D // CD):
                for half in range(2):
                    for side in range(2):
                        first = CD * c + CD // 2 * half + CD // 4 * side
                        acto[side, D // CD * t + c, half, :, rows] = turned[first : first + CD // 4]
            slope[rows, cols] = tangent

    up_rows(pl.ds(own_rows, F))
    swapped.wait_recv()
    up_rows(pl.ds(other_rows, F))
    own_ff = pl.ds(core * (C // 2), C // 2)
    other_ff = pl.ds((1 - core) * (C // 2), C // 2)
    lent_act = lend(1, acto.at[1, :, 1 - parity], att.at[1, own_ff], mate, att.at[1, own_ff])
    swapped_first = swap(10, acto.at[0], n.atf.at[own_ff], n.atf.at[other_ff])
    swapped_act = swap(2, acto.at[1, :, parity], att.at[0, own_ff], att.at[0, other_ff])
    loads[16].wait()
    loads[17].wait()
    part = n.part

    def part_swap(index):
        n.part_out[index] = part[pl.ds(other_rows, F)].astype(BF16)
        return swap(3 + 2 * index, n.part_out.at[index], n.part_in.at[index], n.part_in.at[index])

    part[...] = nn(act[...], n.wd[...])
    part_arrives = part_swap(0)
    n.atf[own_ff] = acto[0]
    att[0, own_ff] = acto[1, :, parity]
    n.xbt[...] = xb[...].T
    upstream = n.cot[...].astype(F32)
    small[SHIFT2 : SHIFT2 + 1] = jnp.sum(upstream, axis=0, keepdims=True)
    part_arrives.wait_recv()
    second_normal, second_scale = norm_parts(
        n.x1[...] + part[pl.ds(own_rows, F)] + n.part_in[0].astype(F32) + vec(DOWN_BIAS)
    )
    n.out_low[...] = (second_normal * vec(GAIN2) + vec(SHIFT2)).astype(BF16)
    residual = norm_back(upstream * vec(GAIN2), second_normal, second_scale)
    n.dh2[...] = residual
    low = residual.astype(BF16)
    df = n.df
    df[pl.ds(own_rows, F)] = low
    swapped = swap(4, df.at[pl.ds(own_rows, F)], df.at[pl.ds(own_rows, F)], df.at[pl.ds(other_rows, F)])
    dfm = n.dfm
    lent_df = []
    for c in range(2):
        start(
            remote(
                df.at[pl.ds(own_rows, F), pl.ds(DH * c, DH)],
                dfm.at[pl.ds(own_rows, F)],
                n.y_send.at[2 + c],
                n.y_recv.at[2 + core],
                (2 * chip + c, mate_row),
            )
        )
        lent_df.append(
            remote(
                df.at[pl.ds(own_rows, F), pl.ds(DH * c, DH)],
                dfm.at[pl.ds(F * c, F)],
                n.y_send.at[2 + c],
                n.y_recv.at[2 + c],
                (2 * chip + c, mate_row),
            )
        )
    small[GAIN2 : GAIN2 + 1] = jnp.sum(upstream * second_normal, axis=0, keepdims=True)
    small[DOWN_BIAS : DOWN_BIAS + 1] = jnp.sum(low.astype(F32), axis=0, keepdims=True)
    swapped.wait_recv()

    class Flow:
        def __init__(self, index, chunk, landing, split, ready=None):
            self.index, self.chunk, self.landing, self.split, self.ready = index, chunk, landing, split, ready
            self.last = [None, None]

        def parts(self, d, distance):
            where = around(distance if d == 0 else -distance)
            src, dst = self.chunk(where), self.landing.at[d, distance - 1]
            if distance == N:
                src, dst = src.at[self.split[d]], dst.at[self.split[d]]
            send, recv = n.r_send.at[self.index, d], n.r_recv.at[self.index, d, distance - 1]
            return remote(src, dst, send, recv, ring[d]), dst

        def put(self, d, distance):
            if distance < N:
                self.last[d].wait_send()
            self.last[d] = self.parts(d, distance)[0]
            self.last[d].start()

        def sent(self):
            for copy in self.last:
                copy.wait_send()

        def begin(self):
            if self.ready is not None:
                self.ready(around(N))
            self.put(0, N)
            self.put(1, N)

        def step(self, distance):
            for d in range(2):
                where = around(distance if d == 0 else -distance)
                if self.ready is not None:
                    self.ready(where)
                arriving, landed = self.parts(d, distance + 1)
                arriving.wait_recv()
                target = self.chunk(where)
                if distance + 1 == N:
                    target = target.at[self.split[d]]
                target[...] = (target[...].astype(F32) + landed[...].astype(F32)).astype(BF16)
                self.put(d, distance)

        def end(self):
            if self.ready is not None:
                self.ready(pos)
            found = self.chunk(pos)[...].astype(F32)
            for d in range(2):
                arriving, landed = self.parts(d, 1)
                arriving.wait_recv()
                found = found + landed[...].astype(F32)
            return found

    def add_lent(first, lent, where):
        c = chip_at(where)
        lent(c).wait_recv()
        both = pl.ds(first, 2)
        n.ap[c, parity, both] = (n.ap[c, parity, both].astype(F32) + n.am[c, both].astype(F32)).astype(BF16)

    def lent_query(c):
        return remote(n.ap.at[c, 1 - parity, 0], n.am.at[c, 0], n.yq_send.at[0], n.yq_recv.at[c], mate)

    def lent_pair(c):
        both = pl.ds(2, 2)
        return remote(n.ap.at[c, 1 - parity, both], n.am.at[c, both], n.ya_send.at[0], n.ya_recv.at[c], mate)

    whole = slice(None)
    if CD % 128 == 0:
        split_d = [pl.ds(0, CD // 8), pl.ds(CD // 8, CD // 8)]
    else:
        split_d = [(whole, pl.ds(0, 128)), (whole, pl.ds(128, DH - 128))]
    flow_d = Flow(0, lambda where: n.gd_sum.at[chip_at(where)], n.gd_in, split_d)
    flow_e = Flow(4, lambda where: n.ge_sum.at[chip_at(where)], n.ge_in, [pl.ds(0, 1), pl.ds(1, 1)])
    flow_u = Flow(
        1,
        lambda where: n.gu_sum.at[chip_at(where)],
        n.gu_in,
        [(whole, pl.ds(0, FH // 4)), (whole, pl.ds(FH // 4, FH // 4))],
    )
    flow_a = Flow(
        2,
        lambda where: n.ap.at[chip_at(where), parity, pl.ds(2, 2)],
        n.ga_in,
        [pl.ds(0, 1), pl.ds(1, 1)],
        functools.partial(add_lent, 2, lent_pair),
    )
    flow_b = Flow(
        5,
        lambda where: n.ap.at[chip_at(where), parity, pl.ds(0, 2)],
        n.gb_in,
        [pl.ds(0, 1), pl.ds(1, 1)],
        functools.partial(add_lent, 0, lent_query),
    )
    flow_x = Flow(3, lambda where: n.ix_sum.at[where], n.ix_in, [pl.ds(0, F // 2), pl.ds(F // 2, F // 2)])

    scattered = []

    def scatter(index, source, gathered, split):
        while scattered:
            sent(scattered.pop())
        deliver(source.at[core] if split else source, gathered.at[row, core], 2 + index)
        for k, (r, c) in enumerate(others):
            view = source.at[c] if split else source
            start(
                remote(
                    view, gathered.at[row, core], n.f_send.at[k], n.f_recv.at[index, row, core], (2 * chip + c, r)
                )
            )
            scattered.append(started[-1])

    def collect(index, source, gathered, split):
        for r, c in others:
            view = source.at[c] if split else source
            remote(
                view, gathered.at[r, c], n.f_send.at[0], n.f_recv.at[index, r, c], (2 * chip + c, r)
            ).wait_recv()

    def spread(index, source, gathered):
        pl.when(core == parity)(spread_own(index, source, gathered).start)
        for k in range(R):
            copy = spread_copy(index, source, gathered, k)
            if k == 0:
                pl.when(core != parity)(copy.start)
            else:
                copy.start()

    def spread_own(index, source, gathered):
        return pltpu.make_async_copy(source, gathered.at[row // 2, core], n.out_sem.at[2 + index])

    def spread_copy(index, source, gathered, k):
        device = (2 * chip + parity, lax.rem(row + k, R))
        return remote(
            source, gathered.at[row // 2, core], n.h_send.at[index, k], n.f_recv.at[index, row // 2, core], device
        )

    def spread_done(index, source, gathered):
        for q in range(R // 2):
            for c in range(2):
                arriving = remote(
                    source, gathered.at[q, c], n.h_send.at[index, 0], n.f_recv.at[index, q, c], sibling
                )
                pl.when((2 * q + core != row) | (core != c))(arriving.wait_recv)
        pl.when(core == parity)(spread_own(index, source, gathered).wait)
        for k in range(R):
            copy = spread_copy(index, source, gathered, k)
            if k == 0:
                pl.when(core != parity)(copy.wait_send)
            else:
                copy.wait_send()

    def down_end():
        n.fd[...] = flow_d.end().astype(n.fd.dtype)
        spread(0, n.fd, n.yd)

    def first_end():
        n.fe[...] = flow_e.end().astype(n.fe.dtype)
        scatter(4, n.fe, n.ye, True)

    def up_end():
        found = flow_u.end()
        for c in range(2):
            n.fu[c] = found[CR // 2 * c : CR // 2 * (c + 1)].astype(n.fu.dtype)
        scatter(5, n.fu, n.yu, True)

    def input_step(distance):
        join(around(distance))
        join(around(-distance))
        flow_x.step(distance)

    def input_end():
        join(pos)
        n.dh2[...] = n.x1[...] + flow_x.end()
        deliver(n.dh2, n.grad_x, 1)

    def query_begin():
        lent_out.wait_recv()
        flow_b.begin()

    def attention_end(flow, index, source, gathered):
        source[...] = flow.end().astype(source.dtype)
        spread(index, source, gathered)

    def chain(step, end):
        return [functools.partial(step, distance) for distance in range(N - 1, 0, -1)] + [end]

    chain_d = chain(flow_d.step, down_end)
    chain_u = chain(flow_u.step, up_end)
    chain_e = chain(flow_e.step, first_end)
    chain_x = chain(input_step, input_end)
    chain_a = [flow_a.begin] + chain(flow_a.step, functools.partial(attention_end, flow_a, 2, n.fa, n.ya))
    chain_b = [query_begin] + chain(flow_b.step, functools.partial(attention_end, flow_b, 1, n.fb, n.yb))

    def advance(one):
        one.pop(0)()

    def wide(p, first=0):
        return slice(first + 2 * HEAD * p, first + 2 * HEAD * (p + 1))

    def long(p):
        return slice(2 * T * p, 2 * T * (p + 1))

    def find_probs(where):
        rows, bias = key_rows(where), score_bias(where)
        for p in range(pairs):
            n.slope[:, long(p)] = nt(n.kva[rows, wide(p)], n.qm[p])
        for p in range(pairs):
            probs = jnp.exp(n.slope[:, long(p)] + bias - n.lse[p])
            n.slope[:, long(p)] = probs
            n.probs[:, long(p)] = probs.astype(BF16)

    def backward_block(where, ready):
        rows = key_rows(where)
        bias = None if ready else score_bias(where)
        keys_t = n.kt[:, rows] if roomy else n.kva[rows, :DH].T

        for p in range(pairs):
            if not ready:
                n.slope[:, long(p)] = nt(n.kva[rows, wide(p)], n.qm[p])
            n.grad_probs[:, long(p)] = nt(n.kva[rows, wide(p, DH)], n.dm[p])
        for p in range(pairs):
            if ready:
                probs = n.slope[:, long(p)]
            else:
                probs = jnp.exp(n.slope[:, long(p)] + bias - n.lse[p])
                n.probs[:, long(p)] = probs.astype(BF16)
            n.grad_scores[:, long(p)] = (probs * (n.grad_probs[:, long(p)] - n.delta[p])).astype(BF16)
        for p in range(pairs):
            low = nn(n.probs[:, long(p)], n.dm[p]).astype(BF16)
            n.kva[rows, wide(p, DH)] = low
            n.kva[rows, wide(p)] = nn(n.grad_scores[:, long(p)], n.qm[p]).astype(BF16)
            n.vsum[:, wide(p)] += jnp.sum(low.astype(F32), axis=0, keepdims=True)
        for j in range(heads):
            n.dqt[of_head(j)] += nn(keys_t[of_head(j)], n.grad_scores[:, T * j : T * (j + 1)])
        return nt(n.kva[rows], n.wkv[...])

    swapped_first.wait_recv()
    for t in range(C // 2):
        two = slice(2 * t, 2 * t + 2)
        found = nn(n.atf[two].reshape(CD, T), df[:, pl.ds(half_d, DH)])
        n.ge_sum[two] = found.astype(BF16).reshape(2, 2, CD // 4, DH)
    flow_e.begin()
    for t in range(FH // D):
        cols = slice(D * t, D * (t + 1))
        low = (nt(df[...], n.wd[cols, :]) * slope[:, cols]).astype(BF16)
        du[:, cols] = low
        small[pl.ds(UP_BIAS + core * (FH // D) + t, 1)] = jnp.sum(low.astype(F32), axis=0, keepdims=True)

    quarter = pl.multiple_of(parity * (FH // 2), FH // 2)
    other_quarter = pl.multiple_of((1 - parity) * (FH // 2), FH // 2)
    lent_du = lend(4, du.at[:, pl.ds(other_quarter, FH // 2)], n.dum, mate, n.dum)
    part[...] = nt(du[...], n.wu[...])
    part_arrives = part_swap(1)

    find_probs(around(N))
    part_arrives.wait_recv()
    grad_normed = n.dh2[...] + part[pl.ds(own_rows, F)] + n.part_in[1].astype(F32)
    normal = n.n1[...]
    small[GAIN1 : GAIN1 + 1] = jnp.sum(grad_normed * normal, axis=0, keepdims=True)
    small[SHIFT1 : SHIFT1 + 1] = jnp.sum(grad_normed, axis=0, keepdims=True)
    grad_branch = norm_back(grad_normed * vec(GAIN1), normal, first_scale)
    n.x1[...] = grad_branch
    low = grad_branch.astype(BF16)
    da = n.da
    da[pl.ds(own_rows, F)] = low
    swapped = swap(6, da.at[pl.ds(own_rows, F)], da.at[pl.ds(own_rows, F)], da.at[pl.ds(other_rows, F)])
    small[OUT_BIAS : OUT_BIAS + 1] = jnp.sum(low.astype(F32), axis=0, keepdims=True)
    swapped.wait_recv()

    advance(chain_e)
    grad_mixed = nt(da[...], n.wo[own_half]).astype(BF16).astype(F32)
    head_masked(grad_mixed, n.dm)
    grad_mixed_t = grad_mixed.T
    for j in range(heads):
        n.delta[j // 2, :, of_pair(j)] = jnp.sum(grad_mixed_t[of_head(j)] * n.ot[of_head(j)], axis=0, keepdims=True)

    def grad_down():
        swapped_act.wait_recv()
        swapped_actm.wait_recv()
        rows = CD // 2
        for lent in lent_df:
            lent.wait_recv()
        for t in range(C // 2):
            two = slice(2 * t, 2 * t + 2)
            found = nn(att[0, two].reshape(rows, T), df[:, pl.ds(half_d, DH)])
            found = found + nn(att[1, two].reshape(rows, T), dfm[...])
            n.gd_sum[two] = found.astype(BF16).reshape(2, CD // 4, DH)

    def forward_xb():
        lent_xb.wait_recv()
        return swap(8, xbm.at[pl.ds(own_rows, F)], xbm.at[pl.ds(own_rows, F)], xbm.at[pl.ds(other_rows, F)])

    def grad_up():
        swapped_xbm.wait_recv()
        n.xmt[...] = xbm[...].T
        lent_du.wait_recv()
        for t in range(FH // 2 // TILE):
            cols = slice(TILE * t, TILE * (t + 1))
            found = nn(n.xbt[...], du[:, pl.ds(pl.multiple_of(quarter + t * TILE, TILE), TILE)])
            found = (found + nn(n.xmt[...], n.dum[:, cols])).astype(BF16)
            for c in range(C):
                n.gu_sum[c, :, cols] = found[CR * c : CR * (c + 1)]

    def grad_attention(indices, left, right):
        for t in range(2):
            found = nn(left(pl.ds(DH * t, DH)), right)
            for k, index in enumerate(indices):
                for c in range(DH // CR):
                    for half in range(2):
                        first = CR * c + CR // 2 * half
                        n.ap[DH // CR * t + c, half, index] = found[
                            first : first + CR // 2, DH * k : DH * (k + 1)
                        ].astype(BF16)

    n.dqt[...] = jnp.zeros(n.dqt.shape, F32)
    n.vsum[...] = jnp.zeros(n.vsum.shape, F32)

    crossing, turn_of_cross = [], [0]

    def put_cross(where):
        if len(crossing) == 2:
            crossing.pop(0).wait_send()
        crossing.append(cross(where))
        crossing[-1].start()

    def cross(where):
        send, recv = n.c_send.at[turn_of_cross[0] % 2], n.c_recv.at[where]
        return remote(xa.at[where, pl.ds(0, F)], xa.at[where, pl.ds(F, F)], send, recv, sibling)

    def key_block(where, extra=None, ready=False):
        found = backward_block(where, ready)
        if extra is not None:
            found = found + extra()
        found = found.astype(BF16)
        first, second = found[:F], found[F:]
        xa[where, pl.ds(0, F)] = jnp.where(core == 0, second, first)
        n.ix_sum[where] = jnp.where(core == 0, first, second)

    def join(where):
        cross(where).wait_recv()
        n.ix_sum[where] = (
            n.ix_sum[where].astype(F32) + xa[where, pl.ds(F, F)].astype(F32)
        ).astype(BF16)

    def query_part():
        grad_query = (n.dqt[...] * 0.125).T.astype(BF16)
        n.dq[...] = grad_query
        return nt(grad_query, n.wq[...])

    around_small = n.small_ring
    mine = pl.ds(pl.multiple_of(core * 8, 8), 8)

    def small_send(d, h):
        view = around_small.at[around(1 - h if d == 0 else h - 1)]
        return remote(view, view, n.sr_send.at[d], n.sr_recv.at[d, h - 1], ring[d])

    def small_recv(d, h):
        view = around_small.at[around(-h if d == 0 else h)]
        return remote(view, view, n.sr_send.at[d], n.sr_recv.at[d, h - 1], ring[d])

    small_last = [None, None]

    def small_put(d, h):
        if small_last[d] is not None:
            small_last[d].wait_send()
        small_last[d] = small_send(d, h)
        small_last[d].start()


    def small_step(h):
        small_recv(0, h).wait_recv()
        if h < N:
            small_recv(1, h).wait_recv()
            small_put(0, h + 1)
            if h + 1 < N:
                small_put(1, h + 1)

    def small_end():
        found = around_small[0].astype(F32)
        for where in range(1, C):
            found = found + around_small[where].astype(F32)
        n.fs[:, :DH] = found[:8]
        n.fs[:, DH:] = found[8:]
        scatter(3, n.fs, n.ys, False)

    chain_s = [functools.partial(small_step, h) for h in range(1, N + 1)] + [small_end]
    blocks = [N] + [side * d for d in range(N - 1, 0, -1) for side in (1, -1)] + [0]
    if N == 4:
        due = [""] * 8
        due[0], due[1], due[3], due[4], due[5], due[7] = "mfF", "De", "dOx", "U", "e", "u"
        middle, last = "Sx", "basubasduaebsduabsxdsabx"
    else:
        due = ["mfFD", "e"] + ["ed"[b % 4 // 2] if b % 2 == 0 else "x" for b in range(2, 2 * N)]
        due[4] += "OU"
        middle, last = "S", "ebaxdus" * (N + 2)
    chains = dict(e=chain_e, d=chain_d, u=chain_u, x=chain_x, a=chain_a, b=chain_b, s=chain_s)

    def begin_input():
        join(around(N))
        flow_x.begin()

    def begin_down():
        grad_down()
        flow_d.begin()

    def begin_forward():
        nonlocal swapped_xbm
        swapped_xbm = forward_xb()

    def begin_up():
        grad_up()
        flow_u.begin()

    def begin_out():
        nonlocal lent_out
        grad_attention([1], lambda rows: obt[rows], da[:, pl.ds(half_d, DH)])
        lent_out = lend(5, n.ap.at[:, 1 - parity, 1], n.am.at[:, 1], mate, n.am.at[:, 1])

    def begin_small():
        small_swap.wait_recv()
        both = (n.small[0, mine] + n.small[1, mine]).astype(BF16)
        around_small[pos] = jnp.concatenate([both[:, :DH], both[:, DH:]])
        small_put(0, 1)
        small_put(1, 1)

    def mate_hidden():
        nonlocal swapped_actm
        lent_act.wait_recv()
        swapped_actm = swap(9, att.at[1, own_ff], att.at[1, own_ff], att.at[1, other_ff])

    swapped_xbm = lent_out = swapped_actm = small_swap = None
    begins = dict(m=mate_hidden, F=begin_input, D=begin_down, U=begin_up, O=begin_out, S=begin_small, f=begin_forward)

    def work(letters):
        for letter in letters:
            if letter in begins:
                begins[letter]()
            elif chains[letter]:
                chains[letter].pop(0)()

    for index, step in enumerate(blocks):
        key_block(around(step), query_part if step == 0 else None, index == 0)
        turn_of_cross[0] = index
        put_cross(around(step))
        if step == 0:
            small[Q_BIAS : Q_BIAS + 1, pl.ds(half_d, DH)] = jnp.sum(n.dq[...].astype(F32), axis=0, keepdims=True)
            small[V_BIAS : V_BIAS + 1, pl.ds(half_d, DH)] = n.vsum[...]
            small_swap = swap(7, small, small, n.small.at[1 - core])
        work(due[index])
    grad_attention([0], lambda rows: n.xt[rows, key_rows(pos)], n.dq[...])
    ordered = [around(d) for d in [N] + [side * d for d in range(N - 1, 0, -1) for side in (1, -1)] + [0]]
    for where in ordered[:3]:
        lent_query(chip_at(where)).start()
    deliver(n.out_low, n.out, 0)
    work(middle)
    grad_attention([2, 3], lambda rows: n.xt[rows], n.kva[...])
    for k, where in enumerate(ordered):
        if k >= 3:
            lent_query(chip_at(where)).start()
        lent_pair(chip_at(where)).start()

    work(last)
    assert not any(chains.values())
    spread_done(0, n.fd, n.yd)
    collect(5, n.fu, n.yu, True)
    collect(4, n.fe, n.ye, True)
    collect(3, n.fs, n.ys, False)
    spread_done(2, n.fa, n.ya)
    spread_done(1, n.fb, n.yb)
    for copy in started:
        copy.wait_send()
    for copy in delivered:
        copy.wait()
    for flow in (flow_e, flow_d, flow_u, flow_x, flow_a, flow_b):
        flow.sent()
    remote(n.ap.at[:, 1 - parity, 0], n.am.at[:, 0], n.yq_send.at[0], n.yq_recv.at[0], mate).wait_send()
    both = pl.ds(2, 2)
    remote(n.ap.at[:, 1 - parity, both], n.am.at[:, both], n.ya_send.at[0], n.ya_recv.at[0], mate).wait_send()
    for copy in crossing:
        copy.wait_send()
    for copy in small_last:
        if copy is not None:
            copy.wait_send()


def finish_kernel(out, grad_x, yd, ye, yu, ya, yb, ys, *targets):
    (
        to_out,
        to_grad_x,
        to_query,
        to_query_bias,
        to_key,
        to_value,
        to_value_bias,
        to_o,
        to_out_bias,
        to_gain1,
        to_shift1,
        to_up,
        to_up_bias,
        to_down,
        to_down_bias,
        to_gain2,
        to_shift2,
    ) = targets
    R = yu.shape[0]
    D = out.shape[1]
    place = lax.axis_index("seq")

    def over_rows(gathered, *index, first=0, by=1):
        found = gathered[(first, *index)].astype(F32)
        for r in range(first + by, gathered.shape[0], by):
            found = found + gathered[(r, *index)].astype(F32)
        return found

    to_out[...] = out[...]
    to_grad_x[...] = grad_x[...]
    for c in range(2):
        width = yd.shape[-1]
        rows = yd.shape[2]
        to_down[:rows, width * c : width * (c + 1)] = over_rows(ye, c)
        to_down[rows:, width * c : width * (c + 1)] = over_rows(yd, c)
        for gathered, index, target in ((yb, 0, to_query), (yb, 1, to_o), (ya, 0, to_key), (ya, 1, to_value)):
            target[:, width * c : width * (c + 1)] = over_rows(gathered, c, index)
        width = yu.shape[-1]
        for half in range(2):
            first = width * (2 * c + half)
            to_up[:, first : first + width] = over_rows(yu, c, first=half, by=2)
    sums = jnp.concatenate([over_rows(ys, 0), over_rows(ys, 1)])
    width = to_query_bias.shape[0]
    turned = pltpu.roll(sums, lax.rem(D - place * width, D), 1)
    for index, target in (
        (Q_BIAS, to_query_bias),
        (V_BIAS, to_value_bias),
        (OUT_BIAS, to_out_bias),
        (GAIN1, to_gain1),
        (SHIFT1, to_shift1),
        (DOWN_BIAS, to_down_bias),
        (GAIN2, to_gain2),
        (SHIFT2, to_shift2),
    ):
        target[...] = turned[index, :width]
    width = to_up_bias.shape[0]
    per = D // width
    turned = pltpu.roll(sums, lax.rem(D - lax.rem(place, per) * width, D), 1)
    line = lax.broadcasted_iota(jnp.int32, sums.shape, 0) == UP_BIAS + place // per
    to_up_bias[...] = jnp.sum(jnp.where(line, turned, 0.0), axis=0)[:width]


def on_device(
    inputs,
    cotangent,
    clip_lengths,
    query_weight,
    query_bias,
    key_weight,
    value_weight,
    value_bias,
    out_weight,
    out_bias,
    first_gain,
    first_shift,
    up_weight,
    up_bias,
    down_weight,
    down_bias,
    second_gain,
    second_shift,
):
    S, R = lax.axis_size("seq"), lax.axis_size("row")
    _, F, D = inputs.shape
    FF = up_weight.shape[1]
    C = S // 2
    N = C // 2
    T, DH, FH, CR, CD = 2 * F, D // 2, FF // 2, D // C, FF // C
    heads = DH // HEAD
    keys = C * T
    wire = BF16 if CR % 32 == 0 else F32
    wire_d = BF16 if CD % 64 == 0 else F32
    vmem = pl.BlockSpec(memory_space=pltpu.VMEM)
    hbm = pl.BlockSpec(memory_space=pl.ANY)
    operands = dict(
        x=(inputs[0], hbm),
        cot_hbm=(cotangent[0], hbm),
        lens_hbm=(clip_lengths, hbm),
        bias_q=(query_bias, hbm),
        bias_v=(value_bias, hbm),
        bias_o=(out_bias, hbm),
        gain1=(first_gain, hbm),
        shift1=(first_shift, hbm),
        bias_d=(down_bias, hbm),
        gain2=(second_gain, hbm),
        shift2=(second_shift, hbm),
        bias_u=(up_bias, hbm),
        wq_hbm=(query_weight, hbm),
        wk_hbm=(key_weight, hbm),
        wv_hbm=(value_weight, hbm),
        wo_hbm=(out_weight, hbm),
        wu_hbm=(up_weight, hbm),
        wd_hbm=(down_weight, hbm),
    )
    results = dict(
        out=((F, D), BF16),
        grad_x=((F, D), F32),
        yd=((R // 2, 2, CD // 4, DH), wire_d),
        ye=((R, 2, CD // 4, DH), wire_d),
        yu=((R, 2, CR // 2, FH // 2), wire),
        ya=((R // 2, 2, 2, CR // 2, DH), wire),
        yb=((R // 2, 2, 2, CR // 2, DH), wire),
        ys=((R, 2, 8, D), F32),
    )
    dma = pltpu.SemaphoreType.DMA
    scratch = dict(
        wq=pltpu.VMEM((D, DH), BF16),
        wkv=pltpu.VMEM((D, D), BF16),
        wo=pltpu.VMEM((D, D), BF16),
        wu=pltpu.VMEM((D, FH), BF16),
        wd=pltpu.VMEM((FH, D), BF16),
        xa=pltpu.VMEM((C, T, D), BF16),
        xt=pltpu.VMEM((D, keys), BF16),
        kva=pltpu.VMEM((keys, D), BF16),
        qm=pltpu.VMEM((heads // 2, 2 * T, 2 * HEAD), BF16),
        dm=pltpu.VMEM((heads // 2, 2 * T, 2 * HEAD), BF16),
        grad_probs=pltpu.VMEM((T, heads * T), F32),
        probs=pltpu.VMEM((T, heads * T), BF16),
        grad_scores=pltpu.VMEM((T, heads * T), BF16),
        cot=pltpu.VMEM((F, D), BF16),
        lens=pltpu.SMEM(clip_lengths.shape, jnp.int32),
        thin0=pltpu.VMEM((D,), BF16),
        thin1=pltpu.VMEM((D,), BF16),
        thin2=pltpu.VMEM((D,), BF16),
        thin3=pltpu.VMEM((D,), BF16),
        thin4=pltpu.VMEM((D,), BF16),
        thin5=pltpu.VMEM((D,), BF16),
        thin6=pltpu.VMEM((D,), BF16),
        thin7=pltpu.VMEM((D,), BF16),
        thin_u=pltpu.VMEM((FF,), BF16),
        out_low=pltpu.VMEM((F, D), BF16),
        dh2=pltpu.VMEM((F, D), F32),
        vec=pltpu.VMEM((8 + FF // D, D), F32),
        top=pltpu.VMEM((heads // 2, 1, 2 * T), F32),
        tot=pltpu.VMEM((heads // 2, 1, 2 * T), F32),
        lse=pltpu.VMEM((heads // 2, 1, 2 * T), F32),
        delta=pltpu.VMEM((heads // 2, 1, 2 * T), F32),
        ot=pltpu.VMEM((DH, T), F32),
        dqt=pltpu.VMEM((DH, T), F32),
        dq=pltpu.VMEM((T, DH), BF16),
        vsum=pltpu.VMEM((1, DH), F32),
        obt=pltpu.VMEM((D, T), BF16),
        n1=pltpu.VMEM((F, D), F32),
        x1=pltpu.VMEM((F, D), F32),
        xb=pltpu.VMEM((T, D), BF16),
        xbt=pltpu.VMEM((D, T), BF16),
        df=pltpu.VMEM((T, D), BF16),
        da=pltpu.VMEM((T, D), BF16),
        act=pltpu.VMEM((T, FH), BF16),
        acto=pltpu.VMEM((2, C // 2, 2, CD // 4, T), BF16),
        atf=pltpu.VMEM((C, 2, CD // 4, T), BF16),
        att=pltpu.VMEM((2, C, CD // 4, T), BF16),
        xbm=pltpu.VMEM((T, D), BF16),
        xmt=pltpu.VMEM((D, T), BF16),
        dfm=pltpu.VMEM((T, DH), BF16),
        dum=pltpu.VMEM((T, FH // 2), BF16),
        slope=pltpu.VMEM((T, FH), F32),
        part=pltpu.VMEM((T, D), F32),
        part_in=pltpu.VMEM((2, F, D), BF16),
        part_out=pltpu.VMEM((2, F, D), BF16),
        gd_sum=pltpu.VMEM((C, CD // 4, DH), BF16),
        gd_in=pltpu.VMEM((2, N, CD // 4, DH), BF16),
        ge_sum=pltpu.VMEM((C, 2, CD // 4, DH), BF16),
        ge_in=pltpu.VMEM((2, N, 2, CD // 4, DH), BF16),
        gu_sum=pltpu.VMEM((C, CR, FH // 2), BF16),
        gu_in=pltpu.VMEM((2, N, CR, FH // 2), BF16),
        ap=pltpu.VMEM((C, 2, 4, CR // 2, DH), BF16),
        am=pltpu.VMEM((C, 4, CR // 2, DH), BF16),
        ga_in=pltpu.VMEM((2, N, 2, CR // 2, DH), BF16),
        gb_in=pltpu.VMEM((2, N, 2, CR // 2, DH), BF16),
        ix_sum=pltpu.VMEM((C, F, D), BF16),
        ix_in=pltpu.VMEM((2, N, F, D), BF16),
        fd=pltpu.VMEM((CD // 4, DH), wire_d),
        fe=pltpu.VMEM((2, CD // 4, DH), wire_d),
        fu=pltpu.VMEM((2, CR // 2, FH // 2), wire),
        fa=pltpu.VMEM((2, CR // 2, DH), wire),
        fb=pltpu.VMEM((2, CR // 2, DH), wire),
        small=pltpu.VMEM((2, 16, D), F32),
        small_ring=pltpu.VMEM((C, 16, DH), BF16),
        fs=pltpu.VMEM((8, D), F32),
        load_sem=dma((18,)),
        g_send=dma((2, PIECES)),
        g_recv=dma((2, N, PIECES)),
        s_send=dma((2,)),
        s_recv=dma((C,)),
        m_send=dma((3,)),
        m_recv=dma((11,)),
        r_send=dma((6, 2)),
        r_recv=dma((6, 2, N)),
        out_sem=dma((8,)),
        y_send=dma((6,)),
        y_recv=dma((6,)),
        ya_send=dma((1,)),
        ya_recv=dma((C,)),
        yq_send=dma((1,)),
        yq_recv=dma((C,)),
        c_send=dma((2,)),
        c_recv=dma((C,)),
        sr_send=dma((2,)),
        sr_recv=dma((2, N)),
        f_send=dma((2 * R - 1,)),
        h_send=dma((3, R)),
        f_recv=dma((6, R, 2)),
    )
    if C <= 8:
        scratch.update(kt=pltpu.VMEM((DH, keys), BF16))
    names = [*operands, *results, *scratch]
    roomy = C <= 8
    found = pl.pallas_call(
        functools.partial(layer_kernel, names, S, R),
        out_shape=[(pltpu.VMEM if roomy else jax.ShapeDtypeStruct)(shape, kind) for shape, kind in results.values()],
        in_specs=[spec for _, spec in operands.values()],
        out_specs=[hbm] * len(results),
        scratch_shapes=list(scratch.values()),
        compiler_params=pltpu.CompilerParams(
            collective_id=0, has_side_effects=True, vmem_limit_bytes=(56 if roomy else 62) * 1024 * 1024
        ),
        name="layer",
    )(*[value for value, _ in operands.values()])
    shapes = [(F, D), (F, D), (D // S, D), (D // S,), (D // S, D), (D // S, D), (D // S,), (D // S, D)]
    shapes += [(D // S,)] * 3 + [(D // S, FF), (FF // S,), (FF // S, D)] + [(D // S,)] * 3
    kinds = [BF16] + [F32] * (len(shapes) - 1)
    if roomy:
        found = [pltpu.with_memory_space_constraint(one, pltpu.VMEM) for one in found]
    final = pl.pallas_call(
        finish_kernel,
        out_shape=[jax.ShapeDtypeStruct(shape, kind) for shape, kind in zip(shapes, kinds, strict=True)],
        in_specs=[vmem] * len(found),
        out_specs=[vmem] * len(shapes),
        name="finish",
    )(*found)
    return (final[0][None], final[1][None], *final[2:])


def solution(mesh):
    shared = P("seq", None)
    part = P("seq")
    return jax.shard_map(
        on_device,
        mesh=mesh,
        in_specs=(P("row", "seq", None), P("row", "seq", None), P("row", None)) + (P(),) * 15,
        out_specs=(
            P("row", "seq", None),
            P("row", "seq", None),
            shared,
            part,
            shared,
            shared,
            part,
            shared,
            part,
            part,
            part,
            shared,
            part,
            shared,
            part,
            part,
            part,
        ),
        check_vma=False,
    )
```

```python
import functools
from types import SimpleNamespace as Refs

import jax
import jax.numpy as jnp
from jax import lax
from jax.experimental import pallas as pl
from jax.experimental.pallas import tpu as pltpu
from jax.sharding import PartitionSpec as P

H = 12
HEAD = 64
PIECES = 4
EPSILON = 1e-05
NEGATIVE = -1e30
MASKED = -2e30
MESH = pl.DeviceIdType.MESH
F32 = jnp.float32
BF16 = jnp.bfloat16


def nn(left, right):
    return lax.dot_general(left, right, (((1,), (0,)), ((), ())), preferred_element_type=F32)


def nt(left, right):
    return lax.dot_general(left, right, (((1,), (1,)), ((), ())), preferred_element_type=F32)


def norm_parts(summed):
    centre = summed - jnp.mean(summed, axis=-1, keepdims=True)
    variance = jnp.mean(centre * centre, axis=-1, keepdims=True)
    scale_inv = lax.rsqrt(variance + EPSILON)
    return (centre * scale_inv, scale_inv)


def norm_back(upstream, normal, scale_inv):
    return scale_inv * (
        upstream
        - jnp.mean(upstream, axis=-1, keepdims=True)
        - normal * jnp.mean(upstream * normal, axis=-1, keepdims=True)
    )


def gelu_parts(hidden):
    cumulative = 0.5 * (1.0 + lax.erf(hidden * 0.7071067811865476))
    density = jnp.exp(-0.5 * hidden * hidden) * 0.3989422804014327
    return hidden * cumulative, cumulative + hidden * density


Q_BIAS, V_BIAS, OUT_BIAS, GAIN1, SHIFT1, DOWN_BIAS, GAIN2, SHIFT2, UP_BIAS = range(9)


def layer_kernel(names, S, R, *refs):
    n = Refs(**dict(zip(names, refs, strict=True)))
    D = n.x.shape[1]
    F = n.x.shape[0]
    FF = n.wd_hbm.shape[0]
    T, DH, FH = 2 * F, D // 2, FF // 2
    C = S // 2
    N = C // 2
    CR = D // C
    CD = FF // C
    pairs = DH // (2 * HEAD)
    heads = DH // HEAD
    TILE = 256
    roomy = C <= 8
    tiles = FH // TILE

    place = lax.axis_index("seq")
    row = lax.axis_index("row")
    core = lax.rem(place, 2)
    chip = place // 2
    pos = jnp.where(lax.rem(chip, 2) == 0, chip // 2, C - 1 - chip // 2)

    def around(steps):
        return lax.rem(pos + (steps + C), C)

    def chip_at(where):
        return jnp.where(where < N, 2 * where, 2 * (C - 1 - where) + 1)

    sibling = (2 * chip + 1 - core, row)
    right = (2 * chip_at(around(1)) + core, row)
    left = (2 * chip_at(around(-1)) + core, row)
    ring = (right, left)
    parity = lax.rem(row, 2)
    mate_row = row + 1 - 2 * parity
    mate = (place, mate_row)
    others = []
    for dr in range(R):
        for dc in range(2):
            if dr or dc:
                others.append((lax.rem(row + dr, R), lax.rem(core + dc, 2)))

    def remote(src, dst, send, recv, device):
        return pltpu.make_async_remote_copy(
            src_ref=src, dst_ref=dst, send_sem=send, recv_sem=recv, device_id=device, device_id_type=MESH
        )

    started = []

    def start(copy):
        copy.start()
        started.append(copy)

    barrier = pltpu.get_barrier_semaphore()
    partners = [right, left] + [(2 * chip + c, r) for r, c in others]
    for device in partners:
        pl.semaphore_signal(barrier, inc=1, device_id=device, device_id_type=MESH)

    xa = n.xa
    own_rows = pl.multiple_of(core * F, F)
    other_rows = pl.multiple_of((1 - core) * F, F)
    half_d = pl.multiple_of(core * DH, 128)
    half_f = pl.multiple_of(core * FH, 128)
    other_f = pl.multiple_of((1 - core) * FH, 128)
    own_slot = 1 if roomy else 0
    loads = []
    for source, target in (
        (n.x, xa.at[pos, pl.ds(own_rows, F)]),
        (n.wq_hbm.at[:, pl.ds(half_d, DH)], n.wq),
        (n.wk_hbm.at[:, pl.ds(half_d, DH)], n.wkv.at[:, pl.ds(0, DH)]),
        (n.wv_hbm.at[:, pl.ds(half_d, DH)], n.wkv.at[:, pl.ds(DH, DH)]),
        (n.lens_hbm, n.lens),
        (n.bias_q, n.thin0),
        (n.bias_v, n.thin1),
        (n.bias_o, n.thin2),
        (n.gain1, n.thin3),
        (n.shift1, n.thin4),
        (n.bias_d, n.thin5),
        (n.gain2, n.thin6),
        (n.shift2, n.thin7),
        (n.bias_u, n.thin_u),
        (n.wo_hbm, n.wo),
        (n.wu_hbm.at[:, pl.ds(other_f, FH)], n.wu.at[0]),
        (n.wd_hbm.at[pl.ds(other_f, FH)], n.wd.at[0]),
        (n.cot_hbm, n.cot),
        (n.wu_hbm.at[:, pl.ds(half_f, FH)], n.wu.at[own_slot]),
        (n.wd_hbm.at[pl.ds(half_f, FH)], n.wd.at[own_slot]),
    ):
        loads.append(pltpu.make_async_copy(source, target, n.load_sem.at[len(loads)]))
        if roomy or len(loads) <= 18:
            loads[-1].start()

    pl.semaphore_wait(barrier, len(partners))

    step_rows = F // PIECES

    def hop_view(where, piece):
        return xa.at[where, pl.ds(pl.multiple_of(own_rows + piece * step_rows, step_rows), step_rows)]

    def hop_send(d, h, turn):
        view = hop_view(around((h - 1) * (2 * d - 1)), lax.rem(turn + d * (PIECES // 2), PIECES))
        return remote(view, view, n.g_send.at[d, turn], n.g_recv.at[d, h - 1, turn], ring[d])

    def hop_first(d, turn):
        first = lax.rem(turn + d * (PIECES // 2), PIECES)
        src = n.x.at[pl.ds(first * step_rows, step_rows)]
        return remote(src, hop_view(pos, first), n.g_send.at[d, turn], n.g_recv.at[d, 0, turn], ring[d])

    def hop_recv(d, h, turn):
        view = hop_view(around(h * (2 * d - 1)), lax.rem(turn + d * (PIECES // 2), PIECES))
        return remote(view, view, n.g_send.at[d, turn], n.g_recv.at[d, h - 1, turn], ring[d])

    def share_send(where, d=0):
        view = xa.at[where, pl.ds(own_rows, F)]
        return remote(view, view, n.s_send.at[d], n.s_recv.at[where], sibling)

    def share_recv(where):
        view = xa.at[where, pl.ds(other_rows, F)]
        return remote(view, view, n.s_send.at[0], n.s_recv.at[where], sibling)

    for turn in range(PIECES):
        hop_first(0, turn).start()
        hop_first(1, turn).start()
        if turn == 0:
            remote(n.x, xa.at[pos, pl.ds(own_rows, F)], n.s_send.at[0], n.s_recv.at[pos], sibling).start()

    def gather_step(h, turn):
        for d in range(2):
            hop_recv(d, h, turn).wait_recv()
            hop_send(d, h, turn).wait_send()

        @pl.when((h < N - 1) | (turn < PIECES // 2))
        def _():
            hop_send(0, h + 1, turn).start()
            hop_send(1, h + 1, turn).start()

        @pl.when(turn == PIECES - 1)
        def _():
            share_send(pos, 0).wait_send()
            pl.when(h > 1)(share_send(pos, 1).wait_send)
            share_send(around(-h), 0).start()
            share_send(around(h), 1).start()

    def gather_last():
        for turn in range(PIECES // 2):
            for d in range(2):
                hop_recv(d, N, turn).wait_recv()
                hop_send(d, N, turn).wait_send()
        share_send(pos, 0).wait_send()
        share_send(around(N), 0).start()

    def gather_sent():
        share_send(pos, 0).wait_send()
        share_send(pos, 1).wait_send()

    for load in loads[:14]:
        load.wait()
    for index, thin in enumerate((n.thin0, n.thin1, n.thin2, n.thin3, n.thin4, n.thin5, n.thin6, n.thin7)):
        n.vec[index : index + 1] = thin[...].astype(F32).reshape(1, D)
    for index in range(FF // D):
        n.vec[UP_BIAS + index : UP_BIAS + index + 1] = (
            n.thin_u[D * index : D * (index + 1)].astype(F32).reshape(1, D)
        )

    ends = []
    total = 0
    for i in range(n.lens.shape[1]):
        total = total + n.lens[0, i]
        ends.append(total)

    def ids(positions, padding):
        counted = jnp.zeros_like(positions)
        for end in ends:
            counted = counted + (positions >= end).astype(jnp.int32)
        return jnp.where(positions < ends[-1], counted, padding)

    query_ids = ids(lax.broadcasted_iota(jnp.int32, (1, T), 1) + chip * T, -1)

    def score_bias(where, first=0, size=None):
        size = T if size is None else size
        key_ids = ids(lax.broadcasted_iota(jnp.int32, (size, 1), 0) + (chip_at(where) * T + first), -2)
        found = jnp.where(key_ids == query_ids, 0.0, MASKED)
        return jnp.concatenate([found, found], axis=1)

    lane = lax.broadcasted_iota(jnp.int32, (T, 2 * HEAD), 1)

    def head_masked(values, target):
        for pair in range(pairs):
            both = values[:, 2 * HEAD * pair : 2 * HEAD * (pair + 1)]
            target[pair, :T] = jnp.where(lane < HEAD, both, 0.0).astype(BF16)
            target[pair, T:] = jnp.where(lane < HEAD, 0.0, both).astype(BF16)

    def of_pair(j):
        return slice(T * (j % 2), T * (j % 2 + 1))

    def of_head(j):
        return slice(HEAD * j, HEAD * (j + 1))

    def key_rows(where):
        return pl.ds(pl.multiple_of(where * T, T), T)

    def forward_block(where, first=0, size=None):
        size = T if size is None else size
        rows = pl.ds(pl.multiple_of(where * T + first, size), size)
        xk = xa[where, pl.ds(first, size)]
        both = nn(xk, n.wkv[...])
        keys = both[:, :DH].astype(BF16)
        scores = [nt(keys[:, 2 * HEAD * p : 2 * HEAD * (p + 1)], n.qm[p]) for p in range(pairs)]
        n.kva[rows, :DH] = keys
        if roomy:
            n.kt[:, rows] = keys.T
        values = (both[:, DH:] + n.vec[V_BIAS : V_BIAS + 1, pl.ds(half_d, DH)]).astype(BF16)
        n.kva[rows, DH:] = values
        values_t = values.T
        n.xt[:, rows] = xk.T
        bias = score_bias(where, first, size)
        weights, factors = [], []
        for p in range(pairs):
            st = scores[p] + bias
            top = n.top[p]
            new_top = jnp.maximum(top, jnp.max(st, axis=0, keepdims=True))
            found = jnp.exp(st - new_top)
            factors.append(jnp.exp(top - new_top))
            n.tot[p] = n.tot[p] * factors[p] + jnp.sum(found, axis=0, keepdims=True)
            n.top[p] = new_top
            weights.append(found.astype(BF16))
        for j in range(heads):
            n.ot[of_head(j)] = n.ot[of_head(j)] * factors[j // 2][:, of_pair(j)] + nn(
                values_t[of_head(j)], weights[j // 2][:, of_pair(j)]
            )

    n.top[...] = jnp.full(n.top.shape, NEGATIVE, F32)
    n.tot[...] = jnp.zeros(n.tot.shape, F32)
    n.ot[...] = jnp.zeros(n.ot.shape, F32)
    small = n.small.at[core]
    small[...] = jnp.zeros(small.shape, F32)

    share_recv(pos).wait_recv()
    queries = (nn(xa[pos], n.wq[...]) + n.vec[Q_BIAS : Q_BIAS + 1, pl.ds(half_d, DH)]).astype(BF16)
    head_masked(queries.astype(F32) * 0.125, n.qm)

    def forward_step(step, carry):
        h, turn = 1 + step // PIECES, lax.rem(step, PIECES)
        gather_step(h, turn)

        @pl.when((step == 0) | ((h > 1) & (turn < 2)))
        def _():
            where = around((h - 1) * (2 * turn - 1))

            @pl.when(step > 0)
            def _():
                share_recv(where).wait_recv()

            forward_block(where)

        return carry

    lax.fori_loop(0, PIECES * (N - 1), forward_step, 0)

    def forward_last(step, carry):
        where = around((N - 1) * (2 * step - 1))

        @pl.when(step == 1)
        def _():
            gather_last()

        share_recv(where).wait_recv()
        forward_block(where)
        return carry

    lax.fori_loop(0, 2, forward_last, 0)

    def forward_half(step, carry):
        @pl.when(step == 1)
        def _():
            share_recv(around(N)).wait_recv()

        forward_block(around(N), pl.multiple_of(own_rows + step * (other_rows - own_rows), F), F)
        return carry

    lax.fori_loop(0, 2, forward_half, 0)

    gather_sent()
    safe = jnp.where(n.tot[...] > 0.5, n.tot[...], 1.0)
    n.lse[...] = n.top[...] + jnp.log(safe)
    for j in range(heads):
        n.ot[of_head(j)] = n.ot[of_head(j)] / safe[j // 2][:, of_pair(j)]

    swaps = []

    def swap(index, src, dst, landed):
        if len(swaps) >= 3:
            sent(swaps[-3])
        send, recv = n.m_send.at[len(swaps) % 3], n.m_recv.at[index]
        start(remote(src, dst, send, recv, sibling))
        swaps.append(started[-1])
        return remote(src, landed, send, recv, sibling)

    def lend(index, src, dst, device, landed, recv_index=None):
        recv_index = index if recv_index is None else recv_index
        start(remote(src, dst, n.y_send.at[index], n.y_recv.at[recv_index], device))
        return remote(src, landed, n.y_send.at[index], n.y_recv.at[index], device)

    def deliver(src, dst, index):
        copy = pltpu.make_async_copy(src, dst, n.out_sem.at[index])
        copy.start()
        delivered.append(copy)

    delivered = []

    def sent(copy):
        started[:] = [other for other in started if other is not copy]
        copy.wait_send()

    obt = n.obt
    own_half = pl.ds(pl.multiple_of(core * DH, DH), DH)
    other_half = pl.ds(pl.multiple_of((1 - core) * DH, DH), DH)
    obt[own_half] = n.ot[...].astype(BF16)
    swapped = swap(0, obt.at[own_half], obt.at[own_half], obt.at[other_half])
    loads[14].wait()
    branch = nn(obt[own_half, pl.ds(own_rows, F)].T, n.wo[own_half])
    swapped.wait_recv()

    def vec(index):
        return n.vec[index : index + 1]

    branch = branch + nn(obt[other_half, pl.ds(own_rows, F)].T, n.wo[other_half]) + vec(OUT_BIAS)
    first_normal, first_scale = norm_parts(xa[pos, pl.ds(own_rows, F)].astype(F32) + branch)
    n.n1[...] = first_normal
    normed = first_normal * vec(GAIN1) + vec(SHIFT1)
    n.x1[...] = normed
    xb = n.xb
    xb[pl.ds(own_rows, F)] = normed.astype(BF16)
    swapped_xb = swap(1, xb.at[pl.ds(own_rows, F)], xb.at[pl.ds(own_rows, F)], xb.at[pl.ds(other_rows, F)])
    xbm = n.xbm
    lent_xb = lend(0, xb.at[pl.ds(own_rows, F)], xbm.at[pl.ds(own_rows, F)], mate, xbm.at[pl.ds(own_rows, F)])
    act, slope = n.act, n.slope
    acto, att = n.acto, n.att
    du = act

    def up_half(i):
        half = 1 - core if i == 0 else core
        rows = slice(F * i, F * (i + 1))
        for t in range(FH // D):
            cols = slice(D * t, D * (t + 1))
            bias = n.vec[pl.ds(UP_BIAS + half * (FH // D) + t, 1)]
            hidden = nn(xb[pl.ds(own_rows, F)], n.wu[own_slot * i, :, cols]) + bias
            value, tangent = gelu_parts(hidden)
            low = value.astype(BF16)
            act[rows, cols] = low
            turned = low.T
            for c in range(D // CD):
                for side in range(2):
                    for q in range(2):
                        first = CD * c + CD // 2 * q + CD // 4 * side
                        acto[side, half * (C // 2) + D // CD * t + c, q] = turned[first : first + CD // 4]
            if i == 0:
                n.slope_out[:, cols] = tangent.astype(BF16)
            else:
                slope[pl.ds(own_rows, F), cols] = tangent

    loads[15].wait()
    if roomy:
        loads[18].wait()
    up_half(0)
    if not roomy:
        loads[18].start()
        loads[18].wait()
    up_half(1)
    own_cols, other_cols = pl.ds(own_rows, F), pl.ds(other_rows, F)
    lent_act = lend(1, acto.at[1, :, 1 - parity], att.at[1, :, :, own_cols], mate, att.at[1, :, :, own_cols])
    swapped_slope = swap(3, n.slope_out, n.slope_in, n.slope_in)
    swapped_first = swap(10, acto.at[0], n.atf.at[:, :, :, own_cols], n.atf.at[:, :, :, other_cols])
    swapped_act = swap(2, acto.at[1, :, parity], att.at[0, :, :, own_cols], att.at[0, :, :, other_cols])
    loads[16].wait()
    loads[17].wait()
    if roomy:
        loads[19].wait()
    part = n.part

    def part_swap():
        n.part_out[...] = part[pl.ds(other_rows, F)].astype(BF16)
        return swap(5, n.part_out, n.part_in, n.part_in)

    fed = nn(act[:F], n.wd[0])
    if not roomy:
        part[:F] = fed
        loads[19].start()
        loads[19].wait()
        fed = part[:F]
    fed = fed + nn(act[F:], n.wd[own_slot])
    upstream = n.cot[...].astype(F32)
    second_normal, second_scale = norm_parts(
        n.x1[...] + fed + vec(DOWN_BIAS)
    )
    n.out_low[...] = (second_normal * vec(GAIN2) + vec(SHIFT2)).astype(BF16)
    residual = norm_back(upstream * vec(GAIN2), second_normal, second_scale)
    n.dh2[...] = residual
    low = residual.astype(BF16)
    df = n.df
    df[pl.ds(own_rows, F)] = low
    swapped = swap(4, df.at[pl.ds(own_rows, F)], df.at[pl.ds(own_rows, F)], df.at[pl.ds(other_rows, F)])
    dfm = n.dfm
    lent_df = []
    for c in range(2):
        start(
            remote(
                df.at[pl.ds(own_rows, F), pl.ds(DH * c, DH)],
                dfm.at[pl.ds(own_rows, F)],
                n.y_send.at[2 + c],
                n.y_recv.at[2 + core],
                (2 * chip + c, mate_row),
            )
        )
        lent_df.append(
            remote(
                df.at[pl.ds(own_rows, F), pl.ds(DH * c, DH)],
                dfm.at[pl.ds(F * c, F)],
                n.y_send.at[2 + c],
                n.y_recv.at[2 + c],
                (2 * chip + c, mate_row),
            )
        )
    small[SHIFT2 : SHIFT2 + 1] = jnp.sum(upstream, axis=0, keepdims=True)
    small[GAIN2 : GAIN2 + 1] = jnp.sum(upstream * second_normal, axis=0, keepdims=True)
    small[DOWN_BIAS : DOWN_BIAS + 1] = jnp.sum(low.astype(F32), axis=0, keepdims=True)
    n.atf[:, :, :, own_cols] = acto[0]
    att[0, :, :, own_cols] = acto[1, :, parity]
    swapped_xb.wait_recv()
    n.xbt[...] = xb[...].T
    swapped_slope.wait_recv()
    slope[pl.ds(other_rows, F)] = n.slope_in[...].astype(F32)
    swapped.wait_recv()

    class Flow:
        def __init__(self, index, chunk, landing, split, ready=None):
            self.index, self.chunk, self.landing, self.split, self.ready = index, chunk, landing, split, ready
            self.last = [None, None]

        def parts(self, d, distance):
            where = around(distance if d == 0 else -distance)
            src, dst = self.chunk(where), self.landing.at[d, distance - 1]
            if distance == N:
                src, dst = src.at[self.split[d]], dst.at[self.split[d]]
            send, recv = n.r_send.at[self.index, d], n.r_recv.at[self.index, d, distance - 1]
            return remote(src, dst, send, recv, ring[d]), dst

        def put(self, d, distance):
            if distance < N:
                self.last[d].wait_send()
            self.last[d] = self.parts(d, distance)[0]
            self.last[d].start()

        def sent(self):
            for copy in self.last:
                copy.wait_send()

        def begin(self):
            if self.ready is not None:
                self.ready(around(N))
            self.put(0, N)
            self.put(1, N)

        def step(self, distance):
            for d in range(2):
                where = around(distance if d == 0 else -distance)
                if self.ready is not None:
                    self.ready(where)
                arriving, landed = self.parts(d, distance + 1)
                arriving.wait_recv()
                target = self.chunk(where)
                if distance + 1 == N:
                    target = target.at[self.split[d]]
                target[...] = (target[...].astype(F32) + landed[...].astype(F32)).astype(BF16)
                self.put(d, distance)

        def end(self):
            if self.ready is not None:
                self.ready(pos)
            found = self.chunk(pos)[...].astype(F32)
            for d in range(2):
                arriving, landed = self.parts(d, 1)
                arriving.wait_recv()
                found = found + landed[...].astype(F32)
            return found

    def add_lent(first, lent, where):
        c = chip_at(where)
        lent(c).wait_recv()
        both = pl.ds(first, 2)
        n.ap[c, parity, both] = (n.ap[c, parity, both].astype(F32) + n.am[c, both].astype(F32)).astype(BF16)

    def lent_query(c):
        return remote(n.ap.at[c, 1 - parity, 0], n.am.at[c, 0], n.yq_send.at[0], n.yq_recv.at[c], mate)

    def lent_pair(c):
        both = pl.ds(2, 2)
        return remote(n.ap.at[c, 1 - parity, both], n.am.at[c, both], n.ya_send.at[0], n.ya_recv.at[c], mate)

    whole = slice(None)
    if CD % 128 == 0:
        split_d = [pl.ds(0, CD // 8), pl.ds(CD // 8, CD // 8)]
    else:
        split_d = [(whole, pl.ds(0, 128)), (whole, pl.ds(128, DH - 128))]
    flow_d = Flow(0, lambda where: n.gd_sum.at[chip_at(where)], n.gd_in, split_d)
    flow_e = Flow(4, lambda where: n.ge_sum.at[chip_at(where)], n.ge_in, [pl.ds(0, 1), pl.ds(1, 1)])
    flow_u = Flow(
        1,
        lambda where: n.gu_sum.at[chip_at(where)],
        n.gu_in,
        [(whole, pl.ds(0, FH // 4)), (whole, pl.ds(FH // 4, FH // 4))],
    )
    flow_a = Flow(
        2,
        lambda where: n.ap.at[chip_at(where), parity, pl.ds(2, 2)],
        n.ga_in,
        [pl.ds(0, 1), pl.ds(1, 1)],
        functools.partial(add_lent, 2, lent_pair),
    )
    flow_b = Flow(
        5,
        lambda where: n.ap.at[chip_at(where), parity, pl.ds(0, 2)],
        n.gb_in,
        [pl.ds(0, 1), pl.ds(1, 1)],
        functools.partial(add_lent, 0, lent_query),
    )
    flow_x = Flow(3, lambda where: n.ix_sum.at[where], n.ix_in, [pl.ds(0, F // 2), pl.ds(F // 2, F // 2)])

    scattered = []

    def scatter(index, source, gathered, split):
        while scattered:
            sent(scattered.pop())
        deliver(source.at[core] if split else source, gathered.at[row, core], 2 + index)
        for k, (r, c) in enumerate(others):
            view = source.at[c] if split else source
            start(
                remote(
                    view, gathered.at[row, core], n.f_send.at[k], n.f_recv.at[index, row, core], (2 * chip + c, r)
                )
            )
            scattered.append(started[-1])

    def collect(index, source, gathered, split):
        for r, c in others:
            view = source.at[c] if split else source
            remote(
                view, gathered.at[r, c], n.f_send.at[0], n.f_recv.at[index, r, c], (2 * chip + c, r)
            ).wait_recv()

    def spread(index, source, gathered):
        pl.when(core == parity)(spread_own(index, source, gathered).start)
        for k in range(R):
            copy = spread_copy(index, source, gathered, k)
            if k == 0:
                pl.when(core != parity)(copy.start)
            else:
                copy.start()

    def spread_own(index, source, gathered):
        return pltpu.make_async_copy(source, gathered.at[row // 2, core], n.out_sem.at[2 + index])

    def spread_copy(index, source, gathered, k):
        device = (2 * chip + parity, lax.rem(row + k, R))
        return remote(
            source, gathered.at[row // 2, core], n.h_send.at[index, k], n.f_recv.at[index, row // 2, core], device
        )

    def spread_done(index, source, gathered):
        for q in range(R // 2):
            for c in range(2):
                arriving = remote(
                    source, gathered.at[q, c], n.h_send.at[index, 0], n.f_recv.at[index, q, c], sibling
                )
                pl.when((2 * q + core != row) | (core != c))(arriving.wait_recv)
        pl.when(core == parity)(spread_own(index, source, gathered).wait)
        for k in range(R):
            copy = spread_copy(index, source, gathered, k)
            if k == 0:
                pl.when(core != parity)(copy.wait_send)
            else:
                copy.wait_send()

    def down_end():
        n.fd[...] = flow_d.end().astype(n.fd.dtype)
        spread(0, n.fd, n.yd)

    def first_end():
        n.fe[...] = flow_e.end().astype(n.fe.dtype)
        scatter(4, n.fe, n.ye, True)

    def up_end():
        found = flow_u.end()
        for c in range(2):
            n.fu[c] = found[CR // 2 * c : CR // 2 * (c + 1)].astype(n.fu.dtype)
        scatter(5, n.fu, n.yu, True)

    def input_step(distance):
        join(around(distance))
        join(around(-distance))
        flow_x.step(distance)

    def input_end():
        join(pos)
        n.dh2[...] = n.x1[...] + flow_x.end()
        deliver(n.dh2, n.grad_x, 1)

    def query_begin():
        lent_out.wait_recv()
        flow_b.begin()

    def attention_end(flow, index, source, gathered):
        source[...] = flow.end().astype(source.dtype)
        spread(index, source, gathered)

    def chain(step, end):
        return [functools.partial(step, distance) for distance in range(N - 1, 0, -1)] + [end]

    chain_d = chain(flow_d.step, down_end)
    chain_u = chain(flow_u.step, up_end)
    chain_e = chain(flow_e.step, first_end)
    chain_x = chain(input_step, input_end)
    chain_a = [flow_a.begin] + chain(flow_a.step, functools.partial(attention_end, flow_a, 2, n.fa, n.ya))
    chain_b = [query_begin] + chain(flow_b.step, functools.partial(attention_end, flow_b, 1, n.fb, n.yb))

    def advance(one):
        one.pop(0)()

    def wide(p, first=0):
        return slice(first + 2 * HEAD * p, first + 2 * HEAD * (p + 1))

    def long(p):
        return slice(2 * T * p, 2 * T * (p + 1))

    def find_probs(where):
        rows, bias = key_rows(where), score_bias(where)
        for p in range(pairs):
            n.slope[:, long(p)] = nt(n.kva[rows, wide(p)], n.qm[p])
        for p in range(pairs):
            probs = jnp.exp(n.slope[:, long(p)] + bias - n.lse[p])
            n.slope[:, long(p)] = probs
            n.probs[:, long(p)] = probs.astype(BF16)

    def backward_block(where, ready):
        rows = key_rows(where)
        bias = None if ready else score_bias(where)
        keys_t = n.kt[:, rows] if roomy else n.kva[rows, :DH].T

        for p in range(pairs):
            if not ready:
                n.slope[:, long(p)] = nt(n.kva[rows, wide(p)], n.qm[p])
            n.grad_probs[:, long(p)] = nt(n.kva[rows, wide(p, DH)], n.dm[p])
        for p in range(pairs):
            if ready:
                probs = n.slope[:, long(p)]
            else:
                probs = jnp.exp(n.slope[:, long(p)] + bias - n.lse[p])
                n.probs[:, long(p)] = probs.astype(BF16)
            n.grad_scores[:, long(p)] = (probs * (n.grad_probs[:, long(p)] - n.delta[p])).astype(BF16)
        for p in range(pairs):
            low = nn(n.probs[:, long(p)], n.dm[p]).astype(BF16)
            n.kva[rows, wide(p, DH)] = low
            n.kva[rows, wide(p)] = nn(n.grad_scores[:, long(p)], n.qm[p]).astype(BF16)
            n.vsum[:, wide(p)] += jnp.sum(low.astype(F32), axis=0, keepdims=True)
        for j in range(heads):
            n.dqt[of_head(j)] += nn(keys_t[of_head(j)], n.grad_scores[:, T * j : T * (j + 1)])
        return nt(n.kva[rows], n.wkv[...])

    swapped_first.wait_recv()
    for t in range(C // 2):
        two = slice(2 * t, 2 * t + 2)
        found = nn(n.atf[two].reshape(CD, T), df[:, pl.ds(half_d, DH)])
        n.ge_sum[two] = found.astype(BF16).reshape(2, 2, CD // 4, DH)
    flow_e.begin()
    for t in range(FH // D):
        cols = slice(D * t, D * (t + 1))
        low = (nt(df[...], n.wd[own_slot, cols, :]) * slope[:, cols]).astype(BF16)
        du[:, cols] = low
        small[pl.ds(UP_BIAS + core * (FH // D) + t, 1)] = jnp.sum(low.astype(F32), axis=0, keepdims=True)

    quarter = pl.multiple_of(parity * (FH // 2), FH // 2)
    other_quarter = pl.multiple_of((1 - parity) * (FH // 2), FH // 2)
    lent_du = lend(4, du.at[:, pl.ds(other_quarter, FH // 2)], n.dum, mate, n.dum)
    part[...] = nt(du[...], n.wu[own_slot])
    part_arrives = part_swap()

    find_probs(around(N))
    part_arrives.wait_recv()
    grad_normed = n.dh2[...] + part[pl.ds(own_rows, F)] + n.part_in[...].astype(F32)
    normal = n.n1[...]
    small[GAIN1 : GAIN1 + 1] = jnp.sum(grad_normed * normal, axis=0, keepdims=True)
    small[SHIFT1 : SHIFT1 + 1] = jnp.sum(grad_normed, axis=0, keepdims=True)
    grad_branch = norm_back(grad_normed * vec(GAIN1), normal, first_scale)
    n.x1[...] = grad_branch
    low = grad_branch.astype(BF16)
    da = n.da
    da[pl.ds(own_rows, F)] = low
    swapped = swap(6, da.at[pl.ds(own_rows, F)], da.at[pl.ds(own_rows, F)], da.at[pl.ds(other_rows, F)])
    small[OUT_BIAS : OUT_BIAS + 1] = jnp.sum(low.astype(F32), axis=0, keepdims=True)
    swapped.wait_recv()

    advance(chain_e)
    grad_mixed = nt(da[...], n.wo[own_half]).astype(BF16).astype(F32)
    head_masked(grad_mixed, n.dm)
    grad_mixed_t = grad_mixed.T
    for j in range(heads):
        n.delta[j // 2, :, of_pair(j)] = jnp.sum(grad_mixed_t[of_head(j)] * n.ot[of_head(j)], axis=0, keepdims=True)

    def grad_down():
        swapped_act.wait_recv()
        swapped_actm.wait_recv()
        rows = CD // 2
        for lent in lent_df:
            lent.wait_recv()
        for t in range(C // 2):
            two = slice(2 * t, 2 * t + 2)
            found = nn(att[0, two].reshape(rows, T), df[:, pl.ds(half_d, DH)])
            found = found + nn(att[1, two].reshape(rows, T), dfm[...])
            n.gd_sum[two] = found.astype(BF16).reshape(2, CD // 4, DH)

    def forward_xb():
        lent_xb.wait_recv()
        return swap(8, xbm.at[pl.ds(own_rows, F)], xbm.at[pl.ds(own_rows, F)], xbm.at[pl.ds(other_rows, F)])

    def grad_up():
        swapped_xbm.wait_recv()
        n.xmt[...] = xbm[...].T
        lent_du.wait_recv()
        for t in range(FH // 2 // TILE):
            cols = slice(TILE * t, TILE * (t + 1))
            found = nn(n.xbt[...], du[:, pl.ds(pl.multiple_of(quarter + t * TILE, TILE), TILE)])
            found = (found + nn(n.xmt[...], n.dum[:, cols])).astype(BF16)
            for c in range(C):
                n.gu_sum[c, :, cols] = found[CR * c : CR * (c + 1)]

    def grad_attention(indices, left, right):
        for t in range(2):
            found = nn(left(pl.ds(DH * t, DH)), right)
            for k, index in enumerate(indices):
                for c in range(DH // CR):
                    for half in range(2):
                        first = CR * c + CR // 2 * half
                        n.ap[DH // CR * t + c, half, index] = found[
                            first : first + CR // 2, DH * k : DH * (k + 1)
                        ].astype(BF16)

    n.dqt[...] = jnp.zeros(n.dqt.shape, F32)
    n.vsum[...] = jnp.zeros(n.vsum.shape, F32)

    crossing, turn_of_cross = [], [0]

    def put_cross(where):
        if len(crossing) == 2:
            crossing.pop(0).wait_send()
        crossing.append(cross(where))
        crossing[-1].start()

    def cross(where):
        send, recv = n.c_send.at[turn_of_cross[0] % 2], n.c_recv.at[where]
        return remote(xa.at[where, pl.ds(0, F)], xa.at[where, pl.ds(F, F)], send, recv, sibling)

    def key_block(where, extra=None, ready=False):
        found = backward_block(where, ready)
        if extra is not None:
            found = found + extra()
        found = found.astype(BF16)
        first, second = found[:F], found[F:]
        xa[where, pl.ds(0, F)] = jnp.where(core == 0, second, first)
        n.ix_sum[where] = jnp.where(core == 0, first, second)

    def join(where):
        cross(where).wait_recv()
        n.ix_sum[where] = (
            n.ix_sum[where].astype(F32) + xa[where, pl.ds(F, F)].astype(F32)
        ).astype(BF16)

    def query_part():
        grad_query = (n.dqt[...] * 0.125).T.astype(BF16)
        n.dq[...] = grad_query
        return nt(grad_query, n.wq[...])

    around_small = n.small_ring
    mine = pl.ds(pl.multiple_of(core * 8, 8), 8)

    def small_send(d, h):
        view = around_small.at[around(1 - h if d == 0 else h - 1)]
        return remote(view, view, n.sr_send.at[d], n.sr_recv.at[d, h - 1], ring[d])

    def small_recv(d, h):
        view = around_small.at[around(-h if d == 0 else h)]
        return remote(view, view, n.sr_send.at[d], n.sr_recv.at[d, h - 1], ring[d])

    small_last = [None, None]

    def small_put(d, h):
        if small_last[d] is not None:
            small_last[d].wait_send()
        small_last[d] = small_send(d, h)
        small_last[d].start()


    def small_step(h):
        small_recv(0, h).wait_recv()
        if h < N:
            small_recv(1, h).wait_recv()
            small_put(0, h + 1)
            if h + 1 < N:
                small_put(1, h + 1)

    def small_end():
        found = around_small[0].astype(F32)
        for where in range(1, C):
            found = found + around_small[where].astype(F32)
        n.fs[:, :DH] = found[:8]
        n.fs[:, DH:] = found[8:]
        scatter(3, n.fs, n.ys, False)

    chain_s = [functools.partial(small_step, h) for h in range(1, N + 1)] + [small_end]
    blocks = [N] + [side * d for d in range(N - 1, 0, -1) for side in (1, -1)] + [0]
    if N == 4:
        due = [""] * 8
        due[0], due[1], due[3], due[4], due[5], due[7] = "mfF", "De", "dx", "UO", "e", "u"
        middle, last = "Sx", "basubasduaebsduabsxdsabx"
    else:
        due = ["mfFD", "e"] + ["ed"[b % 4 // 2] if b % 2 == 0 else "x" for b in range(2, 2 * N)]
        due[4] += "OU"
        middle, last = "S", "ebaxdus" * (N + 2)
    chains = dict(e=chain_e, d=chain_d, u=chain_u, x=chain_x, a=chain_a, b=chain_b, s=chain_s)

    def begin_input():
        join(around(N))
        flow_x.begin()

    def begin_down():
        grad_down()
        flow_d.begin()

    def begin_forward():
        nonlocal swapped_xbm
        swapped_xbm = forward_xb()

    def begin_up():
        grad_up()
        flow_u.begin()

    def begin_out():
        nonlocal lent_out
        grad_attention([1], lambda rows: obt[rows], da[:, pl.ds(half_d, DH)])
        lent_out = lend(5, n.ap.at[:, 1 - parity, 1], n.am.at[:, 1], mate, n.am.at[:, 1])

    def begin_small():
        small_swap.wait_recv()
        both = (n.small[0, mine] + n.small[1, mine]).astype(BF16)
        around_small[pos] = jnp.concatenate([both[:, :DH], both[:, DH:]])
        small_put(0, 1)
        small_put(1, 1)

    def mate_hidden():
        nonlocal swapped_actm
        lent_act.wait_recv()
        swapped_actm = swap(
            9, att.at[1, :, :, own_cols], att.at[1, :, :, own_cols], att.at[1, :, :, other_cols]
        )

    swapped_xbm = lent_out = swapped_actm = small_swap = None
    begins = dict(m=mate_hidden, F=begin_input, D=begin_down, U=begin_up, O=begin_out, S=begin_small, f=begin_forward)

    def work(letters):
        for letter in letters:
            if letter in begins:
                begins[letter]()
            elif chains[letter]:
                chains[letter].pop(0)()

    for index, step in enumerate(blocks):
        key_block(around(step), query_part if step == 0 else None, index == 0)
        turn_of_cross[0] = index
        put_cross(around(step))
        if step == 0:
            small[Q_BIAS : Q_BIAS + 1, pl.ds(half_d, DH)] = jnp.sum(n.dq[...].astype(F32), axis=0, keepdims=True)
            small[V_BIAS : V_BIAS + 1, pl.ds(half_d, DH)] = n.vsum[...]
            small_swap = swap(7, small, small, n.small.at[1 - core])
        work(due[index])
    grad_attention([0], lambda rows: n.xt[rows, key_rows(pos)], n.dq[...])
    ordered = [around(d) for d in [N] + [side * d for d in range(N - 1, 0, -1) for side in (1, -1)] + [0]]
    for where in ordered[:3]:
        lent_query(chip_at(where)).start()
    deliver(n.out_low, n.out, 0)
    work(middle)
    grad_attention([2, 3], lambda rows: n.xt[rows], n.kva[...])
    for k, where in enumerate(ordered):
        if k >= 3:
            lent_query(chip_at(where)).start()
        lent_pair(chip_at(where)).start()

    work(last)
    assert not any(chains.values())
    spread_done(0, n.fd, n.yd)
    collect(5, n.fu, n.yu, True)
    collect(4, n.fe, n.ye, True)
    collect(3, n.fs, n.ys, False)
    spread_done(2, n.fa, n.ya)
    spread_done(1, n.fb, n.yb)
    for copy in started:
        copy.wait_send()
    for copy in delivered:
        copy.wait()
    for flow in (flow_e, flow_d, flow_u, flow_x, flow_a, flow_b):
        flow.sent()
    remote(n.ap.at[:, 1 - parity, 0], n.am.at[:, 0], n.yq_send.at[0], n.yq_recv.at[0], mate).wait_send()
    both = pl.ds(2, 2)
    remote(n.ap.at[:, 1 - parity, both], n.am.at[:, both], n.ya_send.at[0], n.ya_recv.at[0], mate).wait_send()
    for copy in crossing:
        copy.wait_send()
    for copy in small_last:
        if copy is not None:
            copy.wait_send()


def finish_kernel(out, grad_x, yd, ye, yu, ya, yb, ys, *targets):
    (
        to_out,
        to_grad_x,
        to_query,
        to_query_bias,
        to_key,
        to_value,
        to_value_bias,
        to_o,
        to_out_bias,
        to_gain1,
        to_shift1,
        to_up,
        to_up_bias,
        to_down,
        to_down_bias,
        to_gain2,
        to_shift2,
    ) = targets
    R = yu.shape[0]
    D = out.shape[1]
    place = lax.axis_index("seq")

    def over_rows(gathered, *index, first=0, by=1):
        found = gathered[(first, *index)].astype(F32)
        for r in range(first + by, gathered.shape[0], by):
            found = found + gathered[(r, *index)].astype(F32)
        return found

    to_out[...] = out[...]
    to_grad_x[...] = grad_x[...]
    for c in range(2):
        width = yd.shape[-1]
        rows = yd.shape[2]
        to_down[:rows, width * c : width * (c + 1)] = over_rows(ye, c)
        to_down[rows:, width * c : width * (c + 1)] = over_rows(yd, c)
        for gathered, index, target in ((yb, 0, to_query), (yb, 1, to_o), (ya, 0, to_key), (ya, 1, to_value)):
            target[:, width * c : width * (c + 1)] = over_rows(gathered, c, index)
        width = yu.shape[-1]
        for half in range(2):
            first = width * (2 * c + half)
            to_up[:, first : first + width] = over_rows(yu, c, first=half, by=2)
    sums = jnp.concatenate([over_rows(ys, 0), over_rows(ys, 1)])
    width = to_query_bias.shape[0]
    turned = pltpu.roll(sums, lax.rem(D - place * width, D), 1)
    for index, target in (
        (Q_BIAS, to_query_bias),
        (V_BIAS, to_value_bias),
        (OUT_BIAS, to_out_bias),
        (GAIN1, to_gain1),
        (SHIFT1, to_shift1),
        (DOWN_BIAS, to_down_bias),
        (GAIN2, to_gain2),
        (SHIFT2, to_shift2),
    ):
        target[...] = turned[index, :width]
    width = to_up_bias.shape[0]
    per = D // width
    turned = pltpu.roll(sums, lax.rem(D - lax.rem(place, per) * width, D), 1)
    line = lax.broadcasted_iota(jnp.int32, sums.shape, 0) == UP_BIAS + place // per
    to_up_bias[...] = jnp.sum(jnp.where(line, turned, 0.0), axis=0)[:width]


def on_device(
    inputs,
    cotangent,
    clip_lengths,
    query_weight,
    query_bias,
    key_weight,
    value_weight,
    value_bias,
    out_weight,
    out_bias,
    first_gain,
    first_shift,
    up_weight,
    up_bias,
    down_weight,
    down_bias,
    second_gain,
    second_shift,
):
    S, R = lax.axis_size("seq"), lax.axis_size("row")
    _, F, D = inputs.shape
    FF = up_weight.shape[1]
    C = S // 2
    N = C // 2
    T, DH, FH, CR, CD = 2 * F, D // 2, FF // 2, D // C, FF // C
    heads = DH // HEAD
    keys = C * T
    wire = BF16 if CR % 32 == 0 else F32
    wire_d = BF16 if CD % 64 == 0 else F32
    vmem = pl.BlockSpec(memory_space=pltpu.VMEM)
    hbm = pl.BlockSpec(memory_space=pl.ANY)
    operands = dict(
        x=(inputs[0], hbm),
        cot_hbm=(cotangent[0], hbm),
        lens_hbm=(clip_lengths, hbm),
        bias_q=(query_bias, hbm),
        bias_v=(value_bias, hbm),
        bias_o=(out_bias, hbm),
        gain1=(first_gain, hbm),
        shift1=(first_shift, hbm),
        bias_d=(down_bias, hbm),
        gain2=(second_gain, hbm),
        shift2=(second_shift, hbm),
        bias_u=(up_bias, hbm),
        wq_hbm=(query_weight, hbm),
        wk_hbm=(key_weight, hbm),
        wv_hbm=(value_weight, hbm),
        wo_hbm=(out_weight, hbm),
        wu_hbm=(up_weight, hbm),
        wd_hbm=(down_weight, hbm),
    )
    results = dict(
        out=((F, D), BF16),
        grad_x=((F, D), F32),
        yd=((R // 2, 2, CD // 4, DH), wire_d),
        ye=((R, 2, CD // 4, DH), wire_d),
        yu=((R, 2, CR // 2, FH // 2), wire),
        ya=((R // 2, 2, 2, CR // 2, DH), wire),
        yb=((R // 2, 2, 2, CR // 2, DH), wire),
        ys=((R, 2, 8, D), F32),
    )
    roomy = C <= 8
    dma = pltpu.SemaphoreType.DMA
    scratch = dict(
        wq=pltpu.VMEM((D, DH), BF16),
        wkv=pltpu.VMEM((D, D), BF16),
        wo=pltpu.VMEM((D, D), BF16),
        wu=pltpu.VMEM((2 if roomy else 1, D, FH), BF16),
        wd=pltpu.VMEM((2 if roomy else 1, FH, D), BF16),
        xa=pltpu.VMEM((C, T, D), BF16),
        xt=pltpu.VMEM((D, keys), BF16),
        kva=pltpu.VMEM((keys, D), BF16),
        qm=pltpu.VMEM((heads // 2, 2 * T, 2 * HEAD), BF16),
        dm=pltpu.VMEM((heads // 2, 2 * T, 2 * HEAD), BF16),
        grad_probs=pltpu.VMEM((T, heads * T), F32),
        probs=pltpu.VMEM((T, heads * T), BF16),
        grad_scores=pltpu.VMEM((T, heads * T), BF16),
        cot=pltpu.VMEM((F, D), BF16),
        lens=pltpu.SMEM(clip_lengths.shape, jnp.int32),
        thin0=pltpu.VMEM((D,), BF16),
        thin1=pltpu.VMEM((D,), BF16),
        thin2=pltpu.VMEM((D,), BF16),
        thin3=pltpu.VMEM((D,), BF16),
        thin4=pltpu.VMEM((D,), BF16),
        thin5=pltpu.VMEM((D,), BF16),
        thin6=pltpu.VMEM((D,), BF16),
        thin7=pltpu.VMEM((D,), BF16),
        thin_u=pltpu.VMEM((FF,), BF16),
        out_low=pltpu.VMEM((F, D), BF16),
        dh2=pltpu.VMEM((F, D), F32),
        vec=pltpu.VMEM((8 + FF // D, D), F32),
        top=pltpu.VMEM((heads // 2, 1, 2 * T), F32),
        tot=pltpu.VMEM((heads // 2, 1, 2 * T), F32),
        lse=pltpu.VMEM((heads // 2, 1, 2 * T), F32),
        delta=pltpu.VMEM((heads // 2, 1, 2 * T), F32),
        ot=pltpu.VMEM((DH, T), F32),
        dqt=pltpu.VMEM((DH, T), F32),
        dq=pltpu.VMEM((T, DH), BF16),
        vsum=pltpu.VMEM((1, DH), F32),
        obt=pltpu.VMEM((D, T), BF16),
        n1=pltpu.VMEM((F, D), F32),
        x1=pltpu.VMEM((F, D), F32),
        xb=pltpu.VMEM((T, D), BF16),
        xbt=pltpu.VMEM((D, T), BF16),
        df=pltpu.VMEM((T, D), BF16),
        da=pltpu.VMEM((T, D), BF16),
        act=pltpu.VMEM((T, FH), BF16),
        acto=pltpu.VMEM((2, C, 2, CD // 4, F), BF16),
        atf=pltpu.VMEM((C, 2, CD // 4, T), BF16),
        att=pltpu.VMEM((2, C, CD // 4, T), BF16),
        slope_out=pltpu.VMEM((F, FH), BF16),
        slope_in=pltpu.VMEM((F, FH), BF16),
        xbm=pltpu.VMEM((T, D), BF16),
        xmt=pltpu.VMEM((D, T), BF16),
        dfm=pltpu.VMEM((T, DH), BF16),
        dum=pltpu.VMEM((T, FH // 2), BF16),
        slope=pltpu.VMEM((T, FH), F32),
        part=pltpu.VMEM((T, D), F32),
        part_in=pltpu.VMEM((F, D), BF16),
        part_out=pltpu.VMEM((F, D), BF16),
        gd_sum=pltpu.VMEM((C, CD // 4, DH), BF16),
        gd_in=pltpu.VMEM((2, N, CD // 4, DH), BF16),
        ge_sum=pltpu.VMEM((C, 2, CD // 4, DH), BF16),
        ge_in=pltpu.VMEM((2, N, 2, CD // 4, DH), BF16),
        gu_sum=pltpu.VMEM((C, CR, FH // 2), BF16),
        gu_in=pltpu.VMEM((2, N, CR, FH // 2), BF16),
        ap=pltpu.VMEM((C, 2, 4, CR // 2, DH), BF16),
        am=pltpu.VMEM((C, 4, CR // 2, DH), BF16),
        ga_in=pltpu.VMEM((2, N, 2, CR // 2, DH), BF16),
        gb_in=pltpu.VMEM((2, N, 2, CR // 2, DH), BF16),
        ix_sum=pltpu.VMEM((C, F, D), BF16),
        ix_in=pltpu.VMEM((2, N, F, D), BF16),
        fd=pltpu.VMEM((CD // 4, DH), wire_d),
        fe=pltpu.VMEM((2, CD // 4, DH), wire_d),
        fu=pltpu.VMEM((2, CR // 2, FH // 2), wire),
        fa=pltpu.VMEM((2, CR // 2, DH), wire),
        fb=pltpu.VMEM((2, CR // 2, DH), wire),
        small=pltpu.VMEM((2, 16, D), F32),
        small_ring=pltpu.VMEM((C, 16, DH), BF16),
        fs=pltpu.VMEM((8, D), F32),
        load_sem=dma((20,)),
        g_send=dma((2, PIECES)),
        g_recv=dma((2, N, PIECES)),
        s_send=dma((2,)),
        s_recv=dma((C,)),
        m_send=dma((3,)),
        m_recv=dma((11,)),
        r_send=dma((6, 2)),
        r_recv=dma((6, 2, N)),
        out_sem=dma((8,)),
        y_send=dma((6,)),
        y_recv=dma((6,)),
        ya_send=dma((1,)),
        ya_recv=dma((C,)),
        yq_send=dma((1,)),
        yq_recv=dma((C,)),
        c_send=dma((2,)),
        c_recv=dma((C,)),
        sr_send=dma((2,)),
        sr_recv=dma((2, N)),
        f_send=dma((2 * R - 1,)),
        h_send=dma((3, R)),
        f_recv=dma((6, R, 2)),
    )
    if roomy:
        scratch.update(kt=pltpu.VMEM((DH, keys), BF16))
    names = [*operands, *results, *scratch]
    found = pl.pallas_call(
        functools.partial(layer_kernel, names, S, R),
        out_shape=[(pltpu.VMEM if roomy else jax.ShapeDtypeStruct)(shape, kind) for shape, kind in results.values()],
        in_specs=[spec for _, spec in operands.values()],
        out_specs=[hbm] * len(results),
        scratch_shapes=list(scratch.values()),
        compiler_params=pltpu.CompilerParams(
            collective_id=0, has_side_effects=True, vmem_limit_bytes=(56 if roomy else 62) * 1024 * 1024
        ),
        name="layer",
    )(*[value for value, _ in operands.values()])
    shapes = [(F, D), (F, D), (D // S, D), (D // S,), (D // S, D), (D // S, D), (D // S,), (D // S, D)]
    shapes += [(D // S,)] * 3 + [(D // S, FF), (FF // S,), (FF // S, D)] + [(D // S,)] * 3
    kinds = [BF16] + [F32] * (len(shapes) - 1)
    if roomy:
        found = [pltpu.with_memory_space_constraint(one, pltpu.VMEM) for one in found]
    final = pl.pallas_call(
        finish_kernel,
        out_shape=[jax.ShapeDtypeStruct(shape, kind) for shape, kind in zip(shapes, kinds, strict=True)],
        in_specs=[vmem] * len(found),
        out_specs=[vmem] * len(shapes),
        name="finish",
    )(*found)
    return (final[0][None], final[1][None], *final[2:])


def solution(mesh):
    shared = P("seq", None)
    part = P("seq")
    return jax.shard_map(
        on_device,
        mesh=mesh,
        in_specs=(P("row", "seq", None), P("row", "seq", None), P("row", None)) + (P(),) * 15,
        out_specs=(
            P("row", "seq", None),
            P("row", "seq", None),
            shared,
            part,
            shared,
            shared,
            part,
            shared,
            part,
            part,
            part,
            shared,
            part,
            shared,
            part,
            part,
            part,
        ),
        check_vma=False,
    )
```

```python
import functools
from types import SimpleNamespace as Refs

import jax
import jax.numpy as jnp
from jax import lax
from jax.experimental import pallas as pl
from jax.experimental.pallas import tpu as pltpu
from jax.sharding import PartitionSpec as P

H = 12
HEAD = 64
PIECES = 4
EPSILON = 1e-05
NEGATIVE = -1e30
MASKED = -2e30
MESH = pl.DeviceIdType.MESH
F32 = jnp.float32
BF16 = jnp.bfloat16


def nn(left, right):
    return lax.dot_general(left, right, (((1,), (0,)), ((), ())), preferred_element_type=F32)


def nt(left, right):
    return lax.dot_general(left, right, (((1,), (1,)), ((), ())), preferred_element_type=F32)


def norm_parts(summed):
    centre = summed - jnp.mean(summed, axis=-1, keepdims=True)
    variance = jnp.mean(centre * centre, axis=-1, keepdims=True)
    scale_inv = lax.rsqrt(variance + EPSILON)
    return (centre * scale_inv, scale_inv)


def norm_back(upstream, normal, scale_inv):
    return scale_inv * (
        upstream
        - jnp.mean(upstream, axis=-1, keepdims=True)
        - normal * jnp.mean(upstream * normal, axis=-1, keepdims=True)
    )


def gelu_parts(hidden):
    cumulative = 0.5 * (1.0 + lax.erf(hidden * 0.7071067811865476))
    density = jnp.exp(-0.5 * hidden * hidden) * 0.3989422804014327
    return hidden * cumulative, cumulative + hidden * density


Q_BIAS, V_BIAS, OUT_BIAS, GAIN1, SHIFT1, DOWN_BIAS, GAIN2, SHIFT2, UP_BIAS = range(9)


def layer_kernel(names, S, R, *refs):
    n = Refs(**dict(zip(names, refs, strict=True)))
    D = n.x.shape[1]
    F = n.x.shape[0]
    FF = n.wd_hbm.shape[0]
    T, DH, FH = 2 * F, D // 2, FF // 2
    C = S // 2
    N = C // 2
    CR = D // C
    CD = FF // C
    pairs = DH // (2 * HEAD)
    heads = DH // HEAD
    TILE = 256
    roomy = C <= 8
    tiles = FH // TILE

    place = lax.axis_index("seq")
    row = lax.axis_index("row")
    core = lax.rem(place, 2)
    chip = place // 2
    pos = jnp.where(lax.rem(chip, 2) == 0, chip // 2, C - 1 - chip // 2)

    def around(steps):
        return lax.rem(pos + (steps + C), C)

    def chip_at(where):
        return jnp.where(where < N, 2 * where, 2 * (C - 1 - where) + 1)

    sibling = (2 * chip + 1 - core, row)
    right = (2 * chip_at(around(1)) + core, row)
    left = (2 * chip_at(around(-1)) + core, row)
    ring = (right, left)
    parity = lax.rem(row, 2)
    mate_row = row + 1 - 2 * parity
    mate = (place, mate_row)
    others = []
    for dr in range(R):
        for dc in range(2):
            if dr or dc:
                others.append((lax.rem(row + dr, R), lax.rem(core + dc, 2)))

    def remote(src, dst, send, recv, device):
        return pltpu.make_async_remote_copy(
            src_ref=src, dst_ref=dst, send_sem=send, recv_sem=recv, device_id=device, device_id_type=MESH
        )

    started = []

    def start(copy):
        copy.start()
        started.append(copy)

    barrier = pltpu.get_barrier_semaphore()
    partners = [right, left] + [(2 * chip + c, r) for r, c in others]
    for device in partners:
        pl.semaphore_signal(barrier, inc=1, device_id=device, device_id_type=MESH)

    xa = n.xa
    own_rows = pl.multiple_of(core * F, F)
    other_rows = pl.multiple_of((1 - core) * F, F)
    half_d = pl.multiple_of(core * DH, 128)
    half_f = pl.multiple_of(core * FH, 128)
    other_f = pl.multiple_of((1 - core) * FH, 128)
    own_slot = 1 if roomy else 0
    loads = []
    for source, target in (
        (n.x, xa.at[pos, pl.ds(own_rows, F)]),
        (n.wq_hbm.at[:, pl.ds(half_d, DH)], n.wq),
        (n.wk_hbm.at[:, pl.ds(half_d, DH)], n.wkv.at[:, pl.ds(0, DH)]),
        (n.wv_hbm.at[:, pl.ds(half_d, DH)], n.wkv.at[:, pl.ds(DH, DH)]),
        (n.lens_hbm, n.lens),
        (n.bias_q, n.thin0),
        (n.bias_v, n.thin1),
        (n.bias_o, n.thin2),
        (n.gain1, n.thin3),
        (n.shift1, n.thin4),
        (n.bias_d, n.thin5),
        (n.gain2, n.thin6),
        (n.shift2, n.thin7),
        (n.bias_u, n.thin_u),
        (n.wo_hbm, n.wo),
        (n.wu_hbm.at[:, pl.ds(other_f, FH)], n.wu.at[0]),
        (n.wd_hbm.at[pl.ds(other_f, FH)], n.wd.at[0]),
        (n.cot_hbm, n.cot),
        (n.wu_hbm.at[:, pl.ds(half_f, FH)], n.wu.at[own_slot]),
        (n.wd_hbm.at[pl.ds(half_f, FH)], n.wd.at[own_slot]),
    ):
        loads.append(pltpu.make_async_copy(source, target, n.load_sem.at[len(loads)]))
        if roomy or len(loads) <= 18:
            loads[-1].start()

    pl.semaphore_wait(barrier, len(partners))

    step_rows = F // PIECES

    def hop_view(where, piece):
        return xa.at[where, pl.ds(pl.multiple_of(own_rows + piece * step_rows, step_rows), step_rows)]

    def hop_send(d, h, turn):
        view = hop_view(around((h - 1) * (2 * d - 1)), lax.rem(turn + d * (PIECES // 2), PIECES))
        return remote(view, view, n.g_send.at[d, turn], n.g_recv.at[d, h - 1, turn], ring[d])

    def hop_first(d, turn):
        first = lax.rem(turn + d * (PIECES // 2), PIECES)
        src = n.x.at[pl.ds(first * step_rows, step_rows)]
        return remote(src, hop_view(pos, first), n.g_send.at[d, turn], n.g_recv.at[d, 0, turn], ring[d])

    def hop_recv(d, h, turn):
        view = hop_view(around(h * (2 * d - 1)), lax.rem(turn + d * (PIECES // 2), PIECES))
        return remote(view, view, n.g_send.at[d, turn], n.g_recv.at[d, h - 1, turn], ring[d])

    def share_send(where, d=0):
        view = xa.at[where, pl.ds(own_rows, F)]
        return remote(view, view, n.s_send.at[d], n.s_recv.at[where], sibling)

    def share_recv(where):
        view = xa.at[where, pl.ds(other_rows, F)]
        return remote(view, view, n.s_send.at[0], n.s_recv.at[where], sibling)

    for turn in range(PIECES):
        hop_first(0, turn).start()
        hop_first(1, turn).start()
        if turn == 0:
            remote(n.x, xa.at[pos, pl.ds(own_rows, F)], n.s_send.at[0], n.s_recv.at[pos], sibling).start()

    def gather_step(h, turn):
        for d in range(2):
            hop_recv(d, h, turn).wait_recv()
            hop_send(d, h, turn).wait_send()

        @pl.when((h < N - 1) | (turn < PIECES // 2))
        def _():
            hop_send(0, h + 1, turn).start()
            hop_send(1, h + 1, turn).start()

        @pl.when(turn == PIECES - 1)
        def _():
            share_send(pos, 0).wait_send()
            pl.when(h > 1)(share_send(pos, 1).wait_send)
            share_send(around(-h), 0).start()
            share_send(around(h), 1).start()

    def gather_last():
        for turn in range(PIECES // 2):
            for d in range(2):
                hop_recv(d, N, turn).wait_recv()
                hop_send(d, N, turn).wait_send()
        share_send(pos, 0).wait_send()
        share_send(around(N), 0).start()

    def gather_sent():
        share_send(pos, 0).wait_send()
        share_send(pos, 1).wait_send()

    for load in loads[:14]:
        load.wait()
    for index, thin in enumerate((n.thin0, n.thin1, n.thin2, n.thin3, n.thin4, n.thin5, n.thin6, n.thin7)):
        n.vec[index : index + 1] = thin[...].astype(F32).reshape(1, D)
    for index in range(FF // D):
        n.vec[UP_BIAS + index : UP_BIAS + index + 1] = (
            n.thin_u[D * index : D * (index + 1)].astype(F32).reshape(1, D)
        )

    ends = []
    total = 0
    for i in range(n.lens.shape[1]):
        total = total + n.lens[0, i]
        ends.append(total)

    def ids(positions, padding):
        counted = jnp.zeros_like(positions)
        for end in ends:
            counted = counted + (positions >= end).astype(jnp.int32)
        return jnp.where(positions < ends[-1], counted, padding)

    query_ids = ids(lax.broadcasted_iota(jnp.int32, (1, T), 1) + chip * T, -1)

    def score_bias(where, first=0, size=None):
        size = T if size is None else size
        key_ids = ids(lax.broadcasted_iota(jnp.int32, (size, 1), 0) + (chip_at(where) * T + first), -2)
        found = jnp.where(key_ids == query_ids, 0.0, MASKED)
        return jnp.concatenate([found, found], axis=1)

    lane = lax.broadcasted_iota(jnp.int32, (T, 2 * HEAD), 1)

    def head_masked(values, target):
        for pair in range(pairs):
            both = values[:, 2 * HEAD * pair : 2 * HEAD * (pair + 1)]
            target[pair, :T] = jnp.where(lane < HEAD, both, 0.0).astype(BF16)
            target[pair, T:] = jnp.where(lane < HEAD, 0.0, both).astype(BF16)

    def of_pair(j):
        return slice(T * (j % 2), T * (j % 2 + 1))

    def of_head(j):
        return slice(HEAD * j, HEAD * (j + 1))

    def key_rows(where):
        return pl.ds(pl.multiple_of(where * T, T), T)

    def forward_block(where, first=0, size=None):
        size = T if size is None else size
        rows = pl.ds(pl.multiple_of(where * T + first, size), size)
        xk = xa[where, pl.ds(first, size)]
        both = nn(xk, n.wkv[...])
        keys = both[:, :DH].astype(BF16)
        scores = [nt(keys[:, 2 * HEAD * p : 2 * HEAD * (p + 1)], n.qm[p]) for p in range(pairs)]
        n.kva[rows, :DH] = keys
        if roomy:
            n.kt[:, rows] = keys.T
        values = (both[:, DH:] + n.vec[V_BIAS : V_BIAS + 1, pl.ds(half_d, DH)]).astype(BF16)
        n.kva[rows, DH:] = values
        values_t = values.T
        n.xt[:, rows] = xk.T
        bias = score_bias(where, first, size)
        weights, factors = [], []
        for p in range(pairs):
            st = scores[p] + bias
            top = n.top[p]
            new_top = jnp.maximum(top, jnp.max(st, axis=0, keepdims=True))
            found = jnp.exp(st - new_top)
            factors.append(jnp.exp(top - new_top))
            n.tot[p] = n.tot[p] * factors[p] + jnp.sum(found, axis=0, keepdims=True)
            n.top[p] = new_top
            weights.append(found.astype(BF16))
        for j in range(heads):
            n.ot[of_head(j)] = n.ot[of_head(j)] * factors[j // 2][:, of_pair(j)] + nn(
                values_t[of_head(j)], weights[j // 2][:, of_pair(j)]
            )

    n.top[...] = jnp.full(n.top.shape, NEGATIVE, F32)
    n.tot[...] = jnp.zeros(n.tot.shape, F32)
    n.ot[...] = jnp.zeros(n.ot.shape, F32)
    small = n.small.at[core]
    small[...] = jnp.zeros(small.shape, F32)

    share_recv(pos).wait_recv()
    queries = (nn(xa[pos], n.wq[...]) + n.vec[Q_BIAS : Q_BIAS + 1, pl.ds(half_d, DH)]).astype(BF16)
    head_masked(queries.astype(F32) * 0.125, n.qm)

    def forward_step(step, carry):
        h, turn = 1 + step // PIECES, lax.rem(step, PIECES)
        gather_step(h, turn)

        @pl.when((step == 0) | ((h > 1) & (turn < 2)))
        def _():
            where = around((h - 1) * (2 * turn - 1))

            @pl.when(step > 0)
            def _():
                share_recv(where).wait_recv()

            forward_block(where)

        return carry

    lax.fori_loop(0, PIECES * (N - 1), forward_step, 0)

    def forward_last(step, carry):
        where = around((N - 1) * (2 * step - 1))

        @pl.when(step == 1)
        def _():
            gather_last()

        share_recv(where).wait_recv()
        forward_block(where)
        return carry

    lax.fori_loop(0, 2, forward_last, 0)

    def forward_half(step, carry):
        @pl.when(step == 1)
        def _():
            share_recv(around(N)).wait_recv()

        forward_block(around(N), pl.multiple_of(own_rows + step * (other_rows - own_rows), F), F)
        return carry

    lax.fori_loop(0, 2, forward_half, 0)

    gather_sent()
    safe = jnp.where(n.tot[...] > 0.5, n.tot[...], 1.0)
    n.lse[...] = n.top[...] + jnp.log(safe)
    for j in range(heads):
        n.ot[of_head(j)] = n.ot[of_head(j)] / safe[j // 2][:, of_pair(j)]

    swaps = []

    def swap(index, src, dst, landed):
        if len(swaps) >= 3:
            sent(swaps[-3])
        send, recv = n.m_send.at[len(swaps) % 3], n.m_recv.at[index]
        start(remote(src, dst, send, recv, sibling))
        swaps.append(started[-1])
        return remote(src, landed, send, recv, sibling)

    def lend(index, src, dst, device, landed, recv_index=None):
        recv_index = index if recv_index is None else recv_index
        start(remote(src, dst, n.y_send.at[index], n.y_recv.at[recv_index], device))
        return remote(src, landed, n.y_send.at[index], n.y_recv.at[index], device)

    def deliver(src, dst, index):
        copy = pltpu.make_async_copy(src, dst, n.out_sem.at[index])
        copy.start()
        delivered.append(copy)

    delivered = []

    def sent(copy):
        started[:] = [other for other in started if other is not copy]
        copy.wait_send()

    obt = n.obt
    own_half = pl.ds(pl.multiple_of(core * DH, DH), DH)
    other_half = pl.ds(pl.multiple_of((1 - core) * DH, DH), DH)
    obt[own_half] = n.ot[...].astype(BF16)
    swapped = swap(0, obt.at[own_half], obt.at[own_half], obt.at[other_half])
    loads[14].wait()
    branch = nn(obt[own_half, pl.ds(own_rows, F)].T, n.wo[own_half])
    swapped.wait_recv()

    def vec(index):
        return n.vec[index : index + 1]

    branch = branch + nn(obt[other_half, pl.ds(own_rows, F)].T, n.wo[other_half]) + vec(OUT_BIAS)
    first_normal, first_scale = norm_parts(xa[pos, pl.ds(own_rows, F)].astype(F32) + branch)
    n.n1[...] = first_normal
    normed = first_normal * vec(GAIN1) + vec(SHIFT1)
    n.x1[...] = normed
    xb = n.xb
    xb[pl.ds(own_rows, F)] = normed.astype(BF16)
    swapped_xb = swap(1, xb.at[pl.ds(own_rows, F)], xb.at[pl.ds(own_rows, F)], xb.at[pl.ds(other_rows, F)])
    xbm = n.xbm
    lent_xb = lend(0, xb.at[pl.ds(own_rows, F)], xbm.at[pl.ds(own_rows, F)], mate, xbm.at[pl.ds(own_rows, F)])
    act, slope = n.act, n.slope
    acto, att = n.acto, n.att
    du = act

    def up_half(i):
        half = 1 - core if i == 0 else core
        rows = slice(F * i, F * (i + 1))
        for t in range(FH // D):
            cols = slice(D * t, D * (t + 1))
            bias = n.vec[pl.ds(UP_BIAS + half * (FH // D) + t, 1)]
            hidden = nn(xb[pl.ds(own_rows, F)], n.wu[own_slot * i, :, cols]) + bias
            value, tangent = gelu_parts(hidden)
            low = value.astype(BF16)
            act[rows, cols] = low
            turned = low.T
            for c in range(D // CD):
                for side in range(2):
                    for q in range(2):
                        first = CD * c + CD // 2 * q + CD // 4 * side
                        acto[side, half * (C // 2) + D // CD * t + c, q] = turned[first : first + CD // 4]
            if i == 0:
                n.slope_out[:, cols] = tangent.astype(BF16)
            else:
                slope[pl.ds(own_rows, F), cols] = tangent

    loads[15].wait()
    if roomy:
        loads[18].wait()
    up_half(0)
    if not roomy:
        loads[18].start()
        loads[18].wait()
    up_half(1)
    own_cols, other_cols = pl.ds(own_rows, F), pl.ds(other_rows, F)
    lent_act = lend(1, acto.at[1, :, 1 - parity], att.at[1, :, :, own_cols], mate, att.at[1, :, :, own_cols])
    swapped_slope = swap(3, n.slope_out, n.slope_in, n.slope_in)
    swapped_first = swap(10, acto.at[0], n.atf.at[:, :, :, own_cols], n.atf.at[:, :, :, other_cols])
    swapped_act = swap(2, acto.at[1, :, parity], att.at[0, :, :, own_cols], att.at[0, :, :, other_cols])
    loads[16].wait()
    loads[17].wait()
    if roomy:
        loads[19].wait()
    part = n.part

    def part_swap():
        n.part_out[...] = part[pl.ds(other_rows, F)].astype(BF16)
        return swap(5, n.part_out, n.part_in, n.part_in)

    fed = nn(act[:F], n.wd[0])
    if not roomy:
        part[:F] = fed
        loads[19].start()
        loads[19].wait()
        fed = part[:F]
    fed = fed + nn(act[F:], n.wd[own_slot])
    upstream = n.cot[...].astype(F32)
    second_normal, second_scale = norm_parts(
        n.x1[...] + fed + vec(DOWN_BIAS)
    )
    n.out_low[...] = (second_normal * vec(GAIN2) + vec(SHIFT2)).astype(BF16)
    residual = norm_back(upstream * vec(GAIN2), second_normal, second_scale)
    n.dh2[...] = residual
    low = residual.astype(BF16)
    df = n.df
    df[pl.ds(own_rows, F)] = low
    swapped = swap(4, df.at[pl.ds(own_rows, F)], df.at[pl.ds(own_rows, F)], df.at[pl.ds(other_rows, F)])
    dfm = n.dfm
    lent_df = []
    for c in range(2):
        start(
            remote(
                df.at[pl.ds(own_rows, F), pl.ds(DH * c, DH)],
                dfm.at[pl.ds(own_rows, F)],
                n.y_send.at[2 + c],
                n.y_recv.at[2 + core],
                (2 * chip + c, mate_row),
            )
        )
        lent_df.append(
            remote(
                df.at[pl.ds(own_rows, F), pl.ds(DH * c, DH)],
                dfm.at[pl.ds(F * c, F)],
                n.y_send.at[2 + c],
                n.y_recv.at[2 + c],
                (2 * chip + c, mate_row),
            )
        )
    small[SHIFT2 : SHIFT2 + 1] = jnp.sum(upstream, axis=0, keepdims=True)
    small[GAIN2 : GAIN2 + 1] = jnp.sum(upstream * second_normal, axis=0, keepdims=True)
    small[DOWN_BIAS : DOWN_BIAS + 1] = jnp.sum(low.astype(F32), axis=0, keepdims=True)
    n.atf[:, :, :, own_cols] = acto[0]
    att[0, :, :, own_cols] = acto[1, :, parity]
    swapped_xb.wait_recv()
    n.xbt[...] = xb[...].T
    swapped_slope.wait_recv()
    slope[pl.ds(other_rows, F)] = n.slope_in[...].astype(F32)
    swapped.wait_recv()

    class Flow:
        def __init__(self, index, chunk, landing, split, ready=None):
            self.index, self.chunk, self.landing, self.split, self.ready = index, chunk, landing, split, ready
            self.last = [None, None]

        def parts(self, d, distance):
            where = around(distance if d == 0 else -distance)
            src, dst = self.chunk(where), self.landing.at[d, distance - 1]
            if distance == N:
                src, dst = src.at[self.split[d]], dst.at[self.split[d]]
            send, recv = n.r_send.at[self.index, d], n.r_recv.at[self.index, d, distance - 1]
            return remote(src, dst, send, recv, ring[d]), dst

        def put(self, d, distance):
            if distance < N:
                self.last[d].wait_send()
            self.last[d] = self.parts(d, distance)[0]
            self.last[d].start()

        def sent(self):
            for copy in self.last:
                copy.wait_send()

        def begin(self):
            if self.ready is not None:
                self.ready(around(N))
            self.put(0, N)
            self.put(1, N)

        def step(self, distance):
            for d in range(2):
                where = around(distance if d == 0 else -distance)
                if self.ready is not None:
                    self.ready(where)
                arriving, landed = self.parts(d, distance + 1)
                arriving.wait_recv()
                target = self.chunk(where)
                if distance + 1 == N:
                    target = target.at[self.split[d]]
                target[...] = (target[...].astype(F32) + landed[...].astype(F32)).astype(BF16)
                self.put(d, distance)

        def end(self):
            if self.ready is not None:
                self.ready(pos)
            found = self.chunk(pos)[...].astype(F32)
            for d in range(2):
                arriving, landed = self.parts(d, 1)
                arriving.wait_recv()
                found = found + landed[...].astype(F32)
            return found

    def add_lent(first, lent, where):
        c = chip_at(where)
        lent(c).wait_recv()
        both = pl.ds(first, 2)
        n.ap[c, parity, both] = (n.ap[c, parity, both].astype(F32) + n.am[c, both].astype(F32)).astype(BF16)

    def lent_query(c):
        return remote(n.ap.at[c, 1 - parity, 0], n.am.at[c, 0], n.yq_send.at[0], n.yq_recv.at[c], mate)

    def lent_pair(c):
        both = pl.ds(2, 2)
        return remote(n.ap.at[c, 1 - parity, both], n.am.at[c, both], n.ya_send.at[0], n.ya_recv.at[c], mate)

    whole = slice(None)
    if CD % 128 == 0:
        split_d = [pl.ds(0, CD // 8), pl.ds(CD // 8, CD // 8)]
    else:
        split_d = [(whole, pl.ds(0, 128)), (whole, pl.ds(128, DH - 128))]
    flow_d = Flow(0, lambda where: n.gd_sum.at[chip_at(where)], n.gd_in, split_d)
    flow_e = Flow(4, lambda where: n.ge_sum.at[chip_at(where)], n.ge_in, [pl.ds(0, 1), pl.ds(1, 1)])
    flow_u = Flow(
        1,
        lambda where: n.gu_sum.at[chip_at(where)],
        n.gu_in,
        [(whole, pl.ds(0, FH // 4)), (whole, pl.ds(FH // 4, FH // 4))],
    )
    flow_a = Flow(
        2,
        lambda where: n.ap.at[chip_at(where), parity, pl.ds(2, 2)],
        n.ga_in,
        [pl.ds(0, 1), pl.ds(1, 1)],
        functools.partial(add_lent, 2, lent_pair),
    )
    flow_b = Flow(
        5,
        lambda where: n.ap.at[chip_at(where), parity, pl.ds(0, 2)],
        n.gb_in,
        [pl.ds(0, 1), pl.ds(1, 1)],
        functools.partial(add_lent, 0, lent_query),
    )
    flow_x = Flow(3, lambda where: n.ix_sum.at[where], n.ix_in, [pl.ds(0, F // 2), pl.ds(F // 2, F // 2)])

    scattered = []

    def scatter(index, source, gathered, split):
        while scattered:
            sent(scattered.pop())
        deliver(source.at[core] if split else source, gathered.at[row, core], 2 + index)
        for k, (r, c) in enumerate(others):
            view = source.at[c] if split else source
            start(
                remote(
                    view, gathered.at[row, core], n.f_send.at[k], n.f_recv.at[index, row, core], (2 * chip + c, r)
                )
            )
            scattered.append(started[-1])

    def collect(index, source, gathered, split):
        for r, c in others:
            view = source.at[c] if split else source
            remote(
                view, gathered.at[r, c], n.f_send.at[0], n.f_recv.at[index, r, c], (2 * chip + c, r)
            ).wait_recv()

    def spread(index, source, gathered):
        pl.when(core == parity)(spread_own(index, source, gathered).start)
        for k in range(R):
            copy = spread_copy(index, source, gathered, k)
            if k == 0:
                pl.when(core != parity)(copy.start)
            else:
                copy.start()

    def spread_own(index, source, gathered):
        return pltpu.make_async_copy(source, gathered.at[row // 2, core], n.out_sem.at[2 + index])

    def spread_copy(index, source, gathered, k):
        device = (2 * chip + parity, lax.rem(row + k, R))
        return remote(
            source, gathered.at[row // 2, core], n.h_send.at[index, k], n.f_recv.at[index, row // 2, core], device
        )

    def spread_done(index, source, gathered):
        for q in range(R // 2):
            for c in range(2):
                arriving = remote(
                    source, gathered.at[q, c], n.h_send.at[index, 0], n.f_recv.at[index, q, c], sibling
                )
                pl.when((2 * q + core != row) | (core != c))(arriving.wait_recv)
        pl.when(core == parity)(spread_own(index, source, gathered).wait)
        for k in range(R):
            copy = spread_copy(index, source, gathered, k)
            if k == 0:
                pl.when(core != parity)(copy.wait_send)
            else:
                copy.wait_send()

    def down_end():
        n.fd[...] = flow_d.end().astype(n.fd.dtype)
        spread(0, n.fd, n.yd)

    def first_end():
        n.fe[...] = flow_e.end().astype(n.fe.dtype)
        scatter(4, n.fe, n.ye, True)

    def up_end():
        found = flow_u.end()
        for c in range(2):
            n.fu[c] = found[CR // 2 * c : CR // 2 * (c + 1)].astype(n.fu.dtype)
        scatter(5, n.fu, n.yu, True)

    def input_step(distance):
        join(around(distance))
        join(around(-distance))
        flow_x.step(distance)

    def input_end():
        join(pos)
        n.dh2[...] = n.x1[...] + flow_x.end()
        deliver(n.dh2, n.grad_x, 1)

    def query_begin():
        lent_out.wait_recv()
        flow_b.begin()

    def attention_end(flow, index, source, gathered):
        source[...] = flow.end().astype(source.dtype)
        spread(index, source, gathered)

    def chain(step, end):
        return [functools.partial(step, distance) for distance in range(N - 1, 0, -1)] + [end]

    chain_d = chain(flow_d.step, down_end)
    chain_u = chain(flow_u.step, up_end)
    chain_e = chain(flow_e.step, first_end)
    chain_x = chain(input_step, input_end)
    chain_a = [flow_a.begin] + chain(flow_a.step, functools.partial(attention_end, flow_a, 2, n.fa, n.ya))
    chain_b = [query_begin] + chain(flow_b.step, functools.partial(attention_end, flow_b, 1, n.fb, n.yb))

    def advance(one):
        one.pop(0)()

    def wide(p, first=0):
        return slice(first + 2 * HEAD * p, first + 2 * HEAD * (p + 1))

    def long(p):
        return slice(2 * T * p, 2 * T * (p + 1))

    def find_probs(where):
        rows, bias = key_rows(where), score_bias(where)
        for p in range(pairs):
            n.slope[:, long(p)] = nt(n.kva[rows, wide(p)], n.qm[p])
        for p in range(pairs):
            probs = jnp.exp(n.slope[:, long(p)] + bias - n.lse[p])
            n.slope[:, long(p)] = probs
            n.probs[:, long(p)] = probs.astype(BF16)

    def backward_block(where, ready):
        rows = key_rows(where)
        bias = None if ready else score_bias(where)
        keys_t = n.kt[:, rows] if roomy else n.kva[rows, :DH].T

        for p in range(pairs):
            if not ready:
                n.slope[:, long(p)] = nt(n.kva[rows, wide(p)], n.qm[p])
            n.grad_probs[:, long(p)] = nt(n.kva[rows, wide(p, DH)], n.dm[p])
        for p in range(pairs):
            if ready:
                probs = n.slope[:, long(p)]
            else:
                probs = jnp.exp(n.slope[:, long(p)] + bias - n.lse[p])
                n.probs[:, long(p)] = probs.astype(BF16)
            n.grad_scores[:, long(p)] = (probs * (n.grad_probs[:, long(p)] - n.delta[p])).astype(BF16)
        for p in range(pairs):
            low = nn(n.probs[:, long(p)], n.dm[p]).astype(BF16)
            n.kva[rows, wide(p, DH)] = low
            n.kva[rows, wide(p)] = nn(n.grad_scores[:, long(p)], n.qm[p]).astype(BF16)
            n.vsum[:, wide(p)] += jnp.sum(low.astype(F32), axis=0, keepdims=True)
        for j in range(heads):
            n.dqt[of_head(j)] += nn(keys_t[of_head(j)], n.grad_scores[:, T * j : T * (j + 1)])
        return nt(n.kva[rows], n.wkv[...])

    swapped_first.wait_recv()
    for t in range(C // 2):
        two = slice(2 * t, 2 * t + 2)
        found = nn(n.atf[two].reshape(CD, T), df[:, pl.ds(half_d, DH)])
        n.ge_sum[two] = found.astype(BF16).reshape(2, 2, CD // 4, DH)
    flow_e.begin()
    for t in range(FH // D):
        cols = slice(D * t, D * (t + 1))
        low = (nt(df[...], n.wd[own_slot, cols, :]) * slope[:, cols]).astype(BF16)
        du[:, cols] = low
        small[pl.ds(UP_BIAS + core * (FH // D) + t, 1)] = jnp.sum(low.astype(F32), axis=0, keepdims=True)

    quarter = pl.multiple_of(parity * (FH // 2), FH // 2)
    other_quarter = pl.multiple_of((1 - parity) * (FH // 2), FH // 2)
    lent_du = lend(4, du.at[:, pl.ds(other_quarter, FH // 2)], n.dum, mate, n.dum)
    part[...] = nt(du[...], n.wu[own_slot])
    part_arrives = part_swap()

    find_probs(around(N))
    part_arrives.wait_recv()
    grad_normed = n.dh2[...] + part[pl.ds(own_rows, F)] + n.part_in[...].astype(F32)
    normal = n.n1[...]
    small[GAIN1 : GAIN1 + 1] = jnp.sum(grad_normed * normal, axis=0, keepdims=True)
    small[SHIFT1 : SHIFT1 + 1] = jnp.sum(grad_normed, axis=0, keepdims=True)
    grad_branch = norm_back(grad_normed * vec(GAIN1), normal, first_scale)
    n.x1[...] = grad_branch
    low = grad_branch.astype(BF16)
    da = n.da
    da[pl.ds(own_rows, F)] = low
    swapped = swap(6, da.at[pl.ds(own_rows, F)], da.at[pl.ds(own_rows, F)], da.at[pl.ds(other_rows, F)])
    small[OUT_BIAS : OUT_BIAS + 1] = jnp.sum(low.astype(F32), axis=0, keepdims=True)
    swapped.wait_recv()

    advance(chain_e)
    grad_mixed = nt(da[...], n.wo[own_half]).astype(BF16).astype(F32)
    head_masked(grad_mixed, n.dm)
    grad_mixed_t = grad_mixed.T
    for j in range(heads):
        n.delta[j // 2, :, of_pair(j)] = jnp.sum(grad_mixed_t[of_head(j)] * n.ot[of_head(j)], axis=0, keepdims=True)

    def grad_down():
        swapped_act.wait_recv()
        swapped_actm.wait_recv()
        rows = CD // 2
        for lent in lent_df:
            lent.wait_recv()
        for t in range(C // 2):
            two = slice(2 * t, 2 * t + 2)
            found = nn(att[0, two].reshape(rows, T), df[:, pl.ds(half_d, DH)])
            found = found + nn(att[1, two].reshape(rows, T), dfm[...])
            n.gd_sum[two] = found.astype(BF16).reshape(2, CD // 4, DH)

    def forward_xb():
        lent_xb.wait_recv()
        return swap(8, xbm.at[pl.ds(own_rows, F)], xbm.at[pl.ds(own_rows, F)], xbm.at[pl.ds(other_rows, F)])

    def grad_up():
        swapped_xbm.wait_recv()
        n.xmt[...] = xbm[...].T
        lent_du.wait_recv()
        for t in range(FH // 2 // TILE):
            cols = slice(TILE * t, TILE * (t + 1))
            found = nn(n.xbt[...], du[:, pl.ds(pl.multiple_of(quarter + t * TILE, TILE), TILE)])
            found = (found + nn(n.xmt[...], n.dum[:, cols])).astype(BF16)
            for c in range(C):
                n.gu_sum[c, :, cols] = found[CR * c : CR * (c + 1)]

    def grad_attention(indices, left, right):
        for t in range(2):
            found = nn(left(pl.ds(DH * t, DH)), right)
            for k, index in enumerate(indices):
                for c in range(DH // CR):
                    for half in range(2):
                        first = CR * c + CR // 2 * half
                        n.ap[DH // CR * t + c, half, index] = found[
                            first : first + CR // 2, DH * k : DH * (k + 1)
                        ].astype(BF16)

    n.dqt[...] = jnp.zeros(n.dqt.shape, F32)
    n.vsum[...] = jnp.zeros(n.vsum.shape, F32)

    crossing, turn_of_cross = [], [0]

    def put_cross(where):
        if len(crossing) == 2:
            crossing.pop(0).wait_send()
        crossing.append(cross(where))
        crossing[-1].start()

    def cross(where):
        send, recv = n.c_send.at[turn_of_cross[0] % 2], n.c_recv.at[where]
        return remote(xa.at[where, pl.ds(0, F)], xa.at[where, pl.ds(F, F)], send, recv, sibling)

    def key_block(where, extra=None, ready=False):
        found = backward_block(where, ready)
        if extra is not None:
            found = found + extra()
        found = found.astype(BF16)
        first, second = found[:F], found[F:]
        xa[where, pl.ds(0, F)] = jnp.where(core == 0, second, first)
        n.ix_sum[where] = jnp.where(core == 0, first, second)

    def join(where):
        cross(where).wait_recv()
        n.ix_sum[where] = (
            n.ix_sum[where].astype(F32) + xa[where, pl.ds(F, F)].astype(F32)
        ).astype(BF16)

    def query_part():
        grad_query = (n.dqt[...] * 0.125).T.astype(BF16)
        n.dq[...] = grad_query
        return nt(grad_query, n.wq[...])

    around_small = n.small_ring
    mine = pl.ds(pl.multiple_of(core * 8, 8), 8)

    def small_send(d, h):
        view = around_small.at[around(1 - h if d == 0 else h - 1)]
        return remote(view, view, n.sr_send.at[d], n.sr_recv.at[d, h - 1], ring[d])

    def small_recv(d, h):
        view = around_small.at[around(-h if d == 0 else h)]
        return remote(view, view, n.sr_send.at[d], n.sr_recv.at[d, h - 1], ring[d])

    small_last = [None, None]

    def small_put(d, h):
        if small_last[d] is not None:
            small_last[d].wait_send()
        small_last[d] = small_send(d, h)
        small_last[d].start()


    def small_step(h):
        small_recv(0, h).wait_recv()
        if h < N:
            small_recv(1, h).wait_recv()
            small_put(0, h + 1)
            if h + 1 < N:
                small_put(1, h + 1)

    def small_end():
        found = around_small[0].astype(F32)
        for where in range(1, C):
            found = found + around_small[where].astype(F32)
        n.fs[:, :DH] = found[:8]
        n.fs[:, DH:] = found[8:]
        scatter(3, n.fs, n.ys, False)

    chain_s = [functools.partial(small_step, h) for h in range(1, N + 1)] + [small_end]
    blocks = [N] + [side * d for d in range(N - 1, 0, -1) for side in (1, -1)] + [0]
    if N == 4:
        due = [""] * 8
        due[0], due[1], due[3], due[4], due[5], due[7] = "mfF", "De", "xd", "UO", "e", "u"
        middle, last = "Sx", "basubasduaebsduabsxdsabx"
    else:
        due = ["mfFD", "e"] + ["ed"[b % 4 // 2] if b % 2 == 0 else "x" for b in range(2, 2 * N)]
        due[4] += "OU"
        middle, last = "S", "ebaxdus" * (N + 2)
    chains = dict(e=chain_e, d=chain_d, u=chain_u, x=chain_x, a=chain_a, b=chain_b, s=chain_s)

    def begin_input():
        join(around(N))
        flow_x.begin()

    def begin_down():
        grad_down()
        flow_d.begin()

    def begin_forward():
        nonlocal swapped_xbm
        swapped_xbm = forward_xb()

    def begin_up():
        grad_up()
        flow_u.begin()

    def begin_out():
        nonlocal lent_out
        grad_attention([1], lambda rows: obt[rows], da[:, pl.ds(half_d, DH)])
        lent_out = lend(5, n.ap.at[:, 1 - parity, 1], n.am.at[:, 1], mate, n.am.at[:, 1])

    def begin_small():
        small_swap.wait_recv()
        both = (n.small[0, mine] + n.small[1, mine]).astype(BF16)
        around_small[pos] = jnp.concatenate([both[:, :DH], both[:, DH:]])
        small_put(0, 1)
        small_put(1, 1)

    def mate_hidden():
        nonlocal swapped_actm
        lent_act.wait_recv()
        swapped_actm = swap(
            9, att.at[1, :, :, own_cols], att.at[1, :, :, own_cols], att.at[1, :, :, other_cols]
        )

    swapped_xbm = lent_out = swapped_actm = small_swap = None
    begins = dict(m=mate_hidden, F=begin_input, D=begin_down, U=begin_up, O=begin_out, S=begin_small, f=begin_forward)

    def work(letters):
        for letter in letters:
            if letter in begins:
                begins[letter]()
            elif chains[letter]:
                chains[letter].pop(0)()

    for index, step in enumerate(blocks):
        key_block(around(step), query_part if step == 0 else None, index == 0)
        turn_of_cross[0] = index
        put_cross(around(step))
        if step == 0:
            small[Q_BIAS : Q_BIAS + 1, pl.ds(half_d, DH)] = jnp.sum(n.dq[...].astype(F32), axis=0, keepdims=True)
            small[V_BIAS : V_BIAS + 1, pl.ds(half_d, DH)] = n.vsum[...]
            small_swap = swap(7, small, small, n.small.at[1 - core])
        work(due[index])
    grad_attention([0], lambda rows: n.xt[rows, key_rows(pos)], n.dq[...])
    ordered = [around(d) for d in [N] + [side * d for d in range(N - 1, 0, -1) for side in (1, -1)] + [0]]
    for where in ordered[:3]:
        lent_query(chip_at(where)).start()
    deliver(n.out_low, n.out, 0)
    work(middle)
    grad_attention([2, 3], lambda rows: n.xt[rows], n.kva[...])
    for k, where in enumerate(ordered):
        if k >= 3:
            lent_query(chip_at(where)).start()
        lent_pair(chip_at(where)).start()

    work(last)
    assert not any(chains.values())
    spread_done(0, n.fd, n.yd)
    collect(5, n.fu, n.yu, True)
    collect(4, n.fe, n.ye, True)
    collect(3, n.fs, n.ys, False)
    spread_done(2, n.fa, n.ya)
    spread_done(1, n.fb, n.yb)
    for copy in started:
        copy.wait_send()
    for copy in delivered:
        copy.wait()
    for flow in (flow_e, flow_d, flow_u, flow_x, flow_a, flow_b):
        flow.sent()
    remote(n.ap.at[:, 1 - parity, 0], n.am.at[:, 0], n.yq_send.at[0], n.yq_recv.at[0], mate).wait_send()
    both = pl.ds(2, 2)
    remote(n.ap.at[:, 1 - parity, both], n.am.at[:, both], n.ya_send.at[0], n.ya_recv.at[0], mate).wait_send()
    for copy in crossing:
        copy.wait_send()
    for copy in small_last:
        if copy is not None:
            copy.wait_send()


def finish_kernel(out, grad_x, yd, ye, yu, ya, yb, ys, *targets):
    (
        to_out,
        to_grad_x,
        to_query,
        to_query_bias,
        to_key,
        to_value,
        to_value_bias,
        to_o,
        to_out_bias,
        to_gain1,
        to_shift1,
        to_up,
        to_up_bias,
        to_down,
        to_down_bias,
        to_gain2,
        to_shift2,
    ) = targets
    R = yu.shape[0]
    D = out.shape[1]
    place = lax.axis_index("seq")

    def over_rows(gathered, *index, first=0, by=1):
        found = gathered[(first, *index)].astype(F32)
        for r in range(first + by, gathered.shape[0], by):
            found = found + gathered[(r, *index)].astype(F32)
        return found

    to_out[...] = out[...]
    to_grad_x[...] = grad_x[...]
    for c in range(2):
        width = yd.shape[-1]
        rows = yd.shape[2]
        to_down[:rows, width * c : width * (c + 1)] = over_rows(ye, c)
        to_down[rows:, width * c : width * (c + 1)] = over_rows(yd, c)
        for gathered, index, target in ((yb, 0, to_query), (yb, 1, to_o), (ya, 0, to_key), (ya, 1, to_value)):
            target[:, width * c : width * (c + 1)] = over_rows(gathered, c, index)
        width = yu.shape[-1]
        for half in range(2):
            first = width * (2 * c + half)
            to_up[:, first : first + width] = over_rows(yu, c, first=half, by=2)
    sums = jnp.concatenate([over_rows(ys, 0), over_rows(ys, 1)])
    width = to_query_bias.shape[0]
    turned = pltpu.roll(sums, lax.rem(D - place * width, D), 1)
    for index, target in (
        (Q_BIAS, to_query_bias),
        (V_BIAS, to_value_bias),
        (OUT_BIAS, to_out_bias),
        (GAIN1, to_gain1),
        (SHIFT1, to_shift1),
        (DOWN_BIAS, to_down_bias),
        (GAIN2, to_gain2),
        (SHIFT2, to_shift2),
    ):
        target[...] = turned[index, :width]
    width = to_up_bias.shape[0]
    per = D // width
    turned = pltpu.roll(sums, lax.rem(D - lax.rem(place, per) * width, D), 1)
    line = lax.broadcasted_iota(jnp.int32, sums.shape, 0) == UP_BIAS + place // per
    to_up_bias[...] = jnp.sum(jnp.where(line, turned, 0.0), axis=0)[:width]


def on_device(
    inputs,
    cotangent,
    clip_lengths,
    query_weight,
    query_bias,
    key_weight,
    value_weight,
    value_bias,
    out_weight,
    out_bias,
    first_gain,
    first_shift,
    up_weight,
    up_bias,
    down_weight,
    down_bias,
    second_gain,
    second_shift,
):
    S, R = lax.axis_size("seq"), lax.axis_size("row")
    _, F, D = inputs.shape
    FF = up_weight.shape[1]
    C = S // 2
    N = C // 2
    T, DH, FH, CR, CD = 2 * F, D // 2, FF // 2, D // C, FF // C
    heads = DH // HEAD
    keys = C * T
    wire = BF16 if CR % 32 == 0 else F32
    wire_d = BF16 if CD % 64 == 0 else F32
    vmem = pl.BlockSpec(memory_space=pltpu.VMEM)
    hbm = pl.BlockSpec(memory_space=pl.ANY)
    operands = dict(
        x=(inputs[0], hbm),
        cot_hbm=(cotangent[0], hbm),
        lens_hbm=(clip_lengths, hbm),
        bias_q=(query_bias, hbm),
        bias_v=(value_bias, hbm),
        bias_o=(out_bias, hbm),
        gain1=(first_gain, hbm),
        shift1=(first_shift, hbm),
        bias_d=(down_bias, hbm),
        gain2=(second_gain, hbm),
        shift2=(second_shift, hbm),
        bias_u=(up_bias, hbm),
        wq_hbm=(query_weight, hbm),
        wk_hbm=(key_weight, hbm),
        wv_hbm=(value_weight, hbm),
        wo_hbm=(out_weight, hbm),
        wu_hbm=(up_weight, hbm),
        wd_hbm=(down_weight, hbm),
    )
    results = dict(
        out=((F, D), BF16),
        grad_x=((F, D), F32),
        yd=((R // 2, 2, CD // 4, DH), wire_d),
        ye=((R, 2, CD // 4, DH), wire_d),
        yu=((R, 2, CR // 2, FH // 2), wire),
        ya=((R // 2, 2, 2, CR // 2, DH), wire),
        yb=((R // 2, 2, 2, CR // 2, DH), wire),
        ys=((R, 2, 8, D), F32),
    )
    roomy = C <= 8
    dma = pltpu.SemaphoreType.DMA
    scratch = dict(
        wq=pltpu.VMEM((D, DH), BF16),
        wkv=pltpu.VMEM((D, D), BF16),
        wo=pltpu.VMEM((D, D), BF16),
        wu=pltpu.VMEM((2 if roomy else 1, D, FH), BF16),
        wd=pltpu.VMEM((2 if roomy else 1, FH, D), BF16),
        xa=pltpu.VMEM((C, T, D), BF16),
        xt=pltpu.VMEM((D, keys), BF16),
        kva=pltpu.VMEM((keys, D), BF16),
        qm=pltpu.VMEM((heads // 2, 2 * T, 2 * HEAD), BF16),
        dm=pltpu.VMEM((heads // 2, 2 * T, 2 * HEAD), BF16),
        grad_probs=pltpu.VMEM((T, heads * T), F32),
        probs=pltpu.VMEM((T, heads * T), BF16),
        grad_scores=pltpu.VMEM((T, heads * T), BF16),
        cot=pltpu.VMEM((F, D), BF16),
        lens=pltpu.SMEM(clip_lengths.shape, jnp.int32),
        thin0=pltpu.VMEM((D,), BF16),
        thin1=pltpu.VMEM((D,), BF16),
        thin2=pltpu.VMEM((D,), BF16),
        thin3=pltpu.VMEM((D,), BF16),
        thin4=pltpu.VMEM((D,), BF16),
        thin5=pltpu.VMEM((D,), BF16),
        thin6=pltpu.VMEM((D,), BF16),
        thin7=pltpu.VMEM((D,), BF16),
        thin_u=pltpu.VMEM((FF,), BF16),
        out_low=pltpu.VMEM((F, D), BF16),
        dh2=pltpu.VMEM((F, D), F32),
        vec=pltpu.VMEM((8 + FF // D, D), F32),
        top=pltpu.VMEM((heads // 2, 1, 2 * T), F32),
        tot=pltpu.VMEM((heads // 2, 1, 2 * T), F32),
        lse=pltpu.VMEM((heads // 2, 1, 2 * T), F32),
        delta=pltpu.VMEM((heads // 2, 1, 2 * T), F32),
        ot=pltpu.VMEM((DH, T), F32),
        dqt=pltpu.VMEM((DH, T), F32),
        dq=pltpu.VMEM((T, DH), BF16),
        vsum=pltpu.VMEM((1, DH), F32),
        obt=pltpu.VMEM((D, T), BF16),
        n1=pltpu.VMEM((F, D), F32),
        x1=pltpu.VMEM((F, D), F32),
        xb=pltpu.VMEM((T, D), BF16),
        xbt=pltpu.VMEM((D, T), BF16),
        df=pltpu.VMEM((T, D), BF16),
        da=pltpu.VMEM((T, D), BF16),
        act=pltpu.VMEM((T, FH), BF16),
        acto=pltpu.VMEM((2, C, 2, CD // 4, F), BF16),
        atf=pltpu.VMEM((C, 2, CD // 4, T), BF16),
        att=pltpu.VMEM((2, C, CD // 4, T), BF16),
        slope_out=pltpu.VMEM((F, FH), BF16),
        slope_in=pltpu.VMEM((F, FH), BF16),
        xbm=pltpu.VMEM((T, D), BF16),
        xmt=pltpu.VMEM((D, T), BF16),
        dfm=pltpu.VMEM((T, DH), BF16),
        dum=pltpu.VMEM((T, FH // 2), BF16),
        slope=pltpu.VMEM((T, FH), F32),
        part=pltpu.VMEM((T, D), F32),
        part_in=pltpu.VMEM((F, D), BF16),
        part_out=pltpu.VMEM((F, D), BF16),
        gd_sum=pltpu.VMEM((C, CD // 4, DH), BF16),
        gd_in=pltpu.VMEM((2, N, CD // 4, DH), BF16),
        ge_sum=pltpu.VMEM((C, 2, CD // 4, DH), BF16),
        ge_in=pltpu.VMEM((2, N, 2, CD // 4, DH), BF16),
        gu_sum=pltpu.VMEM((C, CR, FH // 2), BF16),
        gu_in=pltpu.VMEM((2, N, CR, FH // 2), BF16),
        ap=pltpu.VMEM((C, 2, 4, CR // 2, DH), BF16),
        am=pltpu.VMEM((C, 4, CR // 2, DH), BF16),
        ga_in=pltpu.VMEM((2, N, 2, CR // 2, DH), BF16),
        gb_in=pltpu.VMEM((2, N, 2, CR // 2, DH), BF16),
        ix_sum=pltpu.VMEM((C, F, D), BF16),
        ix_in=pltpu.VMEM((2, N, F, D), BF16),
        fd=pltpu.VMEM((CD // 4, DH), wire_d),
        fe=pltpu.VMEM((2, CD // 4, DH), wire_d),
        fu=pltpu.VMEM((2, CR // 2, FH // 2), wire),
        fa=pltpu.VMEM((2, CR // 2, DH), wire),
        fb=pltpu.VMEM((2, CR // 2, DH), wire),
        small=pltpu.VMEM((2, 16, D), F32),
        small_ring=pltpu.VMEM((C, 16, DH), BF16),
        fs=pltpu.VMEM((8, D), F32),
        load_sem=dma((20,)),
        g_send=dma((2, PIECES)),
        g_recv=dma((2, N, PIECES)),
        s_send=dma((2,)),
        s_recv=dma((C,)),
        m_send=dma((3,)),
        m_recv=dma((11,)),
        r_send=dma((6, 2)),
        r_recv=dma((6, 2, N)),
        out_sem=dma((8,)),
        y_send=dma((6,)),
        y_recv=dma((6,)),
        ya_send=dma((1,)),
        ya_recv=dma((C,)),
        yq_send=dma((1,)),
        yq_recv=dma((C,)),
        c_send=dma((2,)),
        c_recv=dma((C,)),
        sr_send=dma((2,)),
        sr_recv=dma((2, N)),
        f_send=dma((2 * R - 1,)),
        h_send=dma((3, R)),
        f_recv=dma((6, R, 2)),
    )
    if roomy:
        scratch.update(kt=pltpu.VMEM((DH, keys), BF16))
    names = [*operands, *results, *scratch]
    found = pl.pallas_call(
        functools.partial(layer_kernel, names, S, R),
        out_shape=[(pltpu.VMEM if roomy else jax.ShapeDtypeStruct)(shape, kind) for shape, kind in results.values()],
        in_specs=[spec for _, spec in operands.values()],
        out_specs=[hbm] * len(results),
        scratch_shapes=list(scratch.values()),
        compiler_params=pltpu.CompilerParams(
            collective_id=0, has_side_effects=True, vmem_limit_bytes=(56 if roomy else 62) * 1024 * 1024
        ),
        name="layer",
    )(*[value for value, _ in operands.values()])
    shapes = [(F, D), (F, D), (D // S, D), (D // S,), (D // S, D), (D // S, D), (D // S,), (D // S, D)]
    shapes += [(D // S,)] * 3 + [(D // S, FF), (FF // S,), (FF // S, D)] + [(D // S,)] * 3
    kinds = [BF16] + [F32] * (len(shapes) - 1)
    if roomy:
        found = [pltpu.with_memory_space_constraint(one, pltpu.VMEM) for one in found]
    final = pl.pallas_call(
        finish_kernel,
        out_shape=[jax.ShapeDtypeStruct(shape, kind) for shape, kind in zip(shapes, kinds, strict=True)],
        in_specs=[vmem] * len(found),
        out_specs=[vmem] * len(shapes),
        name="finish",
    )(*found)
    return (final[0][None], final[1][None], *final[2:])


def solution(mesh):
    shared = P("seq", None)
    part = P("seq")
    return jax.shard_map(
        on_device,
        mesh=mesh,
        in_specs=(P("row", "seq", None), P("row", "seq", None), P("row", None)) + (P(),) * 15,
        out_specs=(
            P("row", "seq", None),
            P("row", "seq", None),
            shared,
            part,
            shared,
            shared,
            part,
            shared,
            part,
            part,
            part,
            shared,
            part,
            shared,
            part,
            part,
            part,
        ),
        check_vma=False,
    )
```
